128 devices in a mesh: frame: 16 (over z_lo, x, core), head: 8 (over z_hi, y).
Axes of the slice: x: 4, y: 4, z: 4 (z_hi: 2, z_lo: 2; z = z_hi * 2 + z_lo), core: 2. Of those that a mesh axis runs over, the one named last changes fastest.
Arguments:
- query_in: bfloat16 [16384, 5120], P(('frame', 'head')), may hold values from -9 to 9
- key_in: bfloat16 [16384, 5120], P(('frame', 'head')), may hold values from -5 to 5
- value_in: bfloat16 [16384, 5120], P(('frame', 'head')), may hold values from -6 to 6
- out_grad: bfloat16 [16384, 5120], P(('frame', 'head')), may hold values from -6 to 6
- key_blocks: int32 [40, 128, 12], P('head', 'frame'), may hold values from 0 to 127, as said below
- block_count: int32 [40, 128], P('head', 'frame'), may hold values from 1 to 12
Outputs:
- query_grad: bfloat16 [16384, 5120], P(('frame', 'head'))
- key_grad: bfloat16 [16384, 5120], P(('frame', 'head'))
- value_grad: bfloat16 [16384, 5120], P(('frame', 'head'))
The draws below stay inside these ranges and needn't reach their ends.
Inputs may be any that keep to these rules, and one draw needn't show every extreme that they name: `key_blocks`: for each head and query block b, the first block_count entries are distinct, include b itself, and name blocks whose run b // 8 differs from that of b by at most 2; later entries equal b.
All inputs are finite; a program needn't handle non-finite values.
Results may differ from the reference program's by a relative error of at most 0.017.
Values may be sent and summed in bfloat16 or wider, within the bound.
No kernel may reach another device: no remote copies, remote signals or barrier semaphores. Data moves between devices by JAX's collectives and lax.ppermute only.
A program may use at most 192 MiB of HBM per device.

```python
import jax
import jax.numpy as jnp
from jax import lax

HEADS = 40
HD = 128
BLK = 128
BAND = 2
BPD = 8
MAXK = 12
TOKENS = 16384
QBLOCKS = 128
FEAT = 5120


def shared_keys(key):
    ground = jax.random.truncated_normal(key, -4.0, 4.0, (TOKENS, HEADS * HD), jnp.float32)
    return ground


def mask_lists(key):
    key_rank, key_count, key_full = jax.random.split(key, 3)
    nband = (2 * BAND + 1) * BPD
    query_block = jnp.arange(QBLOCKS, dtype=jnp.int32)[:, None]
    candidate = (query_block // BPD - BAND) * BPD + jnp.arange(nband, dtype=jnp.int32)[None, :]
    distance = jnp.abs(candidate - query_block)
    jitter = jax.random.randint(key_rank, (HEADS, QBLOCKS, nband), 0, 12 * BPD)
    ranking = distance[None] * 4 + jitter
    ranking = jnp.where(distance[None] == 0, -1, ranking)
    inside = (candidate >= 0) & (candidate < QBLOCKS)
    ranking = jnp.where(inside[None], ranking, 1000000)
    ranking = ranking * nband + jnp.arange(nband, dtype=jnp.int32)
    chosen = jnp.argsort(ranking, axis=-1, stable=True)[..., :MAXK]
    picked = jnp.take_along_axis(jnp.broadcast_to(candidate[None], ranking.shape), chosen, axis=-1)
    live_count = jax.random.randint(key_count, (HEADS, QBLOCKS), max(1, MAXK // 3), MAXK + 1)
    forced = jax.random.randint(key_full, (HEADS, 1), 0, QBLOCKS)
    live_count = jnp.where(jnp.arange(QBLOCKS)[None, :] == forced, MAXK, live_count)
    picked = jnp.where(jnp.arange(MAXK)[None, None, :] < live_count[..., None], picked, query_block[None])
    return (picked.astype(jnp.int32), live_count.astype(jnp.int32))


def draw_key_blocks(key, part):
    return mask_lists(key)[0]


def draw_block_count(key, part):
    return mask_lists(key)[1]


def draw_key_in(key, part):
    ground = shared_keys(key)
    return ground.astype(jnp.bfloat16)


def draw_query_in(key, part):
    queries = jax.random.truncated_normal(jax.random.fold_in(key, 7), -4.0, 4.0, (TOKENS, HEADS * HD), jnp.float32)
    return queries.astype(jnp.bfloat16)


def levels(own_key, dims, cuts, least, largest):
    def one(dim, blocks):
        heights = jax.random.uniform(jax.random.fold_in(jax.random.fold_in(own_key, 6), dim), (blocks,), jnp.float32, least / len(cuts), largest / len(cuts))
        return jnp.repeat(jnp.exp(heights), dims[dim] // blocks).reshape((-1,) + (1,) * (len(dims) - dim - 1))

    loudness = one(*cuts[0])
    for cut in cuts[1:]:
        loudness = loudness * one(*cut)
    return loudness


def noise(stream_key, extent, spread, limit, pieces=(), kind=jnp.bfloat16):
    factor_of = levels(stream_key, extent, pieces, -0.22, 0.18) if pieces else 1.0
    result = jax.random.normal(stream_key, extent, jnp.float32) * spread * factor_of
    return jnp.minimum(jnp.maximum(result, -limit), limit).astype(kind)


def setup_inputs(seed: int = 0) -> dict:
    key_list = jax.random.split(jax.random.key(seed), 7)
    query_in = draw_query_in(jax.random.fold_in(key_list[6], 71), 0)
    key_in = draw_key_in(jax.random.fold_in(key_list[6], 71), 0)
    value_in = noise(key_list[2], (TOKENS, FEAT), 1.0, 6.0, ((0, 128),))
    out_grad = noise(key_list[3], (TOKENS, FEAT), 1.0, 6.0, ((0, 128),))
    key_blocks = draw_key_blocks(jax.random.fold_in(key_list[6], 71), 0)
    block_count = draw_block_count(jax.random.fold_in(key_list[6], 71), 0)
    return {"query_in": query_in, "key_in": key_in, "value_in": value_in, "out_grad": out_grad, "key_blocks": key_blocks, "block_count": block_count}


NEG_FILL = -1e30


def head_grads(query_blk, key_sel, value_sel, grad_blk, visible):
    scaling = query_blk.shape[-1] ** -0.5
    f32 = jnp.float32
    scores = jnp.einsum('qid,qmjd->qimj', query_blk.astype(f32), key_sel.astype(f32)) * scaling
    usable = visible[:, None, :, None]
    scores = jnp.where(usable, scores, NEG_FILL)
    row_max = jnp.max(scores, axis=(2, 3), keepdims=True)
    weights = jnp.where(usable, jnp.exp(scores - row_max), 0.0)
    row_sum = jnp.sum(weights, axis=(2, 3), keepdims=True)
    prob_full = weights / row_sum
    prob_half = prob_full.astype(jnp.bfloat16)
    attended = jnp.einsum('qimj,qmjd->qid', prob_half.astype(f32), value_sel.astype(f32))
    row_dot = jnp.sum(grad_blk.astype(f32) * attended, axis=-1)[:, :, None, None]
    prob_grad = jnp.einsum('qid,qmjd->qimj', grad_blk.astype(f32), value_sel.astype(f32))
    score_grad = (prob_full * (prob_grad - row_dot)).astype(jnp.bfloat16)
    grad_query = jnp.einsum('qimj,qmjd->qid', score_grad.astype(f32), key_sel.astype(f32)) * scaling
    grad_key = jnp.einsum('qimj,qid->qmjd', score_grad.astype(f32), query_blk.astype(f32)) * scaling
    grad_value = jnp.einsum('qimj,qid->qmjd', prob_half.astype(f32), grad_blk.astype(f32))
    return grad_query, grad_key, grad_value


def reference(query_in, key_in, value_in, out_grad, key_blocks, block_count):
    def per_head(head_index):
        first = head_index * HD

        def pick(array):
            return lax.dynamic_slice_in_dim(array, first, HD, 1).reshape(QBLOCKS, BLK, HD)

        query_h = pick(query_in)
        key_h = pick(key_in)
        value_h = pick(value_in)
        grad_h = pick(out_grad)
        block_ids = key_blocks[head_index]
        visible = jnp.arange(MAXK, dtype=jnp.int32)[None, :] < block_count[head_index][:, None]
        grad_query, grad_key, grad_value = head_grads(query_h, key_h[block_ids], value_h[block_ids], grad_h, visible)
        onehot = (block_ids.reshape(-1)[:, None] == jnp.arange(QBLOCKS, dtype=jnp.int32)[None, :]).astype(jnp.float32)
        stacked = jnp.stack([grad_key, grad_value]).reshape(2, QBLOCKS * MAXK, BLK, HD)
        summed = jnp.einsum('sn,asjd->anjd', onehot, stacked, precision=lax.Precision.HIGHEST)
        return grad_query.reshape(TOKENS, HD), summed[0].reshape(TOKENS, HD), summed[1].reshape(TOKENS, HD)

    grad_query, grad_key, grad_value = lax.map(per_head, jnp.arange(HEADS).astype(jnp.int32))

    def to_tokens(array):
        return jnp.transpose(array, (1, 0, 2)).reshape(TOKENS, HEADS * HD).astype(jnp.bfloat16)

    return to_tokens(grad_query), to_tokens(grad_key), to_tokens(grad_value)
```

```python
import jax
import jax.numpy as jnp
from jax import lax
from jax.experimental import pallas as pl
from jax.experimental.pallas import tpu as pltpu
from jax.sharding import PartitionSpec as P

HD = 128
BLK = 128
BAND = 2
BPD = 8
MAXK = 12
HPD = 5
CHUNKS = ((0, 5),)
GROUP = 4
NEG = -1e30
LOG2E = 1.4426950408889634
SCALE = HD**-0.5
F32 = jnp.float32
BF16 = jnp.bfloat16
NT = (((1,), (1,)), ((), ()))
NN = (((1,), (0,)), ((), ()))
TN = (((0,), (0,)), ((), ()))

M2, SIB, OWN, OUTER, P2 = range(5)
WINDOW = 5 * BPD


def dot(a, b, dims):
    return lax.dot_general(a, b, dims, preferred_element_type=F32)


def fold(x):
    return x.reshape(-1, 8, HD)


def query_block(n_keys, h, b, ids_ref, count, qd, kv, acc, dq, kcat, s_scr, dp_scr, ds_scr):
    q = qd[h, b, 0]
    do = qd[h, b, 1]
    base = (h * BPD + b) * MAXK
    m8 = jnp.full((8, HD), NEG, F32)
    index = [ids_ref[base + s] for s in range(n_keys)]
    for s in range(n_keys):
        k = kv[h, index[s], 0]
        kcat[pl.ds(s * BLK, BLK), :] = k
        st = dot(k, q, NT)
        if s > n_keys - GROUP:
            st = jnp.where(s < count, st, NEG)
        s_scr[s] = st
        m8 = jnp.maximum(m8, jnp.max(fold(st), axis=0))
        dp_scr[s] = dot(kv[h, index[s], 1], do, NT)
    m = jnp.max(m8, axis=0, keepdims=True) * (SCALE * LOG2E)
    l8 = jnp.zeros((8, HD), F32)
    r8 = jnp.zeros((8, HD), F32)
    for s in range(n_keys):
        p = jnp.exp2(s_scr[s] * (SCALE * LOG2E) - m)
        s_scr[s] = p
        l8 += jnp.sum(fold(p), axis=0)
        r8 += jnp.sum(fold(p * dp_scr[s]), axis=0)
    inv = 1.0 / jnp.sum(l8, axis=0, keepdims=True)
    rd = jnp.sum(r8, axis=0, keepdims=True) * inv
    for s in range(n_keys):
        p = s_scr[s] * inv
        ds = (p * (dp_scr[s] - rd)).astype(BF16)
        ds_scr[pl.ds(s * BLK, BLK), :] = ds
        acc[index[s], 0] += dot(ds, q, NN)
        acc[index[s], 1] += dot(p.astype(BF16), do, NN)
    rows = pl.ds(0, n_keys * BLK)
    dq[h, b] = (dot(ds_scr[rows, :], kcat[rows, :], TN) * SCALE).astype(BF16)


def attention_kernel(
    n, ids_ref, cnt_ref, m2_in, sib_in, own_in, outer_in, p2_in, qd_in,
    dq_out, m2_out, sx_out, own_out, p2_out,
    kv, qd, acc, stage, dq, kcat, s_scr, dp_scr, ds_scr, in_sem, out_sem, dq_sem,
):
    sources = (m2_in, sib_in, own_in, outer_in, p2_in)

    def fetch(h, i):
        if i == 5:
            return pltpu.make_async_copy(qd_in.at[:, h], qd.at[h], in_sem.at[h, 5])
        return pltpu.make_async_copy(
            sources[i].at[:, h], kv.at[h, pl.ds(i * BPD, BPD)], in_sem.at[h, i]
        )

    def put(h, i):
        slot = h % 2
        target = (m2_out, sx_out.at[0], own_out, sx_out.at[1], p2_out)[i]
        return pltpu.make_async_copy(
            stage.at[slot, pl.ds(i * BPD, BPD)], target.at[:, h], out_sem.at[slot, i]
        )

    for h in range(n):
        for i in range(6):
            fetch(h, i).start()
    for h in range(n):
        acc[...] = jnp.zeros_like(acc)
        for i in range(6):
            fetch(h, i).wait()

        def one(b, carry):
            count = cnt_ref[h * BPD + b]
            for upto in range(GROUP, MAXK + 1, GROUP):

                @pl.when((count > upto - GROUP) & (count <= upto))
                def _():
                    query_block(
                        upto, h, b, ids_ref, count, qd, kv, acc, dq, kcat, s_scr, dp_scr, ds_scr
                    )

            return carry

        lax.fori_loop(0, BPD, one, 0)
        if h >= 2:
            for i in range(5):
                put(h - 2, i).wait()

        def convert(i, carry):
            stage[h % 2, i, 0] = (acc[i, 0] * SCALE).astype(BF16)
            stage[h % 2, i, 1] = acc[i, 1].astype(BF16)
            return carry

        lax.fori_loop(0, WINDOW, convert, 0)
        for i in range(5):
            put(h, i).start()
        pltpu.make_async_copy(dq.at[h], dq_out.at[:, h], dq_sem.at[h]).start()
    for h in range(max(0, n - 2), n):
        for i in range(5):
            put(h, i).wait()
    for h in range(n):
        pltpu.make_async_copy(dq.at[h], dq_out.at[:, h], dq_sem.at[h]).wait()


def attention(ids, counts, m2, sib, own, outer, p2, qd):
    n = own.shape[1]
    block = jax.ShapeDtypeStruct((BPD, n, 2, BLK, HD), BF16)
    smem = pl.BlockSpec(memory_space=pltpu.SMEM)
    hbm = pl.BlockSpec(memory_space=pl.ANY)
    pairs = n * BPD * 8
    return pl.pallas_call(
        lambda *refs: attention_kernel(n, *refs),
        out_shape=(
            jax.ShapeDtypeStruct((BPD, n, BLK, HD), BF16),
            block,
            jax.ShapeDtypeStruct((2, BPD, n, 2, BLK, HD), BF16),
            block,
            block,
        ),
        in_specs=[smem, smem] + [hbm] * 6,
        out_specs=[hbm] * 5,
        scratch_shapes=[
            pltpu.VMEM((n, WINDOW, 2, BLK, HD), BF16),
            pltpu.VMEM((n, BPD, 2, BLK, HD), BF16),
            pltpu.VMEM((WINDOW, 2, BLK, HD), F32),
            pltpu.VMEM((2, WINDOW, 2, BLK, HD), BF16),
            pltpu.VMEM((n, BPD, BLK, HD), BF16),
            pltpu.VMEM((MAXK * BLK, HD), BF16),
            pltpu.VMEM((MAXK, BLK, HD), F32),
            pltpu.VMEM((MAXK, BLK, HD), F32),
            pltpu.VMEM((MAXK * BLK, HD), BF16),
            pltpu.SemaphoreType.DMA((n, 6)),
            pltpu.SemaphoreType.DMA((2, 5)),
            pltpu.SemaphoreType.DMA((n,)),
        ],
        compiler_params=pltpu.CompilerParams(vmem_limit_bytes=48 * 2**20),
        cost_estimate=pl.CostEstimate(
            flops=pairs * 10 * BLK * BLK * HD,
            bytes_accessed=n * 12 * BPD * 2 * BLK * HD * 2,
            transcendentals=pairs * BLK * BLK,
        ),
    )(ids, counts, m2, sib, own, outer, p2, qd)


def shift(value, axis, steps):
    count = lax.axis_size(axis)
    pairs = [(s, s + steps) for s in range(max(0, -steps), min(count, count - steps))]
    return lax.ppermute(value, axis, pairs)


def swap(value, senders=(0, 1)):
    count = lax.axis_size("frame")
    return lax.ppermute(value, "frame", [(s, s ^ 1) for s in range(count) if s % 2 in senders])


def exchange_in(first, second, lo, hi):
    def split(x):
        x = x.reshape(BLK, -1, HPD, HD)[:, :, lo:hi]
        return jnp.transpose(x, (1, 2, 0, 3))

    return lax.all_to_all(jnp.stack([split(first), split(second)], axis=2), "head", 0, 0)


def shards(query_in, key_in, value_in, out_grad, key_blocks, block_count):
    frame = lax.axis_index("frame")
    core = frame % 2
    rel = key_blocks - (frame - BAND) * BPD
    run = rel // BPD
    side = jnp.where(run == 1 + 2 * (1 - core), SIB, OUTER)
    role = jnp.where(run % 2 == 1, side, run)
    ids = role * BPD + rel % BPD

    results = []
    for lo, hi in CHUNKS:
        own = exchange_in(key_in, value_in, lo, hi)
        below = shift(own, "frame", 2)
        above = shift(own, "frame", -2)
        sib = swap(own)
        qd = exchange_in(query_in, out_grad, lo, hi)
        outer = jnp.where(core == 0, swap(below, (1,)), swap(above, (0,)))
        dq, m2, sx, mine, p2 = attention(
            ids[lo:hi].reshape(-1), block_count[lo:hi].reshape(-1), below, sib, own, outer, above, qd
        )
        sx = swap(sx)
        m2 = m2 + jnp.where(core == 1, sx[1], 0)
        p2 = p2 + jnp.where(core == 0, sx[1], 0)
        from_above = shift(m2, "frame", -2)
        from_below = shift(p2, "frame", 2)
        total = sum(x.astype(F32) for x in (mine, sx[0], from_above, from_below)).astype(BF16)
        dq = lax.all_to_all(dq, "head", 0, 0)
        total = lax.all_to_all(total, "head", 0, 0)
        results.append((dq, total[:, :, 0], total[:, :, 1]))

    def to_tokens(parts):
        whole = jnp.concatenate(parts, axis=1)
        return jnp.transpose(whole, (2, 0, 1, 3)).reshape(BLK, -1)

    return tuple(to_tokens([part[i] for part in results]) for i in range(3))


def solution(mesh):
    tokens = P(("frame", "head"), None)
    return jax.shard_map(
        shards,
        mesh=mesh,
        in_specs=(tokens, tokens, tokens, tokens, P("head", "frame", None), P("head", "frame")),
        out_specs=(tokens, tokens, tokens),
        check_vma=False,
    )
```

```python
import functools

import jax
import jax.numpy as jnp
from jax import lax
from jax.experimental import pallas as pl
from jax.experimental.pallas import tpu as pltpu
from jax.sharding import Mesh
from jax.sharding import PartitionSpec as P

HD = 128
BLK = 128
BAND = 2
BPD = 8
MAXK = 12
HPG = 5
GROUP = 4
ATTENTION_COST = 10
VMEM_LIMIT = 56 * 2**20
NEG = -1e30
LOG2E = 1.4426950408889634
SCALE = HD**-0.5
ORDER = (
    (0, True, None),
    (1, True, None),
    (0, False, None),
    (2, True, 0),
    (1, False, 1),
    (2, False, None),
)
F32 = jnp.float32
BF16 = jnp.bfloat16
NT = (((1,), (1,)), ((), ()))
NN = (((1,), (0,)), ((), ()))
TN = (((0,), (0,)), ((), ()))


def dot(a, b, dims):
    return lax.dot_general(a, b, dims, preferred_element_type=F32)


def fold(x):
    return x.reshape(-1, 8, HD)


def query_block(n_keys, b, ids_ref, count, qd, kv, acc, dq, kcat, s_scr, dp_scr, ds_scr):
    q = qd[b, 0]
    do = qd[b, 1]
    base = b * MAXK
    m8 = jnp.full((8, HD), NEG, F32)
    index = [ids_ref[base + s] for s in range(n_keys)]
    for s in range(n_keys):
        k = kv[index[s], 0]
        kcat[pl.ds(s * BLK, BLK), :] = k
        st = dot(k, q, NT)
        if s > n_keys - GROUP:
            st = jnp.where(s < count, st, NEG)
        s_scr[s] = st
        m8 = jnp.maximum(m8, jnp.max(fold(st), axis=0))
        dp_scr[s] = dot(kv[index[s], 1], do, NT)
    m = jnp.max(m8, axis=0, keepdims=True) * (SCALE * LOG2E)
    l8 = jnp.zeros((8, HD), F32)
    r8 = jnp.zeros((8, HD), F32)
    for s in range(n_keys):
        p = jnp.exp2(s_scr[s] * (SCALE * LOG2E) - m)
        s_scr[s] = p
        l8 += jnp.sum(fold(p), axis=0)
        r8 += jnp.sum(fold(p * dp_scr[s]), axis=0)
    inv = 1.0 / jnp.sum(l8, axis=0, keepdims=True)
    rd = jnp.sum(r8, axis=0, keepdims=True) * inv
    for s in range(n_keys):
        p = s_scr[s] * inv
        ds = (p * (dp_scr[s] - rd)).astype(BF16)
        ds_scr[pl.ds(s * BLK, BLK), :] = ds
        acc[index[s], 0] += dot(ds, q, NN)
        acc[index[s], 1] += dot(p.astype(BF16), do, NN)
    rows = pl.ds(0, n_keys * BLK)
    dq[...] = (dot(ds_scr[rows, :], kcat[rows, :], TN) * SCALE).astype(BF16)


def attention_kernel(parts, size, n_query, ids_ref, cnt_ref, *refs):
    sources, refs = refs[:parts], refs[parts:]
    qd_in, dq_out, refs = refs[0], refs[1], refs[2:]
    targets, refs = refs[:parts], refs[parts:]
    kv, qd, acc, stage, dq, kcat, s_scr, dp_scr, ds_scr, in_sem, out_sem = refs
    fetches = [
        pltpu.make_async_copy(sources[i], kv.at[pl.ds(i * size, size)], in_sem.at[i])
        for i in range(parts)
    ] + [pltpu.make_async_copy(qd_in, qd, in_sem.at[parts])]
    for copy in fetches:
        copy.start()
    acc[...] = jnp.zeros_like(acc)
    for copy in fetches:
        copy.wait()

    first = cnt_ref[n_query]
    if n_query < dq.shape[0]:
        dq[...] = jnp.zeros_like(dq)

    def one(b, carry):
        count = cnt_ref[b]
        for upto in range(GROUP, MAXK + 1, GROUP):

            @pl.when((count > upto - GROUP) & (count <= upto))
            def _():
                query_block(upto, b, ids_ref, count, qd, kv, acc, dq.at[first + b], kcat, s_scr, dp_scr, ds_scr)

        return carry

    lax.fori_loop(0, n_query, one, 0)
    puts = [pltpu.make_async_copy(dq, dq_out, out_sem.at[parts])]
    puts[0].start()
    for i in range(parts):

        def convert(j, carry):
            stage[j, 0] = (acc[j, 0] * SCALE).astype(BF16)
            stage[j, 1] = acc[j, 1].astype(BF16)
            return carry

        lax.fori_loop(i * size, (i + 1) * size, convert, 0)
        puts.append(
            pltpu.make_async_copy(stage.at[pl.ds(i * size, size)], targets[i], out_sem.at[i])
        )
        puts[-1].start()
    for copy in puts:
        copy.wait()


def attention(ids, counts, sources, qd):
    parts, size, n_query = len(sources), sources[0].shape[0], qd.shape[0]
    window = parts * size
    smem = pl.BlockSpec(memory_space=pltpu.SMEM)
    hbm = pl.BlockSpec(memory_space=pl.ANY)
    pairs = n_query * 8
    out = pl.pallas_call(
        functools.partial(attention_kernel, parts, size, n_query),
        out_shape=[jax.ShapeDtypeStruct((size, BLK, HD), BF16)]
        + [jax.ShapeDtypeStruct((size, 2, BLK, HD), BF16)] * parts,
        in_specs=[smem, smem] + [hbm] * (parts + 1),
        out_specs=[hbm] * (parts + 1),
        scratch_shapes=[
            pltpu.VMEM((window, 2, BLK, HD), BF16),
            pltpu.VMEM((n_query, 2, BLK, HD), BF16),
            pltpu.VMEM((window, 2, BLK, HD), F32),
            pltpu.VMEM((window, 2, BLK, HD), BF16),
            pltpu.VMEM((size, BLK, HD), BF16),
            pltpu.VMEM((MAXK * BLK, HD), BF16),
            pltpu.VMEM((MAXK, BLK, HD), F32),
            pltpu.VMEM((MAXK, BLK, HD), F32),
            pltpu.VMEM((MAXK * BLK, HD), BF16),
            pltpu.SemaphoreType.DMA((parts + 1,)),
            pltpu.SemaphoreType.DMA((parts + 1,)),
        ],
        compiler_params=pltpu.CompilerParams(vmem_limit_bytes=VMEM_LIMIT),
        cost_estimate=pl.CostEstimate(
            flops=pairs * ATTENTION_COST * BLK * BLK * HD,
            bytes_accessed=(2 * window + n_query) * 2 * BLK * HD * 2,
            transcendentals=pairs * BLK * BLK,
        ),
        name="attention",
    )(ids, counts, *sources, qd)
    return out[0], out[1:]


def split_kernel(k_ref, v_ref, q_ref, g_ref, kv0_ref, kv1_ref, kv2_ref, qd0_ref, qd1_ref, qd2_ref):
    sides = ((k_ref, v_ref, kv0_ref, kv1_ref, kv2_ref), (q_ref, g_ref, qd0_ref, qd1_ref, qd2_ref))
    for first, second, a0_ref, a1_ref, a2_ref in sides:
        for t, ref in enumerate((first, second)):
            for j in range(a0_ref.shape[1]):

                def head(m):
                    return ref[:, (j * HPG + m) * HD : (j * HPG + m + 1) * HD]

                for core in range(2):
                    a0_ref[core, j, t] = head(2 * core)
                    a1_ref[core, j, t] = head(2 * core + 1)
                for core in range(a2_ref.shape[0]):
                    a2_ref[core, j, t] = head(4)


def split_heads(key_in, value_in, query_in, out_grad):
    groups, step = key_in.shape[1] // (HPG * HD), 2
    a = jax.ShapeDtypeStruct((2, groups, 2, BLK, HD), BF16)
    b = jax.ShapeDtypeStruct((1, groups, 2, BLK, HD), BF16)
    a_spec = pl.BlockSpec((2, step, 2, BLK, HD), lambda j: (0, j, 0, 0, 0))
    b_spec = pl.BlockSpec((1, step, 2, BLK, HD), lambda j: (0, j, 0, 0, 0))
    x_spec = pl.BlockSpec((BLK, step * HPG * HD), lambda j: (0, j))
    out = pl.pallas_call(
        split_kernel,
        grid=(groups // step,),
        out_shape=(a, a, a, a, a, b),
        in_specs=[x_spec] * 4,
        out_specs=(a_spec,) * 5 + (b_spec,),
        compiler_params=pltpu.CompilerParams(vmem_limit_bytes=VMEM_LIMIT),
        cost_estimate=pl.CostEstimate(flops=0, bytes_accessed=16 * key_in.size, transcendentals=0),
        name="split_heads",
    )(key_in, value_in, query_in, out_grad)
    flat = [x.reshape(-1, 2, BLK, HD) for x in out]
    return flat[:3], flat[3:]


def join_kernel(a0_ref, a1_ref, a2_ref, *outs):
    for t, ref in enumerate(outs):
        for j in range(a0_ref.shape[1]):

            def put(m, value):
                ref[:, (j * HPG + m) * HD : (j * HPG + m + 1) * HD] = value

            for core in range(2):
                put(2 * core, a0_ref[core, j, t])
                put(2 * core + 1, a1_ref[core, j, t])
            put(4, (a2_ref[0, j, t].astype(F32) + a2_ref[1, j, t].astype(F32)).astype(BF16))


def join_heads(*parts):
    groups, step = parts[0].shape[0] // 2, 2
    out = jax.ShapeDtypeStruct((BLK, groups * HPG * HD), BF16)
    return pl.pallas_call(
        join_kernel,
        grid=(groups // step,),
        out_shape=(out,) * 3,
        in_specs=[pl.BlockSpec((2, step, 3, BLK, HD), lambda j: (0, j, 0, 0, 0))] * 3,
        out_specs=(pl.BlockSpec((BLK, step * HPG * HD), lambda j: (0, j)),) * 3,
        compiler_params=pltpu.CompilerParams(vmem_limit_bytes=VMEM_LIMIT),
        cost_estimate=pl.CostEstimate(
            flops=0, bytes_accessed=groups * HPG * 3 * BLK * HD * 4, transcendentals=0
        ),
        name="join_heads",
    )(*[x.reshape(2, groups, 3, BLK, HD) for x in parts])


def total_kernel(dq_ref, own_ref, *refs):
    terms, out_ref = refs[:-1], refs[-1]
    out_ref[:, 0] = dq_ref[...]
    total = own_ref[...].astype(F32)
    for term in terms:
        total += term[...].astype(F32)
    out_ref[:, 1:] = total.astype(BF16)


def total_grads(dq, own, terms):
    blocks, step = dq.shape[0], 4
    kv_spec = pl.BlockSpec((step, 2, BLK, HD), lambda i: (i, 0, 0, 0))
    return pl.pallas_call(
        total_kernel,
        grid=(blocks // step,),
        out_shape=jax.ShapeDtypeStruct((blocks, 3, BLK, HD), BF16),
        in_specs=[pl.BlockSpec((step, BLK, HD), lambda i: (i, 0, 0))] + [kv_spec] * (1 + len(terms)),
        out_specs=pl.BlockSpec((step, 3, BLK, HD), lambda i: (i, 0, 0, 0)),
        cost_estimate=pl.CostEstimate(
            flops=0, bytes_accessed=(6 + 2 * len(terms)) * dq.size * 2, transcendentals=0
        ),
        name="total_grads",
    )(dq, own, *terms)


def shift(value, axes, steps):
    count = lax.axis_size(axes)
    pairs = [(s, s + steps) for s in range(max(0, -steps), min(count, count - steps))]
    return lax.ppermute(value, axes, pairs)


PAIR = ("core", "group")
RUNS = ("chip", "core")


def exchange(x, axes):
    return lax.all_to_all(x, axes, 0, 0)


def masks(key_blocks, block_count):
    chip, core = lax.axis_index("chip"), lax.axis_index("core")
    packed = jnp.concatenate([key_blocks, block_count[:, :, None]], axis=2)
    mine = lax.dynamic_slice_in_dim(packed, 2 * core, 2, 0)
    theirs = lax.dynamic_slice_in_dim(packed, 2 - 2 * core, 2, 0)
    theirs = lax.ppermute(theirs, "core", [(0, 1), (1, 0)])
    first, second = jnp.where(core == 0, mine, theirs), jnp.where(core == 0, theirs, mine)
    both = jnp.concatenate([first, second], axis=1)
    first_block = (2 * chip - BAND) * BPD
    result = []
    for part, row in ((both[0], 0), (both[1], 0), (packed[4], core * BPD)):
        counts = jnp.append(part[:, MAXK], jnp.int32(row))
        result.append(((part[:, :MAXK] - first_block).reshape(-1), counts))
    return result


def after(x, *done):
    return lax.optimization_barrier((x, *done))[0]


def shards(query_in, key_in, value_in, out_grad, key_blocks, block_count):
    lists = masks(key_blocks, block_count)
    kv, qd = split_heads(key_in, value_in, query_in, out_grad)
    own, queries, near, last = [None] * 3, [None] * 3, [None] * 3, ()
    for part, is_kv, wait_for in ORDER:
        ready = last if wait_for is None else (*last, *near[wait_for])
        source = after(kv[part] if is_kv else qd[part], *ready)
        got = exchange(source, PAIR if is_kv or part < 2 else "group")
        last = (got,)
        if is_kv:
            own[part] = got
            near[part] = (shift(got, "chip", 1), shift(got, "chip", -1))
        else:
            queries[part] = got
    done = []
    for part, (ids, counts) in enumerate(lists):
        sources = (near[part][0], own[part], near[part][1])
        dq, grads = attention(ids, after(counts, *[x[0] for x in done[-1:]]), sources, queries[part])
        done.append((dq, grads[1], [shift(grads[0], "chip", -1), shift(grads[2], "chip", 1)]))
    back = []
    for part, (dq, mine, terms) in enumerate(done):
        later = [x[0] for x in done[part + 1 : part + 2]] + list(near[2])
        total = total_grads(after(dq, *later, *back[-1:]), mine, terms)
        back.append(exchange(total, PAIR))
    return tuple(join_heads(*back))


def solution(mesh):
    chips = mesh.shape["frame"] // 2
    mesh = Mesh(mesh.devices.reshape(chips, 2, -1), ("chip", "core", "group"))
    tokens = P(("chip", "core", "group"), None)
    return jax.shard_map(
        shards,
        mesh=mesh,
        in_specs=(tokens,) * 4 + (P("group", RUNS, None), P("group", RUNS)),
        out_specs=(tokens,) * 3,
        check_vma=False,
    )
```

```python
import functools

import jax
import jax.numpy as jnp
from jax import lax
from jax.experimental import pallas as pl
from jax.experimental.pallas import tpu as pltpu
from jax.sharding import Mesh
from jax.sharding import PartitionSpec as P

HD = 128
BLK = 128
BAND = 2
BPD = 8
MAXK = 12
HPG = 5
GROUP = 4
ATTENTION_COST = 10
VMEM_LIMIT = 56 * 2**20
NEG = -1e30
LOG2E = 1.4426950408889634
SCALE = HD**-0.5
ORDER = (
    (0, True, None),
    (1, True, None),
    (0, False, None),
    (2, True, 0),
    (1, False, 1),
    (2, False, None),
)
F32 = jnp.float32
BF16 = jnp.bfloat16
NT = (((1,), (1,)), ((), ()))
NN = (((1,), (0,)), ((), ()))
TN = (((0,), (0,)), ((), ()))


def dot(a, b, dims):
    return lax.dot_general(a, b, dims, preferred_element_type=F32)


def fold(x):
    return x.reshape(-1, 8, HD)


def query_block(n_keys, b, ids_ref, count, qd, kv, acc, dq, kcat, s_scr, dp_scr, ds_scr):
    q = qd[b, 0]
    do = qd[b, 1]
    base = b * MAXK
    m8 = jnp.full((8, HD), NEG, F32)
    index = [ids_ref[base + s] for s in range(n_keys)]
    for s in range(n_keys):
        k = kv[index[s], 0]
        kcat[pl.ds(s * BLK, BLK), :] = k
        st = dot(k, q, NT)
        if s > n_keys - GROUP:
            st = jnp.where(s < count, st, NEG)
        s_scr[s] = st
        m8 = jnp.maximum(m8, jnp.max(fold(st), axis=0))
        dp_scr[s] = dot(kv[index[s], 1], do, NT)
    m = jnp.max(m8, axis=0, keepdims=True) * (SCALE * LOG2E)
    l8 = jnp.zeros((8, HD), F32)
    r8 = jnp.zeros((8, HD), F32)
    for s in range(n_keys):
        p = jnp.exp2(s_scr[s] * (SCALE * LOG2E) - m)
        s_scr[s] = p
        l8 += jnp.sum(fold(p), axis=0)
        r8 += jnp.sum(fold(p * dp_scr[s]), axis=0)
    inv = 1.0 / jnp.sum(l8, axis=0, keepdims=True)
    rd = jnp.sum(r8, axis=0, keepdims=True) * inv
    for s in range(n_keys):
        p = s_scr[s] * inv
        ds = (p * (dp_scr[s] - rd)).astype(BF16)
        ds_scr[pl.ds(s * BLK, BLK), :] = ds
        acc[index[s], 0] += dot(ds, q, NN)
        acc[index[s], 1] += dot(p.astype(BF16), do, NN)
    rows = pl.ds(0, n_keys * BLK)
    dq[...] = (dot(ds_scr[rows, :], kcat[rows, :], TN) * SCALE).astype(BF16)


def attention_kernel(parts, size, n_query, ids_ref, cnt_ref, *refs):
    sources, refs = refs[:parts], refs[parts:]
    qd_in, dq_out, refs = refs[0], refs[1], refs[2:]
    targets, refs = refs[:parts], refs[parts:]
    kv, qd, acc, stage, dq, kcat, s_scr, dp_scr, ds_scr, in_sem, out_sem = refs
    fetches = [
        pltpu.make_async_copy(sources[i], kv.at[pl.ds(i * size, size)], in_sem.at[i])
        for i in range(parts)
    ] + [pltpu.make_async_copy(qd_in, qd, in_sem.at[parts])]
    for copy in fetches:
        copy.start()
    acc[...] = jnp.zeros_like(acc)
    for copy in fetches:
        copy.wait()

    first = cnt_ref[n_query]
    if n_query < dq.shape[0]:
        dq[...] = jnp.zeros_like(dq)

    def one(b, carry):
        count = cnt_ref[b]
        for upto in range(GROUP, MAXK + 1, GROUP):

            @pl.when((count > upto - GROUP) & (count <= upto))
            def _():
                query_block(upto, b, ids_ref, count, qd, kv, acc, dq.at[first + b], kcat, s_scr, dp_scr, ds_scr)

        return carry

    lax.fori_loop(0, n_query, one, 0)
    puts = [pltpu.make_async_copy(dq, dq_out, out_sem.at[parts])]
    puts[0].start()
    for i in range(parts):

        def convert(j, carry):
            stage[j, 0] = (acc[j, 0] * SCALE).astype(BF16)
            stage[j, 1] = acc[j, 1].astype(BF16)
            return carry

        lax.fori_loop(i * size, (i + 1) * size, convert, 0)
        puts.append(
            pltpu.make_async_copy(stage.at[pl.ds(i * size, size)], targets[i], out_sem.at[i])
        )
        puts[-1].start()
    for copy in puts:
        copy.wait()


def attention(ids, counts, sources, qd):
    parts, size, n_query = len(sources), sources[0].shape[0], qd.shape[0]
    window = parts * size
    smem = pl.BlockSpec(memory_space=pltpu.SMEM)
    hbm = pl.BlockSpec(memory_space=pl.ANY)
    pairs = n_query * 8
    out = pl.pallas_call(
        functools.partial(attention_kernel, parts, size, n_query),
        out_shape=[jax.ShapeDtypeStruct((size, BLK, HD), BF16)]
        + [jax.ShapeDtypeStruct((size, 2, BLK, HD), BF16)] * parts,
        in_specs=[smem, smem] + [hbm] * (parts + 1),
        out_specs=[hbm] * (parts + 1),
        scratch_shapes=[
            pltpu.VMEM((window, 2, BLK, HD), BF16),
            pltpu.VMEM((n_query, 2, BLK, HD), BF16),
            pltpu.VMEM((window, 2, BLK, HD), F32),
            pltpu.VMEM((window, 2, BLK, HD), BF16),
            pltpu.VMEM((size, BLK, HD), BF16),
            pltpu.VMEM((MAXK * BLK, HD), BF16),
            pltpu.VMEM((MAXK, BLK, HD), F32),
            pltpu.VMEM((MAXK, BLK, HD), F32),
            pltpu.VMEM((MAXK * BLK, HD), BF16),
            pltpu.SemaphoreType.DMA((parts + 1,)),
            pltpu.SemaphoreType.DMA((parts + 1,)),
        ],
        compiler_params=pltpu.CompilerParams(vmem_limit_bytes=VMEM_LIMIT),
        cost_estimate=pl.CostEstimate(
            flops=pairs * ATTENTION_COST * BLK * BLK * HD,
            bytes_accessed=(2 * window + n_query) * 2 * BLK * HD * 2,
            transcendentals=pairs * BLK * BLK,
        ),
        name="attention",
    )(ids, counts, *sources, qd)
    return out[0], out[1:]


def split_kernel(k_ref, v_ref, q_ref, g_ref, kv0_ref, kv1_ref, kv2_ref, qd0_ref, qd1_ref, qd2_ref):
    sides = ((k_ref, v_ref, kv0_ref, kv1_ref, kv2_ref), (q_ref, g_ref, qd0_ref, qd1_ref, qd2_ref))
    for first, second, a0_ref, a1_ref, a2_ref in sides:
        for t, ref in enumerate((first, second)):
            for j in range(a0_ref.shape[1]):

                def head(m):
                    return ref[:, (j * HPG + m) * HD : (j * HPG + m + 1) * HD]

                for core in range(2):
                    a0_ref[core, j, t] = head(2 * core)
                    a1_ref[core, j, t] = head(2 * core + 1)
                for core in range(a2_ref.shape[0]):
                    a2_ref[core, j, t] = head(4)


def split_heads(key_in, value_in, query_in, out_grad):
    groups, step = key_in.shape[1] // (HPG * HD), 2
    a = jax.ShapeDtypeStruct((2, groups, 2, BLK, HD), BF16)
    b = jax.ShapeDtypeStruct((1, groups, 2, BLK, HD), BF16)
    a_spec = pl.BlockSpec((2, step, 2, BLK, HD), lambda j: (0, j, 0, 0, 0))
    b_spec = pl.BlockSpec((1, step, 2, BLK, HD), lambda j: (0, j, 0, 0, 0))
    x_spec = pl.BlockSpec((BLK, step * HPG * HD), lambda j: (0, j))
    out = pl.pallas_call(
        split_kernel,
        grid=(groups // step,),
        out_shape=(a, a, a, a, a, b),
        in_specs=[x_spec] * 4,
        out_specs=(a_spec,) * 5 + (b_spec,),
        compiler_params=pltpu.CompilerParams(vmem_limit_bytes=VMEM_LIMIT),
        cost_estimate=pl.CostEstimate(flops=0, bytes_accessed=16 * key_in.size, transcendentals=0),
        name="split_heads",
    )(key_in, value_in, query_in, out_grad)
    flat = [x.reshape(-1, 2, BLK, HD) for x in out]
    return flat[:3], flat[3:]


def join_kernel(a0_ref, a1_ref, a2_ref, *outs):
    for t, ref in enumerate(outs):
        for j in range(a0_ref.shape[1]):

            def put(m, value):
                ref[:, (j * HPG + m) * HD : (j * HPG + m + 1) * HD] = value

            for core in range(2):
                put(2 * core, a0_ref[core, j, t])
                put(2 * core + 1, a1_ref[core, j, t])
            put(4, (a2_ref[0, j, t].astype(F32) + a2_ref[1, j, t].astype(F32)).astype(BF16))


def join_heads(*parts):
    groups, step = parts[0].shape[0] // 2, 2
    out = jax.ShapeDtypeStruct((BLK, groups * HPG * HD), BF16)
    return pl.pallas_call(
        join_kernel,
        grid=(groups // step,),
        out_shape=(out,) * 3,
        in_specs=[pl.BlockSpec((2, step, 3, BLK, HD), lambda j: (0, j, 0, 0, 0))] * 3,
        out_specs=(pl.BlockSpec((BLK, step * HPG * HD), lambda j: (0, j)),) * 3,
        compiler_params=pltpu.CompilerParams(vmem_limit_bytes=VMEM_LIMIT),
        cost_estimate=pl.CostEstimate(
            flops=0, bytes_accessed=groups * HPG * 3 * BLK * HD * 4, transcendentals=0
        ),
        name="join_heads",
    )(*[x.reshape(2, groups, 3, BLK, HD) for x in parts])


def total_kernel(dq_ref, own_ref, *refs):
    terms, out_ref = refs[:-1], refs[-1]
    out_ref[:, 0] = dq_ref[...]
    total = own_ref[...].astype(F32)
    for term in terms:
        total += term[...].astype(F32)
    out_ref[:, 1:] = total.astype(BF16)


def total_grads(dq, own, terms):
    blocks, step = dq.shape[0], 4
    kv_spec = pl.BlockSpec((step, 2, BLK, HD), lambda i: (i, 0, 0, 0))
    return pl.pallas_call(
        total_kernel,
        grid=(blocks // step,),
        out_shape=jax.ShapeDtypeStruct((blocks, 3, BLK, HD), BF16),
        in_specs=[pl.BlockSpec((step, BLK, HD), lambda i: (i, 0, 0))] + [kv_spec] * (1 + len(terms)),
        out_specs=pl.BlockSpec((step, 3, BLK, HD), lambda i: (i, 0, 0, 0)),
        cost_estimate=pl.CostEstimate(
            flops=0, bytes_accessed=(6 + 2 * len(terms)) * dq.size * 2, transcendentals=0
        ),
        name="total_grads",
    )(dq, own, *terms)


def shift(value, axes, steps):
    count = lax.axis_size(axes)
    return lax.ppermute(value, axes, [(s, (s + steps) % count) for s in range(count)])


PAIR = ("core", "group")
RUNS = ("chip", "core")


def exchange(x, axes):
    return lax.all_to_all(x, axes, 0, 0)


def masks(key_blocks, block_count):
    chip, core = lax.axis_index("chip"), lax.axis_index("core")
    packed = jnp.concatenate([key_blocks, block_count[:, :, None]], axis=2)
    mine = lax.dynamic_slice_in_dim(packed, 2 * core, 2, 0)
    theirs = lax.dynamic_slice_in_dim(packed, 2 - 2 * core, 2, 0)
    theirs = lax.ppermute(theirs, "core", [(0, 1), (1, 0)])
    first, second = jnp.where(core == 0, mine, theirs), jnp.where(core == 0, theirs, mine)
    both = jnp.concatenate([first, second], axis=1)
    first_block = (2 * chip - BAND) * BPD
    result = []
    for part, row in ((both[0], 0), (both[1], 0), (packed[4], core * BPD)):
        counts = jnp.append(part[:, MAXK], jnp.int32(row))
        result.append(((part[:, :MAXK] - first_block).reshape(-1), counts))
    return result


def after(x, *done):
    return lax.optimization_barrier((x, *done))[0]


def shards(query_in, key_in, value_in, out_grad, key_blocks, block_count):
    lists = masks(key_blocks, block_count)
    kv, qd = split_heads(key_in, value_in, query_in, out_grad)
    own, queries, near, last = [None] * 3, [None] * 3, [None] * 3, ()
    for part, is_kv, wait_for in ORDER:
        ready = last if wait_for is None else (*last, *near[wait_for])
        source = after(kv[part] if is_kv else qd[part], *ready)
        got = exchange(source, PAIR if is_kv or part < 2 else "group")
        last = (got,)
        if is_kv:
            own[part] = got
            near[part] = (shift(got, "chip", 1), shift(got, "chip", -1))
        else:
            queries[part] = got
    done = []
    for part, (ids, counts) in enumerate(lists):
        sources = (near[part][0], own[part], near[part][1])
        dq, grads = attention(ids, after(counts, *[x[0] for x in done[-1:]]), sources, queries[part])
        done.append((dq, grads[1], [shift(grads[0], "chip", -1), shift(grads[2], "chip", 1)]))
    back = []
    for part, (dq, mine, terms) in enumerate(done):
        later = [x[0] for x in done[part + 1 : part + 2]] + list(near[2])
        total = total_grads(after(dq, *later, *back[-1:]), mine, terms)
        back.append(exchange(total, PAIR))
    return tuple(join_heads(*back))


def solution(mesh):
    chips = mesh.shape["frame"] // 2
    mesh = Mesh(mesh.devices.reshape(chips, 2, -1), ("chip", "core", "group"))
    tokens = P(("chip", "core", "group"), None)
    return jax.shard_map(
        shards,
        mesh=mesh,
        in_specs=(tokens,) * 4 + (P("group", RUNS, None), P("group", RUNS)),
        out_specs=(tokens,) * 3,
        check_vma=False,
    )
```

```python
import functools

import jax
import jax.numpy as jnp
from jax import lax
from jax.experimental import pallas as pl
from jax.experimental.pallas import tpu as pltpu
from jax.sharding import Mesh
from jax.sharding import PartitionSpec as P

HD = 128
BLK = 128
BAND = 2
BPD = 8
MAXK = 12
HPG = 5
GROUP = 4
ATTENTION_COST = 10
VMEM_LIMIT = 56 * 2**20
NEG = -1e30
LOG2E = 1.4426950408889634
SCALE = HD**-0.5
F32 = jnp.float32
BF16 = jnp.bfloat16
NT = (((1,), (1,)), ((), ()))
NN = (((1,), (0,)), ((), ()))
TN = (((0,), (0,)), ((), ()))


def dot(a, b, dims):
    return lax.dot_general(a, b, dims, preferred_element_type=F32)


def fold(x):
    return x.reshape(-1, 8, HD)


def query_block(n_keys, b, ids_ref, count, qd, keys, values, acc, dq, kcat, s_scr, dp_scr, ds_scr):
    q = qd[b, 0]
    do = qd[b, 1]
    base = b * MAXK
    m8 = jnp.full((8, HD), NEG, F32)
    index = [ids_ref[base + s] for s in range(n_keys)]
    for s in range(n_keys):
        k = keys[index[s]]
        kcat[pl.ds(s * BLK, BLK), :] = k
        st = dot(k, q, NT)
        if s > n_keys - GROUP:
            st = jnp.where(s < count, st, NEG)
        s_scr[s] = st
        m8 = jnp.maximum(m8, jnp.max(fold(st), axis=0))
        dp_scr[s] = dot(values[index[s]], do, NT)
    m = jnp.max(m8, axis=0, keepdims=True) * (SCALE * LOG2E)
    l8 = jnp.zeros((8, HD), F32)
    r8 = jnp.zeros((8, HD), F32)
    for s in range(n_keys):
        p = jnp.exp2(s_scr[s] * (SCALE * LOG2E) - m)
        s_scr[s] = p
        l8 += jnp.sum(fold(p), axis=0)
        r8 += jnp.sum(fold(p * dp_scr[s]), axis=0)
    inv = 1.0 / jnp.sum(l8, axis=0, keepdims=True)
    rd = jnp.sum(r8, axis=0, keepdims=True) * inv
    for s in range(n_keys):
        p = s_scr[s] * inv
        ds = (p * (dp_scr[s] - rd)).astype(BF16)
        ds_scr[pl.ds(s * BLK, BLK), :] = ds
        acc[index[s], 0] += dot(ds, q, NN)
        acc[index[s], 1] += dot(p.astype(BF16), do, NN)
    rows = pl.ds(0, n_keys * BLK)
    dq[...] = (dot(ds_scr[rows, :], kcat[rows, :], TN) * SCALE).astype(BF16)


def attention_kernel(size, n_query, fetches, ids_ref, cnt_ref, place_ref, *refs):
    sources, refs = refs[: len(fetches)], refs[len(fetches) :]
    qd_in, dq_out, left_out, own_out, right_out = refs[:5]
    keys, values, qd, acc, stage, dq, kcat, s_scr, dp_scr, ds_scr, in_sem, out_sem = refs[5:]
    copies = []
    for source, fetch in zip(sources, fetches):
        for src, t, i in fetch(source, place_ref):
            dst = (keys, values)[t].at[pl.ds(i * size, size)]
            copies.append(pltpu.make_async_copy(src, dst, in_sem.at[len(copies)]))
    q_rows = qd_in.at[pl.ds(pl.multiple_of(place_ref[0], 8), n_query)]
    copies.append(pltpu.make_async_copy(q_rows, qd, in_sem.at[len(copies)]))
    for copy in copies:
        copy.start()
    acc[...] = jnp.zeros_like(acc)
    first = place_ref[1]
    if n_query < size:
        dq[...] = jnp.zeros_like(dq)
    for copy in copies:
        copy.wait()

    def one(b, carry):
        count = cnt_ref[b]
        for upto in range(GROUP, MAXK + 1, GROUP):

            @pl.when((count > upto - GROUP) & (count <= upto))
            def _():
                query_block(
                    upto, b, ids_ref, count, qd, keys, values, acc, dq.at[first + b], kcat, s_scr, dp_scr, ds_scr
                )

        return carry

    lax.fori_loop(0, n_query, one, 0)
    puts = [pltpu.make_async_copy(dq, dq_out, out_sem.at[3])]
    puts[0].start()
    for i, target in enumerate((left_out, own_out, right_out)):

        def convert(j, carry):
            stage[j, 0] = (acc[j, 0] * SCALE).astype(BF16)
            stage[j, 1] = acc[j, 1].astype(BF16)
            return carry

        lax.fori_loop(i * size, (i + 1) * size, convert, 0)
        puts.append(pltpu.make_async_copy(stage.at[pl.ds(i * size, size)], target, out_sem.at[i]))
        puts[-1].start()
    for copy in puts:
        copy.wait()


def attention(ids, counts, place, sources, fetches, qd, n_query, size):
    window = 3 * size
    smem = pl.BlockSpec(memory_space=pltpu.SMEM)
    hbm = pl.BlockSpec(memory_space=pl.ANY)
    pairs = n_query * 8
    out = pl.pallas_call(
        functools.partial(attention_kernel, size, n_query, fetches),
        out_shape=[jax.ShapeDtypeStruct((size, BLK, HD), BF16)]
        + [jax.ShapeDtypeStruct((size, 2, BLK, HD), BF16)] * 3,
        in_specs=[smem] * 3 + [hbm] * (len(sources) + 1),
        out_specs=[hbm] * 4,
        scratch_shapes=[
            pltpu.VMEM((window, BLK, HD), BF16),
            pltpu.VMEM((window, BLK, HD), BF16),
            pltpu.VMEM((n_query, 2, BLK, HD), BF16),
            pltpu.VMEM((window, 2, BLK, HD), F32),
            pltpu.VMEM((window, 2, BLK, HD), BF16),
            pltpu.VMEM((size, BLK, HD), BF16),
            pltpu.VMEM((MAXK * BLK, HD), BF16),
            pltpu.VMEM((MAXK, BLK, HD), F32),
            pltpu.VMEM((MAXK, BLK, HD), F32),
            pltpu.VMEM((MAXK * BLK, HD), BF16),
            pltpu.SemaphoreType.DMA((7,)),
            pltpu.SemaphoreType.DMA((4,)),
        ],
        compiler_params=pltpu.CompilerParams(vmem_limit_bytes=VMEM_LIMIT),
        cost_estimate=pl.CostEstimate(
            flops=pairs * ATTENTION_COST * BLK * BLK * HD,
            bytes_accessed=(2 * window + n_query) * 2 * BLK * HD * 2,
            transcendentals=pairs * BLK * BLK,
        ),
        name="attention",
    )(ids, counts, place, *sources, qd)
    return out[0], out[1:]


def split_kernel(k_ref, v_ref, q_ref, g_ref, ka_ref, va_ref, qda_ref, kvb_ref, qdb_ref):
    for j in range(ka_ref.shape[1]):

        def head(ref, m):
            return ref[:, (j * HPG + m) * HD : (j * HPG + m + 1) * HD]

        for m in range(4):
            ka_ref[m, j] = head(k_ref, m)
            va_ref[m, j] = head(v_ref, m)
            qda_ref[m, j, 0] = head(q_ref, m)
            qda_ref[m, j, 1] = head(g_ref, m)
        for core in range(2):
            kvb_ref[core, j, 0] = head(k_ref, 4)
            kvb_ref[core, j, 1] = head(v_ref, 4)
        qdb_ref[j, 0] = head(q_ref, 4)
        qdb_ref[j, 1] = head(g_ref, 4)


def split_heads(key_in, value_in, query_in, out_grad):
    groups, step = key_in.shape[1] // (HPG * HD), 2

    one = pl.BlockSpec((4, step, BLK, HD), lambda j: (0, j, 0, 0))
    two = pl.BlockSpec((4, step, 2, BLK, HD), lambda j: (0, j, 0, 0, 0))
    kvb = pl.BlockSpec((2, step, 2, BLK, HD), lambda j: (0, j, 0, 0, 0))
    qdb = pl.BlockSpec((step, 2, BLK, HD), lambda j: (j, 0, 0, 0))
    shapes = ((4, groups), (4, groups), (4, groups, 2), (2, groups, 2), (groups, 2))
    ka, va, qda, kvb_out, qdb_out = pl.pallas_call(
        split_kernel,
        grid=(groups // step,),
        out_shape=tuple(jax.ShapeDtypeStruct((*x, BLK, HD), BF16) for x in shapes),
        in_specs=[pl.BlockSpec((BLK, step * HPG * HD), lambda j: (0, j))] * 4,
        out_specs=(one, one, two, kvb, qdb),
        compiler_params=pltpu.CompilerParams(vmem_limit_bytes=VMEM_LIMIT),
        cost_estimate=pl.CostEstimate(flops=0, bytes_accessed=16 * key_in.size, transcendentals=0),
        name="split_heads",
    )(key_in, value_in, query_in, out_grad)
    flat = 4 * groups
    return (
        ka.reshape(flat, BLK, HD),
        va.reshape(flat, BLK, HD),
        qda.reshape(flat, 2, BLK, HD),
        kvb_out.reshape(2 * groups, 2, BLK, HD),
        qdb_out,
    )


def join_kernel(dqa_ref, dkva_ref, b_ref, *outs):
    for t, ref in enumerate(outs):
        for j in range(dqa_ref.shape[1]):

            def put(m, value):
                ref[:, (j * HPG + m) * HD : (j * HPG + m + 1) * HD] = value

            for m in range(4):
                put(m, dqa_ref[m, j] if t == 0 else dkva_ref[m, j, t - 1])
            put(4, (b_ref[0, j, t].astype(F32) + b_ref[1, j, t].astype(F32)).astype(BF16))


def join_heads(dqa, dkva, back_b):
    groups, step = dqa.shape[0] // 4, 2
    out = jax.ShapeDtypeStruct((BLK, groups * HPG * HD), BF16)
    return pl.pallas_call(
        join_kernel,
        grid=(groups // step,),
        out_shape=(out,) * 3,
        in_specs=[
            pl.BlockSpec((4, step, BLK, HD), lambda j: (0, j, 0, 0)),
            pl.BlockSpec((4, step, 2, BLK, HD), lambda j: (0, j, 0, 0, 0)),
            pl.BlockSpec((2, step, 3, BLK, HD), lambda j: (0, j, 0, 0, 0)),
        ],
        out_specs=(pl.BlockSpec((BLK, step * HPG * HD), lambda j: (0, j)),) * 3,
        compiler_params=pltpu.CompilerParams(vmem_limit_bytes=VMEM_LIMIT),
        cost_estimate=pl.CostEstimate(
            flops=0, bytes_accessed=groups * HPG * 3 * BLK * HD * 4, transcendentals=0
        ),
        name="join_heads",
    )(
        dqa.reshape(4, groups, BLK, HD),
        dkva.reshape(4, groups, 2, BLK, HD),
        back_b.reshape(2, groups, 3, BLK, HD),
    )


def total_kernel(dq_ref, own_ref, *refs):
    terms, out_ref = refs[:-1], refs[-1]
    out_ref[:, 0] = dq_ref[...]
    total = own_ref[...].astype(F32)
    for term in terms:
        total += term[...].astype(F32)
    out_ref[:, 1:] = total.astype(BF16)


def total_grads(dq, own, terms):
    blocks, step = dq.shape[0], 4
    kv_spec = pl.BlockSpec((step, 2, BLK, HD), lambda i: (i, 0, 0, 0))
    return pl.pallas_call(
        total_kernel,
        grid=(blocks // step,),
        out_shape=jax.ShapeDtypeStruct((blocks, 3, BLK, HD), BF16),
        in_specs=[pl.BlockSpec((step, BLK, HD), lambda i: (i, 0, 0))] + [kv_spec] * (1 + len(terms)),
        out_specs=pl.BlockSpec((step, 3, BLK, HD), lambda i: (i, 0, 0, 0)),
        cost_estimate=pl.CostEstimate(
            flops=0, bytes_accessed=(6 + 2 * len(terms)) * dq.size * 2, transcendentals=0
        ),
        name="total_grads",
    )(dq, own, *terms)


def both_halves_kernel(x_ref, own0, own1, right0, right1, left0, left1, out_ref):
    x = x_ref[0]
    for s, own in enumerate((own0, own1)):
        right = jnp.where(x == x_ref[1], (right1, right0)[s][...], (right0, right1)[s][...])
        left = jnp.where(x == 0, (left1, left0)[s][...], (left0, left1)[s][...])
        total = own[...].astype(F32) + right.astype(F32) + left.astype(F32)
        out_ref[s] = total.astype(BF16)


def both_halves(x, last, own, from_right, from_left):
    blocks, step = own[0].shape[0], 4
    spec = pl.BlockSpec((step, 2, BLK, HD), lambda i: (i, 0, 0, 0))
    out = pl.pallas_call(
        both_halves_kernel,
        grid=(blocks // step,),
        out_shape=jax.ShapeDtypeStruct((2, blocks, 2, BLK, HD), BF16),
        in_specs=[pl.BlockSpec(memory_space=pltpu.SMEM)] + [spec] * 6,
        out_specs=pl.BlockSpec((2, step, 2, BLK, HD), lambda i: (0, i, 0, 0, 0)),
        cost_estimate=pl.CostEstimate(flops=0, bytes_accessed=16 * own[0].size, transcendentals=0),
        name="both_halves",
    )(jnp.stack([x, jnp.int32(last)]), *own, *from_right, *from_left)
    return out.reshape(2 * blocks, 2, BLK, HD)


WIDE = ("half", "core", "group")
PAIR = ("core", "group")
CHIPS = ("half", "x")


def shift(value, axes, steps):
    count = lax.axis_size(axes)
    return lax.ppermute(value, axes, [(s, (s + steps) % count) for s in range(count)])


def exchange(x, axes):
    return lax.all_to_all(x, axes, 0, 0, tiled=True)


def after(x, *done):
    return lax.optimization_barrier((x, *done))[0]


def shards(query_in, key_in, value_in, out_grad, key_blocks, block_count):
    half, x, core = (lax.axis_index(name) for name in ("half", "x", "core"))
    last = lax.axis_size("x") - 1
    packed = jnp.concatenate([key_blocks, block_count[:, :, None]], axis=2)
    ka, va, qda, kvb, qdb = split_heads(key_in, value_in, query_in, out_grad)

    keys = exchange(ka, WIDE)
    key_near = [shift(keys, "x", 1), shift(keys, "x", -1)]
    values = exchange(after(va, keys), WIDE)
    value_near = [shift(values, "x", 1), shift(values, "x", -1)]
    queries = exchange(after(qda, values, *key_near), WIDE)
    lists = lax.all_gather(packed[:4], ("half", "core"))
    lists = lax.dynamic_index_in_dim(lists, 2 * half + core, 1, False)
    own_b = exchange(after(kvb, queries, *key_near, *value_near), PAIR)
    near_b = [shift(own_b, CHIPS, 1), shift(own_b, CHIPS, -1)]
    queries_b = exchange(after(qdb, own_b), "group")

    def plain(lists, chip):
        lists = lists.reshape(-1, MAXK + 1)
        first_block = (chip - 1) * 2 * BPD
        return (lists[:, :MAXK] - first_block).reshape(-1), lists[:, MAXK]

    def third(t, i):
        return lambda ref, place: [(ref.at[pl.ds(pl.multiple_of(place[2 + i], 8), size)], t, i)]

    size = 2 * BPD
    fetches = [third(t, i) for t in range(2) for i in range(3)]
    sources = (key_near[0], keys, key_near[1], value_near[0], values, value_near[1])
    done = []
    for s in range(2):
        ids, counts = plain(lists[2 * s : 2 * s + 2], s * (last + 1) + x)
        left = jnp.where(x == 0, 1 - s, s) * size
        right = jnp.where(x == last, 1 - s, s) * size
        place = jnp.stack([jnp.int32(s * size), jnp.int32(0), left, jnp.int32(s * size), right])
        place = after(place, *[d[0] for d in done])
        dq, grads = attention(ids, counts, place, sources, fetches, queries, size, size)
        done.append((dq, grads, shift(grads[0], "x", -1), shift(grads[2], "x", 1)))

    def pair(i):
        return lambda ref, place: [(ref.at[:, t], t, i) for t in range(2)]

    ids, counts = plain(packed[4], half * (last + 1) + x)
    place = jnp.stack([jnp.int32(0), core * BPD])
    place = after(place, done[1][0], done[0][2], done[0][3])
    dq_b, grads_b = attention(
        ids, counts, place, (near_b[0], own_b, near_b[1]), [pair(i) for i in range(3)], queries_b, BPD, size
    )
    terms_b = [shift(grads_b[0], CHIPS, -1), shift(grads_b[2], CHIPS, 1)]

    dqa = jnp.concatenate([done[0][0], done[1][0]])
    dqa = exchange(after(dqa, *near_b), WIDE)
    dkva = both_halves(
        after(x, dq_b), last, [d[1][1] for d in done], [d[2] for d in done], [d[3] for d in done]
    )
    dkva = exchange(after(dkva, dqa), WIDE)
    back_b = exchange(after(total_grads(dq_b, grads_b[1], terms_b), dkva), PAIR)
    return tuple(join_heads(dqa, dkva, back_b))


def solution(mesh):
    chips = mesh.shape["frame"] // 4
    mesh = Mesh(mesh.devices.reshape(2, chips, 2, -1), ("half", "x", "core", "group"))
    runs = ("half", "x", "core")
    tokens = P((*runs, "group"), None)
    return jax.shard_map(
        shards,
        mesh=mesh,
        in_specs=(tokens,) * 4 + (P("group", runs, None), P("group", runs)),
        out_specs=(tokens,) * 3,
        check_vma=False,
    )
```

```python
import functools

import jax
import jax.numpy as jnp
from jax import lax
from jax.experimental import pallas as pl
from jax.experimental.pallas import tpu as pltpu
from jax.sharding import Mesh
from jax.sharding import PartitionSpec as P

HD = 128
BLK = 128
BAND = 2
BPD = 8
MAXK = 12
HPG = 5
GROUP = 4
ATTENTION_COST = 10
VMEM_LIMIT = 56 * 2**20
NEG = -1e30
LOG2E = 1.4426950408889634
SCALE = HD**-0.5
F32 = jnp.float32
BF16 = jnp.bfloat16
NT = (((1,), (1,)), ((), ()))
NN = (((1,), (0,)), ((), ()))
TN = (((0,), (0,)), ((), ()))


def dot(a, b, dims):
    return lax.dot_general(a, b, dims, preferred_element_type=F32)


def fold(x):
    return x.reshape(-1, 8, HD)


def query_block(n_keys, b, ids_ref, count, qd, keys, values, acc, dq, kcat, s_scr, dp_scr, ds_scr):
    q = qd[b, 0]
    do = qd[b, 1]
    base = b * MAXK
    m8 = jnp.full((8, HD), NEG, F32)
    index = [ids_ref[base + s] for s in range(n_keys)]
    for s in range(n_keys):
        k = keys[index[s]]
        kcat[pl.ds(s * BLK, BLK), :] = k
        st = dot(k, q, NT)
        if s > n_keys - GROUP:
            st = jnp.where(s < count, st, NEG)
        s_scr[s] = st
        m8 = jnp.maximum(m8, jnp.max(fold(st), axis=0))
        dp_scr[s] = dot(values[index[s]], do, NT)
    m = jnp.max(m8, axis=0, keepdims=True) * (SCALE * LOG2E)
    l8 = jnp.zeros((8, HD), F32)
    r8 = jnp.zeros((8, HD), F32)
    for s in range(n_keys):
        p = jnp.exp2(s_scr[s] * (SCALE * LOG2E) - m)
        s_scr[s] = p
        l8 += jnp.sum(fold(p), axis=0)
        r8 += jnp.sum(fold(p * dp_scr[s]), axis=0)
    inv = 1.0 / jnp.sum(l8, axis=0, keepdims=True)
    rd = jnp.sum(r8, axis=0, keepdims=True) * inv
    for s in range(n_keys):
        p = s_scr[s] * inv
        ds = (p * (dp_scr[s] - rd)).astype(BF16)
        ds_scr[pl.ds(s * BLK, BLK), :] = ds
        acc[index[s], 0] += dot(ds, q, NN)
        acc[index[s], 1] += dot(p.astype(BF16), do, NN)
    rows = pl.ds(0, n_keys * BLK)
    dq[...] = (dot(ds_scr[rows, :], kcat[rows, :], TN) * SCALE).astype(BF16)


def attention_kernel(size, n_query, fetches, ids_ref, cnt_ref, place_ref, *refs):
    sources, refs = refs[: len(fetches)], refs[len(fetches) :]
    shared = n_query < size
    qd_in, dq_out, targets = refs[0], refs[1], refs[2:5]
    if shared:
        give_out, refs = refs[5], refs[1:]
    keys, values, qd, acc, stage, dq, kcat, s_scr, dp_scr, ds_scr, in_sem, out_sem = refs[5:]
    copies = []
    for source, fetch in zip(sources, fetches):
        for src, t, i in fetch(source, place_ref):
            dst = (keys, values)[t].at[pl.ds(i * size, size)]
            copies.append(pltpu.make_async_copy(src, dst, in_sem.at[len(copies)]))
    q_rows = qd_in.at[pl.ds(pl.multiple_of(place_ref[0], 8), n_query)]
    copies.append(pltpu.make_async_copy(q_rows, qd, in_sem.at[len(copies)]))
    for copy in copies:
        copy.start()
    acc[...] = jnp.zeros_like(acc)
    for copy in copies:
        copy.wait()

    def one(b, carry):
        count = cnt_ref[b]
        for upto in range(GROUP, MAXK + 1, GROUP):

            @pl.when((count > upto - GROUP) & (count <= upto))
            def _():
                query_block(
                    upto, b, ids_ref, count, qd, keys, values, acc, dq.at[b], kcat, s_scr, dp_scr, ds_scr
                )

        return carry

    lax.fori_loop(0, n_query, one, 0)
    puts = [pltpu.make_async_copy(dq, dq_out, out_sem.at[3])]
    puts[0].start()
    for i, target in enumerate(targets):

        def convert(j, carry):
            stage[j, 0] = (acc[j, 0] * SCALE).astype(BF16)
            stage[j, 1] = acc[j, 1].astype(BF16)
            return carry

        lax.fori_loop(i * size, (i + 1) * size, convert, 0)
        rows = pl.ds(i * size, size)
        if shared:
            keep = pl.multiple_of(i * size + place_ref[1], 8)
            give = pl.multiple_of(i * size + n_query - place_ref[1], 8)
            rows = pl.ds(keep, n_query)
            puts.append(
                pltpu.make_async_copy(stage.at[pl.ds(give, n_query)], give_out.at[i], out_sem.at[4 + i])
            )
            puts[-1].start()
        puts.append(pltpu.make_async_copy(stage.at[rows], target, out_sem.at[i]))
        puts[-1].start()
    for copy in puts:
        copy.wait()


def attention(ids, counts, place, sources, fetches, qd, n_query, size):
    window = 3 * size
    shared = n_query < size
    kept = jax.ShapeDtypeStruct((n_query, 2, BLK, HD), BF16)
    given = [jax.ShapeDtypeStruct((3, n_query, 2, BLK, HD), BF16)] if shared else []
    smem = pl.BlockSpec(memory_space=pltpu.SMEM)
    hbm = pl.BlockSpec(memory_space=pl.ANY)
    pairs = n_query * 8
    out = pl.pallas_call(
        functools.partial(attention_kernel, size, n_query, fetches),
        out_shape=[jax.ShapeDtypeStruct((n_query, BLK, HD), BF16)] + [kept] * 3 + given,
        in_specs=[smem] * 3 + [hbm] * (len(sources) + 1),
        out_specs=[hbm] * (4 + len(given)),
        scratch_shapes=[
            pltpu.VMEM((window, BLK, HD), BF16),
            pltpu.VMEM((window, BLK, HD), BF16),
            pltpu.VMEM((n_query, 2, BLK, HD), BF16),
            pltpu.VMEM((window, 2, BLK, HD), F32),
            pltpu.VMEM((window, 2, BLK, HD), BF16),
            pltpu.VMEM((n_query, BLK, HD), BF16),
            pltpu.VMEM((MAXK * BLK, HD), BF16),
            pltpu.VMEM((MAXK, BLK, HD), F32),
            pltpu.VMEM((MAXK, BLK, HD), F32),
            pltpu.VMEM((MAXK * BLK, HD), BF16),
            pltpu.SemaphoreType.DMA((7,)),
            pltpu.SemaphoreType.DMA((7,)),
        ],
        compiler_params=pltpu.CompilerParams(vmem_limit_bytes=VMEM_LIMIT),
        cost_estimate=pl.CostEstimate(
            flops=0 if shared else pairs * ATTENTION_COST * BLK * BLK * HD,
            bytes_accessed=0 if shared else (2 * window + n_query) * 2 * BLK * HD * 2,
            transcendentals=0 if shared else pairs * BLK * BLK,
        ),
        name="attention",
    )(ids, counts, place, *sources, qd)
    return out[0], out[1:]


def split_kernel(k_ref, v_ref, q_ref, g_ref, ka_ref, va_ref, qda_ref, kvb_ref, qdb_ref):
    for j in range(ka_ref.shape[1]):

        def head(ref, m):
            return ref[:, (j * HPG + m) * HD : (j * HPG + m + 1) * HD]

        for m in range(4):
            ka_ref[m, j] = head(k_ref, m)
            va_ref[m, j] = head(v_ref, m)
            qda_ref[m, j, 0] = head(q_ref, m)
            qda_ref[m, j, 1] = head(g_ref, m)
        for core in range(2):
            kvb_ref[core, j, 0] = head(k_ref, 4)
            kvb_ref[core, j, 1] = head(v_ref, 4)
        qdb_ref[j, 0] = head(q_ref, 4)
        qdb_ref[j, 1] = head(g_ref, 4)


def split_heads(key_in, value_in, query_in, out_grad):
    groups, step = key_in.shape[1] // (HPG * HD), 2

    one = pl.BlockSpec((4, step, BLK, HD), lambda j: (0, j, 0, 0))
    two = pl.BlockSpec((4, step, 2, BLK, HD), lambda j: (0, j, 0, 0, 0))
    kvb = pl.BlockSpec((2, step, 2, BLK, HD), lambda j: (0, j, 0, 0, 0))
    qdb = pl.BlockSpec((step, 2, BLK, HD), lambda j: (j, 0, 0, 0))
    shapes = ((4, groups), (4, groups), (4, groups, 2), (2, groups, 2), (groups, 2))
    ka, va, qda, kvb_out, qdb_out = pl.pallas_call(
        split_kernel,
        grid=(groups // step,),
        out_shape=tuple(jax.ShapeDtypeStruct((*x, BLK, HD), BF16) for x in shapes),
        in_specs=[pl.BlockSpec((BLK, step * HPG * HD), lambda j: (0, j))] * 4,
        out_specs=(one, one, two, kvb, qdb),
        compiler_params=pltpu.CompilerParams(vmem_limit_bytes=VMEM_LIMIT),
        cost_estimate=pl.CostEstimate(flops=0, bytes_accessed=16 * key_in.size, transcendentals=0),
        name="split_heads",
    )(key_in, value_in, query_in, out_grad)
    flat = 4 * groups
    return (
        ka.reshape(flat, BLK, HD),
        va.reshape(flat, BLK, HD),
        qda.reshape(flat, 2, BLK, HD),
        kvb_out.reshape(2 * groups, 2, BLK, HD),
        qdb_out,
    )


def join_kernel(a_ref, b_ref, *outs):
    for t, ref in enumerate(outs):
        for j in range(b_ref.shape[0]):
            for m in range(HPG):
                value = a_ref[m, j, t] if m < 4 else b_ref[j, t]
                ref[:, (j * HPG + m) * HD : (j * HPG + m + 1) * HD] = value


def join_heads(back_a, back_b):
    groups, step = back_b.shape[0], 2
    out = jax.ShapeDtypeStruct((BLK, groups * HPG * HD), BF16)
    return pl.pallas_call(
        join_kernel,
        grid=(groups // step,),
        out_shape=(out,) * 3,
        in_specs=[
            pl.BlockSpec((4, step, 3, BLK, HD), lambda j: (0, j, 0, 0, 0)),
            pl.BlockSpec((step, 3, BLK, HD), lambda j: (j, 0, 0, 0)),
        ],
        out_specs=(pl.BlockSpec((BLK, step * HPG * HD), lambda j: (0, j)),) * 3,
        compiler_params=pltpu.CompilerParams(vmem_limit_bytes=VMEM_LIMIT),
        cost_estimate=pl.CostEstimate(
            flops=0, bytes_accessed=groups * HPG * 3 * BLK * HD * 4, transcendentals=0
        ),
        name="join_heads",
    )(back_a.reshape(4, groups, 3, BLK, HD), back_b)


def total_kernel(dq_ref, own_ref, *refs):
    terms, out_ref = refs[:-1], refs[-1]
    out_ref[:, 0] = dq_ref[...]
    total = own_ref[...].astype(F32)
    for term in terms:
        total += term[...].astype(F32)
    out_ref[:, 1:] = total.astype(BF16)


def total_grads(dq, own, terms):
    blocks, step = dq.shape[0], 4
    kv_spec = pl.BlockSpec((step, 2, BLK, HD), lambda i: (i, 0, 0, 0))
    return pl.pallas_call(
        total_kernel,
        grid=(blocks // step,),
        out_shape=jax.ShapeDtypeStruct((blocks, 3, BLK, HD), BF16),
        in_specs=[pl.BlockSpec((step, BLK, HD), lambda i: (i, 0, 0))] + [kv_spec] * (1 + len(terms)),
        out_specs=pl.BlockSpec((step, 3, BLK, HD), lambda i: (i, 0, 0, 0)),
        cost_estimate=pl.CostEstimate(
            flops=0, bytes_accessed=(6 + 2 * len(terms)) * dq.size * 2, transcendentals=0
        ),
        name="total_grads",
    )(dq, own, *terms)


def both_halves_kernel(x_ref, dq0, dq1, own0, own1, right0, right1, left0, left1, out_ref):
    x = x_ref[0]
    for s, (dq, own) in enumerate(((dq0, own0), (dq1, own1))):
        right = jnp.where(x == x_ref[1], (right1, right0)[s][...], (right0, right1)[s][...])
        left = jnp.where(x == 0, (left1, left0)[s][...], (left0, left1)[s][...])
        total = own[...].astype(F32) + right.astype(F32) + left.astype(F32)
        out_ref[s, :, 0] = dq[...]
        out_ref[s, :, 1:] = total.astype(BF16)


def both_halves(x, last, dq, own, from_right, from_left):
    blocks, step = own[0].shape[0], 4
    spec = pl.BlockSpec((step, 2, BLK, HD), lambda i: (i, 0, 0, 0))
    out = pl.pallas_call(
        both_halves_kernel,
        grid=(blocks // step,),
        out_shape=jax.ShapeDtypeStruct((2, blocks, 3, BLK, HD), BF16),
        in_specs=[pl.BlockSpec(memory_space=pltpu.SMEM)]
        + [pl.BlockSpec((step, BLK, HD), lambda i: (i, 0, 0))] * 2
        + [spec] * 6,
        out_specs=pl.BlockSpec((2, step, 3, BLK, HD), lambda i: (0, i, 0, 0, 0)),
        cost_estimate=pl.CostEstimate(flops=0, bytes_accessed=20 * own[0].size, transcendentals=0),
        name="both_halves",
    )(jnp.stack([x, jnp.int32(last)]), *dq, *own, *from_right, *from_left)
    return out.reshape(2 * blocks, 3, BLK, HD)


WIDE = ("half", "core", "group")
PAIR = ("core", "group")
CHIPS = ("half", "x")


def shift(value, axes, steps):
    count = lax.axis_size(axes)
    return lax.ppermute(value, axes, [(s, (s + steps) % count) for s in range(count)])


def add(a, b):
    return (a.astype(F32) + b.astype(F32)).astype(BF16)


def exchange(x, axes):
    return lax.all_to_all(x, axes, 0, 0, tiled=True)


def after(x, *done):
    return lax.optimization_barrier((x, *done))[0]


def shards(query_in, key_in, value_in, out_grad, key_blocks, block_count):
    half, x, core = (lax.axis_index(name) for name in ("half", "x", "core"))
    last = lax.axis_size("x") - 1
    packed = jnp.concatenate([key_blocks, block_count[:, :, None]], axis=2)
    ka, va, qda, kvb, qdb = split_heads(key_in, value_in, query_in, out_grad)

    keys = exchange(ka, WIDE)
    key_near = [shift(keys, "x", 1), shift(keys, "x", -1)]
    values = exchange(after(va, keys), WIDE)
    value_near = [shift(values, "x", 1), shift(values, "x", -1)]
    queries = exchange(after(qda, values, *key_near), WIDE)
    lists = lax.all_gather(packed[:4], ("half", "core"))
    lists = lax.dynamic_index_in_dim(lists, 2 * half + core, 1, False)
    own_b = exchange(after(kvb, queries, *key_near, *value_near), PAIR)

    def plain(lists, chip):
        lists = lists.reshape(-1, MAXK + 1)
        first_block = (chip - 1) * 2 * BPD
        return (lists[:, :MAXK] - first_block).reshape(-1), lists[:, MAXK]

    def third(t, i):
        return lambda ref, place: [(ref.at[pl.ds(pl.multiple_of(place[2 + i], 8), size)], t, i)]

    size = 2 * BPD
    fetches = [third(t, i) for t in range(2) for i in range(3)]
    sources = (key_near[0], keys, key_near[1], value_near[0], values, value_near[1])
    done = []
    for s in range(2):
        ids, counts = plain(lists[2 * s : 2 * s + 2], s * (last + 1) + x)
        left = jnp.where(x == 0, 1 - s, s) * size
        right = jnp.where(x == last, 1 - s, s) * size
        place = jnp.stack([jnp.int32(s * size), jnp.int32(0), left, jnp.int32(s * size), right])
        place = after(place, *[d[0] for d in done])
        dq, grads = attention(ids, counts, place, sources, fetches, queries, size, size)
        done.append((dq, grads, shift(grads[0], "x", -1), shift(grads[2], "x", 1)))
        if s == 0:
            own_b = after(own_b, dq)
            near_b = [shift(own_b, CHIPS, 1), shift(own_b, CHIPS, -1)]
            queries_b = exchange(after(qdb, own_b), "group")

    def pair(i):
        return lambda ref, place: [(ref.at[:, t], t, i) for t in range(2)]

    ids, counts = plain(packed[4], half * (last + 1) + x)
    place = jnp.stack([jnp.int32(0), core * BPD])
    place = after(place, done[1][0], done[0][2], done[0][3])
    dq_b, (left_b, mine_b, right_b, give_b) = attention(
        ids, counts, place, (near_b[0], own_b, near_b[1]), [pair(i) for i in range(3)], queries_b, BPD, size
    )
    got_b = [lax.ppermute(give_b[i], "core", [(0, 1), (1, 0)]) for i in range(3)]
    terms_b = [
        got_b[1],
        shift(add(left_b, got_b[0]), CHIPS, -1),
        shift(add(right_b, got_b[2]), CHIPS, 1),
    ]
    total_a = both_halves(
        after(x, *terms_b[:1]),
        last,
        [d[0] for d in done],
        [d[1][1] for d in done],
        [d[2] for d in done],
        [d[3] for d in done],
    )
    back_a = exchange(total_a, WIDE)
    back_b = exchange(after(total_grads(dq_b, mine_b, terms_b), back_a), "group")
    return tuple(join_heads(back_a, back_b))


def solution(mesh):
    chips = mesh.shape["frame"] // 4
    mesh = Mesh(mesh.devices.reshape(2, chips, 2, -1), ("half", "x", "core", "group"))
    runs = ("half", "x", "core")
    tokens = P((*runs, "group"), None)
    return jax.shard_map(
        shards,
        mesh=mesh,
        in_specs=(tokens,) * 4 + (P("group", runs, None), P("group", runs)),
        out_specs=(tokens,) * 3,
        check_vma=False,
    )
```

```python
import functools

import jax
import jax.numpy as jnp
from jax import lax
from jax.experimental import pallas as pl
from jax.experimental.pallas import tpu as pltpu
from jax.sharding import Mesh
from jax.sharding import PartitionSpec as P

HD = 128
BLK = 128
BAND = 2
BPD = 8
MAXK = 12
HPG = 5
GROUP = 4
ATTENTION_COST = 10
VMEM_LIMIT = 56 * 2**20
NEG = -1e30
LOG2E = 1.4426950408889634
SCALE = HD**-0.5
F32 = jnp.float32
BF16 = jnp.bfloat16
NT = (((1,), (1,)), ((), ()))
NN = (((1,), (0,)), ((), ()))
TN = (((0,), (0,)), ((), ()))


def dot(a, b, dims):
    return lax.dot_general(a, b, dims, preferred_element_type=F32)


def fold(x):
    return x.reshape(-1, 8, HD)


def query_block(n_keys, b, ids_ref, count, qd, keys, values, acc, dq, kcat, s_scr, dp_scr, ds_scr):
    q = qd[b, 0]
    do = qd[b, 1]
    base = b * MAXK
    m8 = jnp.full((8, HD), NEG, F32)
    index = [ids_ref[base + s] for s in range(n_keys)]
    for s in range(n_keys):
        k = keys[index[s]]
        kcat[pl.ds(s * BLK, BLK), :] = k
        st = dot(k, q, NT)
        if s > n_keys - GROUP:
            st = jnp.where(s < count, st, NEG)
        s_scr[s] = st
        m8 = jnp.maximum(m8, jnp.max(fold(st), axis=0))
        dp_scr[s] = dot(values[index[s]], do, NT)
    m = jnp.max(m8, axis=0, keepdims=True) * (SCALE * LOG2E)
    l8 = jnp.zeros((8, HD), F32)
    r8 = jnp.zeros((8, HD), F32)
    for s in range(n_keys):
        p = jnp.exp2(s_scr[s] * (SCALE * LOG2E) - m)
        s_scr[s] = p
        l8 += jnp.sum(fold(p), axis=0)
        r8 += jnp.sum(fold(p * dp_scr[s]), axis=0)
    inv = 1.0 / jnp.sum(l8, axis=0, keepdims=True)
    rd = jnp.sum(r8, axis=0, keepdims=True) * inv
    for s in range(n_keys):
        p = s_scr[s] * inv
        ds = (p * (dp_scr[s] - rd)).astype(BF16)
        ds_scr[pl.ds(s * BLK, BLK), :] = ds
        acc[index[s], 0] += dot(ds, q, NN)
        acc[index[s], 1] += dot(p.astype(BF16), do, NN)
    rows = pl.ds(0, n_keys * BLK)
    dq[...] = (dot(ds_scr[rows, :], kcat[rows, :], TN) * SCALE).astype(BF16)


def attention_kernel(size, n_query, fetches, ids_ref, cnt_ref, place_ref, *refs):
    sources, refs = refs[: len(fetches)], refs[len(fetches) :]
    shared = n_query < size
    qd_in, dq_out, targets = refs[0], refs[1], refs[2:5]
    if shared:
        give_out, refs = refs[5], refs[1:]
    keys, values, qd, acc, stage, dq, kcat, s_scr, dp_scr, ds_scr, in_sem, out_sem = refs[5:]
    copies = []
    for source, fetch in zip(sources, fetches):
        for src, t, row in fetch(source, place_ref):
            dst = (keys, values)[t].at[pl.ds(row, src.shape[0])]
            copies.append(pltpu.make_async_copy(src, dst, in_sem.at[len(copies)]))
    q_rows = qd_in.at[pl.ds(pl.multiple_of(place_ref[0], 8), n_query), pl.ds(qd_in.shape[1] - 2, 2)]
    copies.append(pltpu.make_async_copy(q_rows, qd, in_sem.at[len(copies)]))
    for copy in copies:
        copy.start()
    acc[...] = jnp.zeros_like(acc)
    for copy in copies:
        copy.wait()

    def one(b, carry):
        count = cnt_ref[b]
        for upto in range(GROUP, MAXK + 1, GROUP):

            @pl.when((count > upto - GROUP) & (count <= upto))
            def _():
                query_block(
                    upto, b, ids_ref, count, qd, keys, values, acc, dq.at[b], kcat, s_scr, dp_scr, ds_scr
                )

        return carry

    lax.fori_loop(0, n_query, one, 0)
    puts = [pltpu.make_async_copy(dq, dq_out, out_sem.at[3])]
    puts[0].start()
    for i, target in enumerate(targets):

        def convert(j, carry):
            stage[j, 0] = (acc[j, 0] * SCALE).astype(BF16)
            stage[j, 1] = acc[j, 1].astype(BF16)
            return carry

        lax.fori_loop(i * size, (i + 1) * size, convert, 0)
        rows = pl.ds(i * size, size)
        if shared:
            keep = pl.multiple_of(i * size + place_ref[1], 8)
            give = pl.multiple_of(i * size + n_query - place_ref[1], 8)
            rows = pl.ds(keep, n_query)
            puts.append(
                pltpu.make_async_copy(stage.at[pl.ds(give, n_query)], give_out.at[i], out_sem.at[4 + i])
            )
            puts[-1].start()
        puts.append(pltpu.make_async_copy(stage.at[rows], target, out_sem.at[i]))
        puts[-1].start()
    for copy in puts:
        copy.wait()


def attention(ids, counts, place, sources, fetches, qd, n_query, size):
    window = 3 * size
    shared = n_query < size
    kept = jax.ShapeDtypeStruct((n_query, 2, BLK, HD), BF16)
    given = [jax.ShapeDtypeStruct((3, n_query, 2, BLK, HD), BF16)] if shared else []
    smem = pl.BlockSpec(memory_space=pltpu.SMEM)
    hbm = pl.BlockSpec(memory_space=pl.ANY)
    pairs = n_query * 8
    out = pl.pallas_call(
        functools.partial(attention_kernel, size, n_query, fetches),
        out_shape=[jax.ShapeDtypeStruct((n_query, BLK, HD), BF16)] + [kept] * 3 + given,
        in_specs=[smem] * 3 + [hbm] * (len(sources) + 1),
        out_specs=[hbm] * (4 + len(given)),
        scratch_shapes=[
            pltpu.VMEM((window, BLK, HD), BF16),
            pltpu.VMEM((window, BLK, HD), BF16),
            pltpu.VMEM((n_query, 2, BLK, HD), BF16),
            pltpu.VMEM((window, 2, BLK, HD), F32),
            pltpu.VMEM((window, 2, BLK, HD), BF16),
            pltpu.VMEM((n_query, BLK, HD), BF16),
            pltpu.VMEM((MAXK * BLK, HD), BF16),
            pltpu.VMEM((MAXK, BLK, HD), F32),
            pltpu.VMEM((MAXK, BLK, HD), F32),
            pltpu.VMEM((MAXK * BLK, HD), BF16),
            pltpu.SemaphoreType.DMA((13,)),
            pltpu.SemaphoreType.DMA((7,)),
        ],
        compiler_params=pltpu.CompilerParams(vmem_limit_bytes=VMEM_LIMIT),
        cost_estimate=pl.CostEstimate(
            flops=0 if shared else pairs * ATTENTION_COST * BLK * BLK * HD,
            bytes_accessed=0 if shared else (2 * window + n_query) * 2 * BLK * HD * 2,
            transcendentals=0 if shared else pairs * BLK * BLK,
        ),
        name="attention",
    )(ids, counts, place, *sources, qd)
    return out[0], out[1:]


def split_kernel(k_ref, v_ref, q_ref, g_ref, ka_ref, va_ref, qda_ref, b_ref):
    for j in range(ka_ref.shape[1]):

        def head(ref, m):
            return ref[:, (j * HPG + m) * HD : (j * HPG + m + 1) * HD]

        for m in range(4):
            ka_ref[m, j] = head(k_ref, m)
            va_ref[m, j] = head(v_ref, m)
            qda_ref[m, j, 0] = head(q_ref, m)
            qda_ref[m, j, 1] = head(g_ref, m)
        for t, ref in enumerate((k_ref, v_ref, q_ref, g_ref)):
            b_ref[j, t] = head(ref, 4)


def split_heads(key_in, value_in, query_in, out_grad):
    groups, step = key_in.shape[1] // (HPG * HD), 2
    one = pl.BlockSpec((4, step, BLK, HD), lambda j: (0, j, 0, 0))
    two = pl.BlockSpec((4, step, 2, BLK, HD), lambda j: (0, j, 0, 0, 0))
    four = pl.BlockSpec((step, 4, BLK, HD), lambda j: (j, 0, 0, 0))
    shapes = ((4, groups), (4, groups), (4, groups, 2), (groups, 4))
    ka, va, qda, b = pl.pallas_call(
        split_kernel,
        grid=(groups // step,),
        out_shape=tuple(jax.ShapeDtypeStruct((*x, BLK, HD), BF16) for x in shapes),
        in_specs=[pl.BlockSpec((BLK, step * HPG * HD), lambda j: (0, j))] * 4,
        out_specs=(one, one, two, four),
        compiler_params=pltpu.CompilerParams(vmem_limit_bytes=VMEM_LIMIT),
        cost_estimate=pl.CostEstimate(flops=0, bytes_accessed=16 * key_in.size, transcendentals=0),
        name="split_heads",
    )(key_in, value_in, query_in, out_grad)
    flat = 4 * groups
    return ka.reshape(flat, BLK, HD), va.reshape(flat, BLK, HD), qda.reshape(flat, 2, BLK, HD), b


def join_kernel(dqa_ref, dkva_ref, b_ref, *outs):
    for t, ref in enumerate(outs):
        for j in range(b_ref.shape[0]):
            for m in range(HPG):
                if m == 4:
                    value = b_ref[j, t]
                else:
                    value = dqa_ref[m, j] if t == 0 else dkva_ref[m, j, t - 1]
                ref[:, (j * HPG + m) * HD : (j * HPG + m + 1) * HD] = value


def join_heads(dqa, dkva, back_b):
    groups, step = back_b.shape[0], 2
    out = jax.ShapeDtypeStruct((BLK, groups * HPG * HD), BF16)
    return pl.pallas_call(
        join_kernel,
        grid=(groups // step,),
        out_shape=(out,) * 3,
        in_specs=[
            pl.BlockSpec((4, step, BLK, HD), lambda j: (0, j, 0, 0)),
            pl.BlockSpec((4, step, 2, BLK, HD), lambda j: (0, j, 0, 0, 0)),
            pl.BlockSpec((step, 3, BLK, HD), lambda j: (j, 0, 0, 0)),
        ],
        out_specs=(pl.BlockSpec((BLK, step * HPG * HD), lambda j: (0, j)),) * 3,
        compiler_params=pltpu.CompilerParams(vmem_limit_bytes=VMEM_LIMIT),
        cost_estimate=pl.CostEstimate(
            flops=0, bytes_accessed=groups * HPG * 3 * BLK * HD * 4, transcendentals=0
        ),
        name="join_heads",
    )(dqa.reshape(4, groups, BLK, HD), dkva.reshape(4, groups, 2, BLK, HD), back_b)


def total_kernel(dq_ref, own_ref, *refs):
    terms, out_ref = refs[:-1], refs[-1]
    out_ref[:, 0] = dq_ref[...]
    total = own_ref[...].astype(F32)
    for term in terms:
        total += term[...].astype(F32)
    out_ref[:, 1:] = total.astype(BF16)


def total_grads(dq, own, terms):
    blocks, step = dq.shape[0], 4
    kv_spec = pl.BlockSpec((step, 2, BLK, HD), lambda i: (i, 0, 0, 0))
    return pl.pallas_call(
        total_kernel,
        grid=(blocks // step,),
        out_shape=jax.ShapeDtypeStruct((blocks, 3, BLK, HD), BF16),
        in_specs=[pl.BlockSpec((step, BLK, HD), lambda i: (i, 0, 0))] + [kv_spec] * (1 + len(terms)),
        out_specs=pl.BlockSpec((step, 3, BLK, HD), lambda i: (i, 0, 0, 0)),
        cost_estimate=pl.CostEstimate(
            flops=0, bytes_accessed=(6 + 2 * len(terms)) * dq.size * 2, transcendentals=0
        ),
        name="total_grads",
    )(dq, own, *terms)


def both_halves_kernel(x_ref, own0, own1, right0, right1, left0, left1, out_ref):
    x = x_ref[0]
    for s, own in enumerate((own0, own1)):
        right = jnp.where(x == x_ref[1], (right1, right0)[s][...], (right0, right1)[s][...])
        left = jnp.where(x == 0, (left1, left0)[s][...], (left0, left1)[s][...])
        total = own[...].astype(F32) + right.astype(F32) + left.astype(F32)
        out_ref[s] = total.astype(BF16)


def both_halves(x, last, own, from_right, from_left):
    blocks, step = own[0].shape[0], 4
    spec = pl.BlockSpec((step, 2, BLK, HD), lambda i: (i, 0, 0, 0))
    out = pl.pallas_call(
        both_halves_kernel,
        grid=(blocks // step,),
        out_shape=jax.ShapeDtypeStruct((2, blocks, 2, BLK, HD), BF16),
        in_specs=[pl.BlockSpec(memory_space=pltpu.SMEM)] + [spec] * 6,
        out_specs=pl.BlockSpec((2, step, 2, BLK, HD), lambda i: (0, i, 0, 0, 0)),
        cost_estimate=pl.CostEstimate(flops=0, bytes_accessed=16 * own[0].size, transcendentals=0),
        name="both_halves",
    )(jnp.stack([x, jnp.int32(last)]), *own, *from_right, *from_left)
    return out.reshape(2 * blocks, 2, BLK, HD)


WIDE = ("half", "core", "group")
PAIR = ("core", "group")
CHIPS = ("half", "x")


def shift(value, axes, steps):
    count = lax.axis_size(axes)
    return lax.ppermute(value, axes, [(s, (s + steps) % count) for s in range(count)])


def add(a, b):
    return (a.astype(F32) + b.astype(F32)).astype(BF16)


def exchange(x, axes):
    return lax.all_to_all(x, axes, 0, 0, tiled=True)


def after(x, *done):
    return lax.optimization_barrier((x, *done))[0]


def swap(value):
    return lax.ppermute(value, "core", [(0, 1), (1, 0)])


def shards(query_in, key_in, value_in, out_grad, key_blocks, block_count):
    half, x, core = (lax.axis_index(name) for name in ("half", "x", "core"))
    last, size = lax.axis_size("x") - 1, 2 * BPD
    packed = jnp.concatenate([key_blocks, block_count[:, :, None]], axis=2)
    lists = lax.all_gather(packed[:4], ("half", "core"))
    lists = lax.dynamic_index_in_dim(lists, 2 * half + core, 1, False)
    ka, va, qda, b = split_heads(key_in, value_in, query_in, out_grad)

    def plain(lists, chip):
        lists = lists.reshape(-1, MAXK + 1)
        first_block = (chip - 1) * 2 * BPD
        return (lists[:, :MAXK] - first_block).reshape(-1), lists[:, MAXK]

    own_b = exchange(b, "group")
    pairs_b = own_b[:, :2]
    mine = (shift(pairs_b, CHIPS, 1), pairs_b, shift(pairs_b, CHIPS, -1))
    theirs = tuple(swap(pairs) for pairs in mine)

    keys = exchange(after(ka, own_b), WIDE)
    key_near = [shift(keys, "x", 1), shift(keys, "x", -1)]
    values = exchange(after(va, keys, *mine), WIDE)
    value_near = [shift(values, "x", 1), shift(values, "x", -1)]

    def run(i, other):
        def fetch(ref, place):
            at = i * size + (BPD - place[1] if other else place[1])
            return [(ref.at[:, t], t, pl.multiple_of(at, 8)) for t in range(2)]

        return fetch

    ids, counts = plain(packed[4], half * (last + 1) + x)
    place = after(jnp.stack([jnp.int32(0), core * BPD]), keys, lists)
    fetches = [run(i, other) for other in range(2) for i in range(3)]
    dq_b, (left_b, mine_b, right_b, give_b) = attention(
        ids, counts, place, mine + theirs, fetches, own_b, BPD, size
    )
    got_b = [swap(give_b[i]) for i in range(3)]
    out_b = lax.optimization_barrier((add(left_b, got_b[0]), add(right_b, got_b[2]), *value_near))
    terms_b = [got_b[1], shift(out_b[0], CHIPS, -1), shift(out_b[1], CHIPS, 1)]

    queries = exchange(after(qda, values, dq_b, *key_near), WIDE)

    def third(t, i):
        return lambda ref, place: [(ref.at[pl.ds(pl.multiple_of(place[1 + i], 8), size)], t, i * size)]

    fetches = [third(t, i) for t in range(2) for i in range(3)]
    sources = (key_near[0], keys, key_near[1], value_near[0], values, value_near[1])
    done, back_b = [], ()
    for s in range(2):
        ids, counts = plain(lists[2 * s : 2 * s + 2], s * (last + 1) + x)
        left = jnp.where(x == 0, 1 - s, s) * size
        right = jnp.where(x == last, 1 - s, s) * size
        place = after(jnp.stack([jnp.int32(s * size), left, jnp.int32(s * size), right]), *back_b)
        dq, grads = attention(ids, counts, place, sources, fetches, queries, size, size)
        done.append((dq, grads, shift(grads[0], "x", -1), shift(grads[2], "x", 1)))
        if s == 0:
            total_b = total_grads(after(dq_b, dq), mine_b, terms_b)
            back_b = (total_b,)
    back_b = exchange(total_b, "group")
    dqa = exchange(after(jnp.concatenate([d[0] for d in done]), *done[0][2:], back_b), WIDE)
    dkva = both_halves(x, last, [d[1][1] for d in done], [d[2] for d in done], [d[3] for d in done])
    dkva = exchange(after(dkva, dqa), WIDE)
    return tuple(join_heads(dqa, dkva, back_b))


def solution(mesh):
    chips = mesh.shape["frame"] // 4
    mesh = Mesh(mesh.devices.reshape(2, chips, 2, -1), ("half", "x", "core", "group"))
    runs = ("half", "x", "core")
    tokens = P((*runs, "group"), None)
    return jax.shard_map(
        shards,
        mesh=mesh,
        in_specs=(tokens,) * 4 + (P("group", runs, None), P("group", runs)),
        out_specs=(tokens,) * 3,
        check_vma=False,
    )
```

```python
import functools

import jax
import jax.numpy as jnp
from jax import lax
from jax.experimental import pallas as pl
from jax.experimental.pallas import tpu as pltpu
from jax.sharding import Mesh
from jax.sharding import PartitionSpec as P

HD = 128
BLK = 128
BAND = 2
BPD = 8
MAXK = 12
HPG = 5
GROUP = 4
ATTENTION_COST = 10
VMEM_LIMIT = 56 * 2**20
NEG = -1e30
LOG2E = 1.4426950408889634
SCALE = HD**-0.5
F32 = jnp.float32
BF16 = jnp.bfloat16
NT = (((1,), (1,)), ((), ()))
NN = (((1,), (0,)), ((), ()))
TN = (((0,), (0,)), ((), ()))


def dot(a, b, dims):
    return lax.dot_general(a, b, dims, preferred_element_type=F32)


def fold(x):
    return x.reshape(-1, 8, HD)


def query_block(n_keys, b, ids_ref, count, qd, keys, values, acc, dq, kcat, s_scr, dp_scr, ds_scr):
    q = qd[b, 0]
    do = qd[b, 1]
    base = b * MAXK
    m8 = jnp.full((8, HD), NEG, F32)
    index = [ids_ref[base + s] for s in range(n_keys)]
    for s in range(n_keys):
        k = keys[index[s]]
        kcat[pl.ds(s * BLK, BLK), :] = k
        st = dot(k, q, NT)
        if s > n_keys - GROUP:
            st = jnp.where(s < count, st, NEG)
        s_scr[s] = st
        m8 = jnp.maximum(m8, jnp.max(fold(st), axis=0))
        dp_scr[s] = dot(values[index[s]], do, NT)
    m = jnp.max(m8, axis=0, keepdims=True) * (SCALE * LOG2E)
    l8 = jnp.zeros((8, HD), F32)
    r8 = jnp.zeros((8, HD), F32)
    for s in range(n_keys):
        p = jnp.exp2(s_scr[s] * (SCALE * LOG2E) - m)
        s_scr[s] = p
        l8 += jnp.sum(fold(p), axis=0)
        r8 += jnp.sum(fold(p * dp_scr[s]), axis=0)
    inv = 1.0 / jnp.sum(l8, axis=0, keepdims=True)
    rd = jnp.sum(r8, axis=0, keepdims=True) * inv
    for s in range(n_keys):
        p = s_scr[s] * inv
        ds = (p * (dp_scr[s] - rd)).astype(BF16)
        ds_scr[pl.ds(s * BLK, BLK), :] = ds
        acc[index[s], 0] += dot(ds, q, NN)
        acc[index[s], 1] += dot(p.astype(BF16), do, NN)
    rows = pl.ds(0, n_keys * BLK)
    dq[...] = (dot(ds_scr[rows, :], kcat[rows, :], TN) * SCALE).astype(BF16)


def attention_kernel(size, n_query, fetches, ids_ref, cnt_ref, place_ref, *refs):
    sources, refs = refs[: len(fetches)], refs[len(fetches) :]
    shared = n_query < size
    qd_in, dq_out, targets = refs[0], refs[1], refs[2:5]
    if shared:
        give_out, refs = refs[5], refs[1:]
    keys, values, qd, acc, stage, dq, kcat, s_scr, dp_scr, ds_scr, in_sem, out_sem = refs[5:]
    copies = []
    for source, fetch in zip(sources, fetches):
        for src, t, row in fetch(source, place_ref):
            dst = (keys, values)[t].at[pl.ds(row, src.shape[0])]
            copies.append(pltpu.make_async_copy(src, dst, in_sem.at[len(copies)]))
    q_rows = qd_in.at[pl.ds(pl.multiple_of(place_ref[0], 8), n_query), pl.ds(qd_in.shape[1] - 2, 2)]
    copies.append(pltpu.make_async_copy(q_rows, qd, in_sem.at[len(copies)]))
    for copy in copies:
        copy.start()
    acc[...] = jnp.zeros_like(acc)
    for copy in copies:
        copy.wait()

    def one(b, carry):
        count = cnt_ref[b]
        for upto in range(GROUP, MAXK + 1, GROUP):

            @pl.when((count > upto - GROUP) & (count <= upto))
            def _():
                query_block(
                    upto, b, ids_ref, count, qd, keys, values, acc, dq.at[b], kcat, s_scr, dp_scr, ds_scr
                )

        return carry

    lax.fori_loop(0, n_query, one, 0)
    puts = [pltpu.make_async_copy(dq, dq_out, out_sem.at[3])]
    puts[0].start()
    for i, target in enumerate(targets):

        def convert(j, carry):
            stage[j, 0] = (acc[j, 0] * SCALE).astype(BF16)
            stage[j, 1] = acc[j, 1].astype(BF16)
            return carry

        lax.fori_loop(i * size, (i + 1) * size, convert, 0)
        rows = pl.ds(i * size, size)
        if shared:
            keep = pl.multiple_of(i * size + place_ref[1], 8)
            give = pl.multiple_of(i * size + n_query - place_ref[1], 8)
            rows = pl.ds(keep, n_query)
            puts.append(
                pltpu.make_async_copy(stage.at[pl.ds(give, n_query)], give_out.at[i], out_sem.at[4 + i])
            )
            puts[-1].start()
        puts.append(pltpu.make_async_copy(stage.at[rows], target, out_sem.at[i]))
        puts[-1].start()
    for copy in puts:
        copy.wait()


def attention(ids, counts, place, sources, fetches, qd, n_query, size):
    window = 3 * size
    shared = n_query < size
    kept = jax.ShapeDtypeStruct((n_query, 2, BLK, HD), BF16)
    given = [jax.ShapeDtypeStruct((3, n_query, 2, BLK, HD), BF16)] if shared else []
    smem = pl.BlockSpec(memory_space=pltpu.SMEM)
    hbm = pl.BlockSpec(memory_space=pl.ANY)
    pairs = n_query * 8
    out = pl.pallas_call(
        functools.partial(attention_kernel, size, n_query, fetches),
        out_shape=[jax.ShapeDtypeStruct((n_query, BLK, HD), BF16)] + [kept] * 3 + given,
        in_specs=[smem] * 3 + [hbm] * (len(sources) + 1),
        out_specs=[hbm] * (4 + len(given)),
        scratch_shapes=[
            pltpu.VMEM((window, BLK, HD), BF16),
            pltpu.VMEM((window, BLK, HD), BF16),
            pltpu.VMEM((n_query, 2, BLK, HD), BF16),
            pltpu.VMEM((window, 2, BLK, HD), F32),
            pltpu.VMEM((window, 2, BLK, HD), BF16),
            pltpu.VMEM((n_query, BLK, HD), BF16),
            pltpu.VMEM((MAXK * BLK, HD), BF16),
            pltpu.VMEM((MAXK, BLK, HD), F32),
            pltpu.VMEM((MAXK, BLK, HD), F32),
            pltpu.VMEM((MAXK * BLK, HD), BF16),
            pltpu.SemaphoreType.DMA((13,)),
            pltpu.SemaphoreType.DMA((7,)),
        ],
        compiler_params=pltpu.CompilerParams(vmem_limit_bytes=VMEM_LIMIT),
        cost_estimate=pl.CostEstimate(
            flops=0 if shared else pairs * ATTENTION_COST * BLK * BLK * HD,
            bytes_accessed=0 if shared else (2 * window + n_query) * 2 * BLK * HD * 2,
            transcendentals=0 if shared else pairs * BLK * BLK,
        ),
        name="attention",
    )(ids, counts, place, *sources, qd)
    return out[0], out[1:]


def split_kernel(k_ref, v_ref, q_ref, g_ref, ka_ref, va_ref, qda_ref, b_ref):
    for j in range(ka_ref.shape[1]):

        def head(ref, m):
            return ref[:, (j * HPG + m) * HD : (j * HPG + m + 1) * HD]

        for m in range(4):
            ka_ref[m, j] = head(k_ref, m)
            va_ref[m, j] = head(v_ref, m)
            qda_ref[m, j, 0] = head(q_ref, m)
            qda_ref[m, j, 1] = head(g_ref, m)
        for t, ref in enumerate((k_ref, v_ref, q_ref, g_ref)):
            b_ref[j, t] = head(ref, 4)


def split_heads(key_in, value_in, query_in, out_grad):
    groups, step = key_in.shape[1] // (HPG * HD), 2
    one = pl.BlockSpec((4, step, BLK, HD), lambda j: (0, j, 0, 0))
    two = pl.BlockSpec((4, step, 2, BLK, HD), lambda j: (0, j, 0, 0, 0))
    four = pl.BlockSpec((step, 4, BLK, HD), lambda j: (j, 0, 0, 0))
    shapes = ((4, groups), (4, groups), (4, groups, 2), (groups, 4))
    ka, va, qda, b = pl.pallas_call(
        split_kernel,
        grid=(groups // step,),
        out_shape=tuple(jax.ShapeDtypeStruct((*x, BLK, HD), BF16) for x in shapes),
        in_specs=[pl.BlockSpec((BLK, step * HPG * HD), lambda j: (0, j))] * 4,
        out_specs=(one, one, two, four),
        compiler_params=pltpu.CompilerParams(vmem_limit_bytes=VMEM_LIMIT),
        cost_estimate=pl.CostEstimate(flops=0, bytes_accessed=16 * key_in.size, transcendentals=0),
        name="split_heads",
    )(key_in, value_in, query_in, out_grad)
    flat = 4 * groups
    return ka.reshape(flat, BLK, HD), va.reshape(flat, BLK, HD), qda.reshape(flat, 2, BLK, HD), b


def join_kernel(dqa_ref, dkva_ref, b_ref, *outs):
    for t, ref in enumerate(outs):
        for j in range(b_ref.shape[0]):
            for m in range(HPG):
                if m == 4:
                    value = b_ref[j, t]
                else:
                    value = dqa_ref[m, j] if t == 0 else dkva_ref[m, j, t - 1]
                ref[:, (j * HPG + m) * HD : (j * HPG + m + 1) * HD] = value


def join_heads(dqa, dkva, back_b):
    groups, step = back_b.shape[0], 2
    out = jax.ShapeDtypeStruct((BLK, groups * HPG * HD), BF16)
    return pl.pallas_call(
        join_kernel,
        grid=(groups // step,),
        out_shape=(out,) * 3,
        in_specs=[
            pl.BlockSpec((4, step, BLK, HD), lambda j: (0, j, 0, 0)),
            pl.BlockSpec((4, step, 2, BLK, HD), lambda j: (0, j, 0, 0, 0)),
            pl.BlockSpec((step, 3, BLK, HD), lambda j: (j, 0, 0, 0)),
        ],
        out_specs=(pl.BlockSpec((BLK, step * HPG * HD), lambda j: (0, j)),) * 3,
        compiler_params=pltpu.CompilerParams(vmem_limit_bytes=VMEM_LIMIT),
        cost_estimate=pl.CostEstimate(
            flops=0, bytes_accessed=groups * HPG * 3 * BLK * HD * 4, transcendentals=0
        ),
        name="join_heads",
    )(dqa.reshape(4, groups, BLK, HD), dkva.reshape(4, groups, 2, BLK, HD), back_b)


def total_kernel(dq_ref, own_ref, *refs):
    terms, out_ref = refs[:-1], refs[-1]
    out_ref[:, 0] = dq_ref[...]
    total = own_ref[...].astype(F32)
    for term in terms:
        total += term[...].astype(F32)
    out_ref[:, 1:] = total.astype(BF16)


def total_grads(dq, own, terms):
    blocks, step = dq.shape[0], 4
    kv_spec = pl.BlockSpec((step, 2, BLK, HD), lambda i: (i, 0, 0, 0))
    return pl.pallas_call(
        total_kernel,
        grid=(blocks // step,),
        out_shape=jax.ShapeDtypeStruct((blocks, 3, BLK, HD), BF16),
        in_specs=[pl.BlockSpec((step, BLK, HD), lambda i: (i, 0, 0))] + [kv_spec] * (1 + len(terms)),
        out_specs=pl.BlockSpec((step, 3, BLK, HD), lambda i: (i, 0, 0, 0)),
        cost_estimate=pl.CostEstimate(
            flops=0, bytes_accessed=(6 + 2 * len(terms)) * dq.size * 2, transcendentals=0
        ),
        name="total_grads",
    )(dq, own, *terms)


def both_halves_kernel(x_ref, own0, own1, right0, right1, left0, left1, out_ref):
    x = x_ref[0]
    for s, own in enumerate((own0, own1)):
        right = jnp.where(x == x_ref[1], (right1, right0)[s][...], (right0, right1)[s][...])
        left = jnp.where(x == 0, (left1, left0)[s][...], (left0, left1)[s][...])
        total = own[...].astype(F32) + right.astype(F32) + left.astype(F32)
        out_ref[s] = total.astype(BF16)


def both_halves(x, last, own, from_right, from_left):
    blocks, step = own[0].shape[0], 4
    spec = pl.BlockSpec((step, 2, BLK, HD), lambda i: (i, 0, 0, 0))
    out = pl.pallas_call(
        both_halves_kernel,
        grid=(blocks // step,),
        out_shape=jax.ShapeDtypeStruct((2, blocks, 2, BLK, HD), BF16),
        in_specs=[pl.BlockSpec(memory_space=pltpu.SMEM)] + [spec] * 6,
        out_specs=pl.BlockSpec((2, step, 2, BLK, HD), lambda i: (0, i, 0, 0, 0)),
        cost_estimate=pl.CostEstimate(flops=0, bytes_accessed=16 * own[0].size, transcendentals=0),
        name="both_halves",
    )(jnp.stack([x, jnp.int32(last)]), *own, *from_right, *from_left)
    return out.reshape(2 * blocks, 2, BLK, HD)


WIDE = ("half", "core", "group")
PAIR = ("core", "group")
CHIPS = ("half", "x")


def shift(value, axes, steps):
    count = lax.axis_size(axes)
    return lax.ppermute(value, axes, [(s, (s + steps) % count) for s in range(count)])


def add(a, b):
    return (a.astype(F32) + b.astype(F32)).astype(BF16)


def exchange(x, axes):
    return lax.all_to_all(x, axes, 0, 0, tiled=True)


def after(x, *done):
    return lax.optimization_barrier((x, *done))[0]


def swap(value):
    return lax.ppermute(value, "core", [(0, 1), (1, 0)])


def shards(query_in, key_in, value_in, out_grad, key_blocks, block_count):
    half, x, core = (lax.axis_index(name) for name in ("half", "x", "core"))
    last, size = lax.axis_size("x") - 1, 2 * BPD
    packed = jnp.concatenate([key_blocks, block_count[:, :, None]], axis=2)
    lists = lax.all_gather(packed, ("half", "core"))
    list_b = lists[2 * half + core, 4]
    lists = lax.dynamic_index_in_dim(lists, 2 * half + core, 1, False)
    ka, va, qda, b = split_heads(key_in, value_in, query_in, out_grad)

    def plain(lists, chip):
        lists = lists.reshape(-1, MAXK + 1)
        first_block = (chip - 1) * 2 * BPD
        return (lists[:, :MAXK] - first_block).reshape(-1), lists[:, MAXK]

    own_b = exchange(b, "group")
    pairs_b = own_b[:, :2]
    mine = (shift(pairs_b, CHIPS, 1), pairs_b, shift(pairs_b, CHIPS, -1))
    theirs = tuple(swap(pairs) for pairs in mine)

    keys = exchange(after(ka, own_b), WIDE)
    key_near = [shift(keys, "x", 1), shift(keys, "x", -1)]
    values = exchange(after(va, keys, *mine), WIDE)
    value_near = [shift(values, "x", 1), shift(values, "x", -1)]

    def run(i, other):
        def fetch(ref, place):
            at = i * size + (BPD - place[1] if other else place[1])
            return [(ref.at[:, t], t, pl.multiple_of(at, 8)) for t in range(2)]

        return fetch

    ids, counts = plain(list_b, half * (last + 1) + x)
    place = jnp.stack([jnp.int32(0), core * BPD])
    fetches = [run(i, other) for other in range(2) for i in range(3)]
    dq_b, (left_b, mine_b, right_b, give_b) = attention(
        ids, counts, place, mine + theirs, fetches, after(own_b, values, *key_near), BPD, size
    )
    got_b = [swap(give_b[i]) for i in range(3)]
    out_b = lax.optimization_barrier((add(left_b, got_b[0]), add(right_b, got_b[2]), *value_near))
    terms_b = [got_b[1], shift(out_b[0], CHIPS, -1), shift(out_b[1], CHIPS, 1)]

    queries = exchange(after(qda, values), WIDE)

    def third(t, i):
        return lambda ref, place: [(ref.at[pl.ds(pl.multiple_of(place[1 + i], 8), size)], t, i * size)]

    fetches = [third(t, i) for t in range(2) for i in range(3)]
    sources = (key_near[0], keys, key_near[1], value_near[0], values, value_near[1])
    done, back_b = [], ()
    for s in range(2):
        ids, counts = plain(lists[2 * s : 2 * s + 2], s * (last + 1) + x)
        left = jnp.where(x == 0, 1 - s, s) * size
        right = jnp.where(x == last, 1 - s, s) * size
        place = after(jnp.stack([jnp.int32(s * size), left, jnp.int32(s * size), right]), *back_b)
        dq, grads = attention(ids, counts, place, sources, fetches, queries, size, size)
        done.append((dq, grads, shift(grads[0], "x", -1), shift(grads[2], "x", 1)))
        if s == 0:
            total_b = total_grads(after(dq_b, dq), mine_b, terms_b)
            back_b = (total_b,)
    back_b = exchange(total_b, "group")
    dqa = exchange(after(jnp.concatenate([d[0] for d in done]), *done[0][2:], back_b), WIDE)
    dkva = both_halves(x, last, [d[1][1] for d in done], [d[2] for d in done], [d[3] for d in done])
    dkva = exchange(after(dkva, dqa), WIDE)
    return tuple(join_heads(dqa, dkva, back_b))


def solution(mesh):
    chips = mesh.shape["frame"] // 4
    mesh = Mesh(mesh.devices.reshape(2, chips, 2, -1), ("half", "x", "core", "group"))
    runs = ("half", "x", "core")
    tokens = P((*runs, "group"), None)
    return jax.shard_map(
        shards,
        mesh=mesh,
        in_specs=(tokens,) * 4 + (P("group", runs, None), P("group", runs)),
        out_specs=(tokens,) * 3,
        check_vma=False,
    )
```

```python
import functools

import jax
import jax.numpy as jnp
from jax import lax
from jax.experimental import pallas as pl
from jax.experimental.pallas import tpu as pltpu
from jax.sharding import Mesh
from jax.sharding import PartitionSpec as P

HD = 128
BLK = 128
BAND = 2
BPD = 8
MAXK = 12
HPG = 5
GROUP = 4
ATTENTION_COST = 10
VMEM_LIMIT = 56 * 2**20
NEG = -1e30
LOG2E = 1.4426950408889634
SCALE = HD**-0.5
F32 = jnp.float32
BF16 = jnp.bfloat16
NT = (((1,), (1,)), ((), ()))
NN = (((1,), (0,)), ((), ()))
TN = (((0,), (0,)), ((), ()))


def dot(a, b, dims):
    return lax.dot_general(a, b, dims, preferred_element_type=F32)


def fold(x):
    return x.reshape(-1, 8, HD)


def query_block(n_keys, b, ids_ref, count, qd, keys, values, acc, dq, kcat, s_scr, dp_scr, ds_scr):
    q = qd[b, 0]
    do = qd[b, 1]
    base = b * MAXK
    m8 = jnp.full((8, HD), NEG, F32)
    index = [ids_ref[base + s] for s in range(n_keys)]
    for s in range(n_keys):
        k = keys[index[s]]
        kcat[pl.ds(s * BLK, BLK), :] = k
        st = dot(k, q, NT)
        if s > n_keys - GROUP:
            st = jnp.where(s < count, st, NEG)
        s_scr[s] = st
        m8 = jnp.maximum(m8, jnp.max(fold(st), axis=0))
        dp_scr[s] = dot(values[index[s]], do, NT)
    m = jnp.max(m8, axis=0, keepdims=True) * (SCALE * LOG2E)
    l8 = jnp.zeros((8, HD), F32)
    r8 = jnp.zeros((8, HD), F32)
    for s in range(n_keys):
        p = jnp.exp2(s_scr[s] * (SCALE * LOG2E) - m)
        s_scr[s] = p
        l8 += jnp.sum(fold(p), axis=0)
        r8 += jnp.sum(fold(p * dp_scr[s]), axis=0)
    inv = 1.0 / jnp.sum(l8, axis=0, keepdims=True)
    rd = jnp.sum(r8, axis=0, keepdims=True) * inv
    for s in range(n_keys):
        p = s_scr[s] * inv
        ds = (p * (dp_scr[s] - rd)).astype(BF16)
        ds_scr[pl.ds(s * BLK, BLK), :] = ds
        acc[index[s], 0] += dot(ds, q, NN)
        acc[index[s], 1] += dot(p.astype(BF16), do, NN)
    rows = pl.ds(0, n_keys * BLK)
    dq[...] = (dot(ds_scr[rows, :], kcat[rows, :], TN) * SCALE).astype(BF16)


def attention_kernel(size, n_query, fetches, ids_ref, cnt_ref, place_ref, *refs):
    sources, refs = refs[: len(fetches)], refs[len(fetches) :]
    shared = n_query < size
    qd_in, dq_out, targets = refs[0], refs[1], refs[2:5]
    if shared:
        give_out, refs = refs[5], refs[1:]
    keys, values, qd, acc, stage, dq, kcat, s_scr, dp_scr, ds_scr, in_sem, out_sem = refs[5:]
    copies = []
    for source, fetch in zip(sources, fetches):
        for src, t, row in fetch(source, place_ref):
            dst = (keys, values)[t].at[pl.ds(row, src.shape[0])]
            copies.append(pltpu.make_async_copy(src, dst, in_sem.at[len(copies)]))
    q_rows = qd_in.at[pl.ds(pl.multiple_of(place_ref[0], 8), n_query), pl.ds(qd_in.shape[1] - 2, 2)]
    copies.append(pltpu.make_async_copy(q_rows, qd, in_sem.at[len(copies)]))
    for copy in copies:
        copy.start()
    acc[...] = jnp.zeros_like(acc)
    for copy in copies:
        copy.wait()

    def one(b, carry):
        count = cnt_ref[b]
        for upto in range(GROUP, MAXK + 1, GROUP):

            @pl.when((count > upto - GROUP) & (count <= upto))
            def _():
                query_block(
                    upto, b, ids_ref, count, qd, keys, values, acc, dq.at[b], kcat, s_scr, dp_scr, ds_scr
                )

        return carry

    lax.fori_loop(0, n_query, one, 0)
    puts = [pltpu.make_async_copy(dq, dq_out, out_sem.at[3])]
    puts[0].start()
    for i, target in enumerate(targets):

        def convert(j, carry):
            stage[j, 0] = (acc[j, 0] * SCALE).astype(BF16)
            stage[j, 1] = acc[j, 1].astype(BF16)
            return carry

        lax.fori_loop(i * size, (i + 1) * size, convert, 0)
        rows = pl.ds(i * size, size)
        if shared:
            keep = pl.multiple_of(i * size + place_ref[1], 8)
            give = pl.multiple_of(i * size + n_query - place_ref[1], 8)
            rows = pl.ds(keep, n_query)
            puts.append(
                pltpu.make_async_copy(stage.at[pl.ds(give, n_query)], give_out.at[i], out_sem.at[4 + i])
            )
            puts[-1].start()
        puts.append(pltpu.make_async_copy(stage.at[rows], target, out_sem.at[i]))
        puts[-1].start()
    for copy in puts:
        copy.wait()


def attention(ids, counts, place, sources, fetches, qd, n_query, size):
    window = 3 * size
    shared = n_query < size
    kept = jax.ShapeDtypeStruct((n_query, 2, BLK, HD), BF16)
    given = [jax.ShapeDtypeStruct((3, n_query, 2, BLK, HD), BF16)] if shared else []
    smem = pl.BlockSpec(memory_space=pltpu.SMEM)
    hbm = pl.BlockSpec(memory_space=pl.ANY)
    pairs = n_query * 8
    out = pl.pallas_call(
        functools.partial(attention_kernel, size, n_query, fetches),
        out_shape=[jax.ShapeDtypeStruct((n_query, BLK, HD), BF16)] + [kept] * 3 + given,
        in_specs=[smem] * 3 + [hbm] * (len(sources) + 1),
        out_specs=[hbm] * (4 + len(given)),
        scratch_shapes=[
            pltpu.VMEM((window, BLK, HD), BF16),
            pltpu.VMEM((window, BLK, HD), BF16),
            pltpu.VMEM((n_query, 2, BLK, HD), BF16),
            pltpu.VMEM((window, 2, BLK, HD), F32),
            pltpu.VMEM((window, 2, BLK, HD), BF16),
            pltpu.VMEM((n_query, BLK, HD), BF16),
            pltpu.VMEM((MAXK * BLK, HD), BF16),
            pltpu.VMEM((MAXK, BLK, HD), F32),
            pltpu.VMEM((MAXK, BLK, HD), F32),
            pltpu.VMEM((MAXK * BLK, HD), BF16),
            pltpu.SemaphoreType.DMA((13,)),
            pltpu.SemaphoreType.DMA((7,)),
        ],
        compiler_params=pltpu.CompilerParams(vmem_limit_bytes=VMEM_LIMIT),
        cost_estimate=pl.CostEstimate(
            flops=0 if shared else pairs * ATTENTION_COST * BLK * BLK * HD,
            bytes_accessed=0 if shared else (2 * window + n_query) * 2 * BLK * HD * 2,
            transcendentals=0 if shared else pairs * BLK * BLK,
        ),
        name="attention",
    )(ids, counts, place, *sources, qd)
    return out[0], out[1:]


def split_kernel(k_ref, v_ref, q_ref, g_ref, ka_ref, va_ref, qda_ref, b_ref):
    for j in range(ka_ref.shape[1]):

        def head(ref, m):
            return ref[:, (j * HPG + m) * HD : (j * HPG + m + 1) * HD]

        for m in range(4):
            ka_ref[m, j] = head(k_ref, m)
            va_ref[m, j] = head(v_ref, m)
            qda_ref[m, j, 0] = head(q_ref, m)
            qda_ref[m, j, 1] = head(g_ref, m)
        for t, ref in enumerate((k_ref, v_ref, q_ref, g_ref)):
            b_ref[j, t] = head(ref, 4)


def split_heads(key_in, value_in, query_in, out_grad):
    groups, step = key_in.shape[1] // (HPG * HD), 2
    one = pl.BlockSpec((4, step, BLK, HD), lambda j: (0, j, 0, 0))
    two = pl.BlockSpec((4, step, 2, BLK, HD), lambda j: (0, j, 0, 0, 0))
    four = pl.BlockSpec((step, 4, BLK, HD), lambda j: (j, 0, 0, 0))
    shapes = ((4, groups), (4, groups), (4, groups, 2), (groups, 4))
    ka, va, qda, b = pl.pallas_call(
        split_kernel,
        grid=(groups // step,),
        out_shape=tuple(jax.ShapeDtypeStruct((*x, BLK, HD), BF16) for x in shapes),
        in_specs=[pl.BlockSpec((BLK, step * HPG * HD), lambda j: (0, j))] * 4,
        out_specs=(one, one, two, four),
        compiler_params=pltpu.CompilerParams(vmem_limit_bytes=VMEM_LIMIT),
        cost_estimate=pl.CostEstimate(flops=0, bytes_accessed=16 * key_in.size, transcendentals=0),
        name="split_heads",
    )(key_in, value_in, query_in, out_grad)
    flat = 4 * groups
    return ka.reshape(flat, BLK, HD), va.reshape(flat, BLK, HD), qda.reshape(flat, 2, BLK, HD), b


def join_kernel(dqa_ref, dkva_ref, b_ref, *outs):
    for t, ref in enumerate(outs):
        for j in range(b_ref.shape[0]):
            for m in range(HPG):
                if m == 4:
                    value = b_ref[j, t]
                else:
                    value = dqa_ref[m, j] if t == 0 else dkva_ref[m, j, t - 1]
                ref[:, (j * HPG + m) * HD : (j * HPG + m + 1) * HD] = value


def join_heads(dqa, dkva, back_b):
    groups, step = back_b.shape[0], 2
    out = jax.ShapeDtypeStruct((BLK, groups * HPG * HD), BF16)
    return pl.pallas_call(
        join_kernel,
        grid=(groups // step,),
        out_shape=(out,) * 3,
        in_specs=[
            pl.BlockSpec((4, step, BLK, HD), lambda j: (0, j, 0, 0)),
            pl.BlockSpec((4, step, 2, BLK, HD), lambda j: (0, j, 0, 0, 0)),
            pl.BlockSpec((step, 3, BLK, HD), lambda j: (j, 0, 0, 0)),
        ],
        out_specs=(pl.BlockSpec((BLK, step * HPG * HD), lambda j: (0, j)),) * 3,
        compiler_params=pltpu.CompilerParams(vmem_limit_bytes=VMEM_LIMIT),
        cost_estimate=pl.CostEstimate(
            flops=0, bytes_accessed=groups * HPG * 3 * BLK * HD * 4, transcendentals=0
        ),
        name="join_heads",
    )(dqa.reshape(4, groups, BLK, HD), dkva.reshape(4, groups, 2, BLK, HD), back_b)


def total_kernel(dq_ref, own_ref, *refs):
    terms, out_ref = refs[:-1], refs[-1]
    out_ref[:, 0] = dq_ref[...]
    total = own_ref[...].astype(F32)
    for term in terms:
        total += term[...].astype(F32)
    out_ref[:, 1:] = total.astype(BF16)


def total_grads(dq, own, terms):
    blocks, step = dq.shape[0], 4
    kv_spec = pl.BlockSpec((step, 2, BLK, HD), lambda i: (i, 0, 0, 0))
    return pl.pallas_call(
        total_kernel,
        grid=(blocks // step,),
        out_shape=jax.ShapeDtypeStruct((blocks, 3, BLK, HD), BF16),
        in_specs=[pl.BlockSpec((step, BLK, HD), lambda i: (i, 0, 0))] + [kv_spec] * (1 + len(terms)),
        out_specs=pl.BlockSpec((step, 3, BLK, HD), lambda i: (i, 0, 0, 0)),
        cost_estimate=pl.CostEstimate(
            flops=0, bytes_accessed=(6 + 2 * len(terms)) * dq.size * 2, transcendentals=0
        ),
        name="total_grads",
    )(dq, own, *terms)


def both_halves_kernel(x_ref, own0, own1, right0, right1, left0, left1, out_ref):
    x = x_ref[0]
    for s, own in enumerate((own0, own1)):
        right = jnp.where(x == x_ref[1], (right1, right0)[s][...], (right0, right1)[s][...])
        left = jnp.where(x == 0, (left1, left0)[s][...], (left0, left1)[s][...])
        total = own[...].astype(F32) + right.astype(F32) + left.astype(F32)
        out_ref[s] = total.astype(BF16)


def both_halves(x, last, own, from_right, from_left):
    blocks, step = own[0].shape[0], 4
    spec = pl.BlockSpec((step, 2, BLK, HD), lambda i: (i, 0, 0, 0))
    out = pl.pallas_call(
        both_halves_kernel,
        grid=(blocks // step,),
        out_shape=jax.ShapeDtypeStruct((2, blocks, 2, BLK, HD), BF16),
        in_specs=[pl.BlockSpec(memory_space=pltpu.SMEM)] + [spec] * 6,
        out_specs=pl.BlockSpec((2, step, 2, BLK, HD), lambda i: (0, i, 0, 0, 0)),
        cost_estimate=pl.CostEstimate(flops=0, bytes_accessed=16 * own[0].size, transcendentals=0),
        name="both_halves",
    )(jnp.stack([x, jnp.int32(last)]), *own, *from_right, *from_left)
    return out.reshape(2 * blocks, 2, BLK, HD)


WIDE = ("half", "core", "group")
PAIR = ("core", "group")
CHIPS = ("half", "x")


def shift(value, axes, steps):
    count = lax.axis_size(axes)
    return lax.ppermute(value, axes, [(s, (s + steps) % count) for s in range(count)])


def add(a, b):
    return (a.astype(F32) + b.astype(F32)).astype(BF16)


def exchange(x, axes):
    return lax.all_to_all(x, axes, 0, 0, tiled=True)


def after(x, *done):
    return lax.optimization_barrier((x, *done))[0]


def swap(value):
    return lax.ppermute(value, "core", [(0, 1), (1, 0)])


def shards(query_in, key_in, value_in, out_grad, key_blocks, block_count):
    half, x, core = (lax.axis_index(name) for name in ("half", "x", "core"))
    last, size = lax.axis_size("x") - 1, 2 * BPD
    packed = jnp.concatenate([key_blocks, block_count[:, :, None]], axis=2)
    gathered = lax.all_gather(packed, ("half", "core"))
    list_b = gathered[2 * half + core, 4]
    lists = lax.dynamic_index_in_dim(gathered, 2 * half + core, 1, False)
    ka, va, qda, b = split_heads(key_in, value_in, query_in, out_grad)

    def plain(lists, chip):
        lists = lists.reshape(-1, MAXK + 1)
        first_block = (chip - 1) * 2 * BPD
        return (lists[:, :MAXK] - first_block).reshape(-1), lists[:, MAXK]

    own_b = exchange(after(b, gathered), "group")
    pairs_b = own_b[:, :2]
    mine = (shift(pairs_b, CHIPS, 1), pairs_b, shift(pairs_b, CHIPS, -1))
    theirs = tuple(swap(pairs) for pairs in mine)

    keys = exchange(after(ka, own_b), WIDE)
    key_near = [shift(keys, "x", 1), shift(keys, "x", -1)]
    values = exchange(after(va, keys, *mine), WIDE)
    value_near = [shift(values, "x", 1), shift(values, "x", -1)]

    def run(i, other):
        def fetch(ref, place):
            at = i * size + (BPD - place[1] if other else place[1])
            return [(ref.at[:, t], t, pl.multiple_of(at, 8)) for t in range(2)]

        return fetch

    ids, counts = plain(list_b, half * (last + 1) + x)
    place = jnp.stack([jnp.int32(0), core * BPD])
    fetches = [run(i, other) for other in range(2) for i in range(3)]
    dq_b, (left_b, mine_b, right_b, give_b) = attention(
        ids, counts, place, mine + theirs, fetches, after(own_b, values, *key_near), BPD, size
    )
    give_b = after(give_b, *value_near)
    got_b = [swap(give_b[i]) for i in range(3)]
    out_b = lax.optimization_barrier((add(left_b, got_b[0]), add(right_b, got_b[2])))
    terms_b = [got_b[1], shift(out_b[0], CHIPS, -1), shift(out_b[1], CHIPS, 1)]

    queries = exchange(after(qda, values), WIDE)

    def third(t, i):
        return lambda ref, place: [(ref.at[pl.ds(pl.multiple_of(place[1 + i], 8), size)], t, i * size)]

    fetches = [third(t, i) for t in range(2) for i in range(3)]
    sources = (key_near[0], keys, key_near[1], value_near[0], values, value_near[1])
    done, back_b = [], ()
    for s in range(2):
        ids, counts = plain(lists[2 * s : 2 * s + 2], s * (last + 1) + x)
        left = jnp.where(x == 0, 1 - s, s) * size
        right = jnp.where(x == last, 1 - s, s) * size
        place = after(jnp.stack([jnp.int32(s * size), left, jnp.int32(s * size), right]), *back_b)
        dq, grads = attention(ids, counts, place, sources, fetches, queries, size, size)
        done.append((dq, grads, shift(grads[0], "x", -1), shift(grads[2], "x", 1)))
        if s == 0:
            total_b = total_grads(after(dq_b, dq), mine_b, terms_b)
            back_b = (total_b,)
    back_b = exchange(total_b, "group")
    dqa = exchange(after(jnp.concatenate([d[0] for d in done]), *done[0][2:], back_b), WIDE)
    dkva = both_halves(x, last, [d[1][1] for d in done], [d[2] for d in done], [d[3] for d in done])
    dkva = exchange(after(dkva, dqa), WIDE)
    return tuple(join_heads(dqa, dkva, back_b))


def solution(mesh):
    chips = mesh.shape["frame"] // 4
    mesh = Mesh(mesh.devices.reshape(2, chips, 2, -1), ("half", "x", "core", "group"))
    runs = ("half", "x", "core")
    tokens = P((*runs, "group"), None)
    return jax.shard_map(
        shards,
        mesh=mesh,
        in_specs=(tokens,) * 4 + (P("group", runs, None), P("group", runs)),
        out_specs=(tokens,) * 3,
        check_vma=False,
    )
```

```python
import functools

import jax
import jax.numpy as jnp
from jax import lax
from jax.experimental import pallas as pl
from jax.experimental.pallas import tpu as pltpu
from jax.sharding import Mesh
from jax.sharding import PartitionSpec as P

HD = 128
BLK = 128
BAND = 2
BPD = 8
MAXK = 12
HPG = 5
WAYS = 2
BUCKETS = (4, 6, 8, 10, 12)
STEP = 2
ATTENTION_COST = 10
VMEM_LIMIT = 56 * 2**20
NEG = -1e30
LOG2E = 1.4426950408889634
SCALE = HD**-0.5
F32 = jnp.float32
BF16 = jnp.bfloat16
NT = (((1,), (1,)), ((), ()))
NN = (((1,), (0,)), ((), ()))
TN = (((0,), (0,)), ((), ()))


def dot(a, b, dims):
    return lax.dot_general(a, b, dims, preferred_element_type=F32)


def fold(x):
    return x.reshape(-1, 8, HD)


def query_blocks(n_keys, blocks, ids_ref, counts, qd, kv, acc, dq, kv_cat, sd_scr, x_cat):
    ways = range(len(blocks))
    index = [[ids_ref[b * MAXK + s] for s in range(n_keys)] for b in blocks]
    rows = [pl.ds(s * BLK, BLK) for s in range(n_keys)]
    for i in ways:
        for s in range(n_keys):
            kv_cat[i, rows[s], :] = kv[index[i][s]]
    w_t = [qd[b] for b in blocks]
    for s in range(0, n_keys, STEP):
        part = pl.ds(s * BLK, min(STEP, n_keys - s) * BLK)
        for i in ways:
            sd_scr[i, part, :] = dot(kv_cat[i, part, :], w_t[i], NT)
    top = []
    for i in ways:
        m8 = jnp.full((8, HD), NEG, F32)
        for s in range(n_keys):
            st = sd_scr[i, rows[s], :HD]
            if s > 0:
                st = jnp.where(s < counts[i], st, NEG)
                sd_scr[i, rows[s], :HD] = st
            m8 = jnp.maximum(m8, jnp.max(fold(st), axis=0))
        top.append(jnp.max(m8, axis=0, keepdims=True) * (SCALE * LOG2E))
    inv, rd = [], []
    for i in ways:
        l8 = jnp.zeros((8, HD), F32)
        r8 = jnp.zeros((8, HD), F32)
        for s in range(n_keys):
            p = jnp.exp2(sd_scr[i, rows[s], :HD] * (SCALE * LOG2E) - top[i])
            sd_scr[i, rows[s], :HD] = p
            l8 += jnp.sum(fold(p), axis=0)
            r8 += jnp.sum(fold(p * sd_scr[i, rows[s], HD:]), axis=0)
        inv.append(1.0 / jnp.sum(l8, axis=0, keepdims=True))
        rd.append(jnp.sum(r8, axis=0, keepdims=True) * inv[i])
    for i in ways:
        for s in range(n_keys):
            p = sd_scr[i, rows[s], :HD] * inv[i]
            x_cat[i, rows[s], :HD] = (p * (sd_scr[i, rows[s], HD:] - rd[i])).astype(BF16)
            x_cat[i, rows[s], HD:] = p.astype(BF16)
        for s in range(0, n_keys, STEP):
            n = min(STEP, n_keys - s)
            terms = dot(x_cat[i, pl.ds(s * BLK, n * BLK), :], qd[blocks[i]], NN)
            for j in range(n):
                acc[index[i][s + j]] += terms[j * BLK : (j + 1) * BLK]
        every = pl.ds(0, n_keys * BLK)
        dq[blocks[i]] = (dot(x_cat[i, every, :HD], kv_cat[i, every, :HD], TN) * SCALE).astype(BF16)


def attention_kernel(size, n_query, fetches, ids_ref, cnt_ref, place_ref, *refs):
    sources, refs = refs[: len(fetches)], refs[len(fetches) :]
    shared = n_query < size
    qd_in, dq_out, targets = refs[0], refs[1], refs[2:5]
    if shared:
        give_out, refs = refs[5], refs[1:]
    kv, qd, acc, stage, dq, kv_cat, sd_scr, x_cat, order, in_sem, out_sem = refs[5:]
    copies = []
    for source, fetch in zip(sources, fetches):
        for src, t, row in fetch(source, place_ref):
            dst = kv.at[pl.ds(row, src.shape[0]), :, pl.ds(t * HD, HD)]
            copies.append(pltpu.make_async_copy(src, dst, in_sem.at[len(copies)]))
    q_rows = pl.ds(pl.multiple_of(place_ref[0], 8), n_query)
    for t in range(2):
        src = qd_in.at[q_rows, qd_in.shape[1] - 2 + t]
        dst = qd.at[:, pl.ds(t * HD, HD), pl.ds(t * HD, HD)]
        copies.append(pltpu.make_async_copy(src, dst, in_sem.at[len(copies)]))
    for copy in copies:
        copy.start()
    acc[...] = jnp.zeros_like(acc)
    for t in range(2):
        qd[:, t * HD : (t + 1) * HD, (1 - t) * HD : (2 - t) * HD] = jnp.zeros((n_query, HD, HD), BF16)
    def rank(k, at):
        def place(b, at):
            hit = cnt_ref[b] == MAXK - k

            @pl.when(hit)
            def _():
                order[at] = b

            return at + hit.astype(jnp.int32)

        return lax.fori_loop(0, n_query, place, at)

    lax.fori_loop(0, MAXK, rank, 0)
    for copy in copies:
        copy.wait()

    def some(k, carry):
        blocks = [order[k * WAYS + i] for i in range(WAYS)]
        counts = [cnt_ref[b] for b in blocks]
        for least, upto in zip((0, *BUCKETS), BUCKETS):

            @pl.when((counts[0] > least) & (counts[0] <= upto))
            def _():
                query_blocks(upto, blocks, ids_ref, counts, qd, kv, acc, dq, kv_cat, sd_scr, x_cat)

        return carry

    lax.fori_loop(0, n_query // WAYS, some, 0)
    puts = [pltpu.make_async_copy(dq, dq_out, out_sem.at[3])]
    puts[0].start()
    for i, target in enumerate(targets):

        def convert(j, carry):
            stage[j, 0] = (acc[j, :, :HD] * SCALE).astype(BF16)
            stage[j, 1] = acc[j, :, HD:].astype(BF16)
            return carry

        lax.fori_loop(i * size, (i + 1) * size, convert, 0)
        rows = pl.ds(i * size, size)
        if shared:
            keep = pl.multiple_of(i * size + place_ref[1], 8)
            give = pl.multiple_of(i * size + n_query - place_ref[1], 8)
            rows = pl.ds(keep, n_query)
            puts.append(
                pltpu.make_async_copy(stage.at[pl.ds(give, n_query)], give_out.at[i], out_sem.at[4 + i])
            )
            puts[-1].start()
        puts.append(pltpu.make_async_copy(stage.at[rows], target, out_sem.at[i]))
        puts[-1].start()
    for copy in puts:
        copy.wait()


def attention(ids, counts, place, sources, fetches, qd, n_query, size):
    window = 3 * size
    shared = n_query < size
    kept = jax.ShapeDtypeStruct((n_query, 2, BLK, HD), BF16)
    given = [jax.ShapeDtypeStruct((3, n_query, 2, BLK, HD), BF16)] if shared else []
    smem = pl.BlockSpec(memory_space=pltpu.SMEM)
    hbm = pl.BlockSpec(memory_space=pl.ANY)
    pairs = n_query * 8
    out = pl.pallas_call(
        functools.partial(attention_kernel, size, n_query, fetches),
        out_shape=[jax.ShapeDtypeStruct((n_query, BLK, HD), BF16)] + [kept] * 3 + given,
        in_specs=[smem] * 3 + [hbm] * (len(sources) + 1),
        out_specs=[hbm] * (4 + len(given)),
        scratch_shapes=[
            pltpu.VMEM((window, BLK, 2 * HD), BF16),
            pltpu.VMEM((n_query, 2 * HD, 2 * HD), BF16),
            pltpu.VMEM((window, BLK, 2 * HD), F32),
            pltpu.VMEM((window, 2, BLK, HD), BF16),
            pltpu.VMEM((n_query, BLK, HD), BF16),
            pltpu.VMEM((WAYS, MAXK * BLK, 2 * HD), BF16),
            pltpu.VMEM((WAYS, MAXK * BLK, 2 * HD), F32),
            pltpu.VMEM((WAYS, MAXK * BLK, 2 * HD), BF16),
            pltpu.SMEM((n_query,), jnp.int32),
            pltpu.SemaphoreType.DMA((14,)),
            pltpu.SemaphoreType.DMA((7,)),
        ],
        compiler_params=pltpu.CompilerParams(vmem_limit_bytes=VMEM_LIMIT),
        cost_estimate=pl.CostEstimate(
            flops=0 if shared else pairs * ATTENTION_COST * BLK * BLK * HD,
            bytes_accessed=0 if shared else (2 * window + n_query) * 2 * BLK * HD * 2,
            transcendentals=0 if shared else pairs * BLK * BLK,
        ),
        name="attention",
    )(ids, counts, place, *sources, qd)
    return out[0], out[1:]


def split_kernel(k_ref, v_ref, q_ref, g_ref, ka_ref, va_ref, qda_ref, b_ref):
    for j in range(ka_ref.shape[1]):

        def head(ref, m):
            return ref[:, (j * HPG + m) * HD : (j * HPG + m + 1) * HD]

        for m in range(4):
            ka_ref[m, j] = head(k_ref, m)
            va_ref[m, j] = head(v_ref, m)
            qda_ref[m, j, 0] = head(q_ref, m)
            qda_ref[m, j, 1] = head(g_ref, m)
        for t, ref in enumerate((k_ref, v_ref, q_ref, g_ref)):
            b_ref[j, t] = head(ref, 4)


def split_heads(key_in, value_in, query_in, out_grad):
    groups, step = key_in.shape[1] // (HPG * HD), 2
    one = pl.BlockSpec((4, step, BLK, HD), lambda j: (0, j, 0, 0))
    two = pl.BlockSpec((4, step, 2, BLK, HD), lambda j: (0, j, 0, 0, 0))
    four = pl.BlockSpec((step, 4, BLK, HD), lambda j: (j, 0, 0, 0))
    shapes = ((4, groups), (4, groups), (4, groups, 2), (groups, 4))
    ka, va, qda, b = pl.pallas_call(
        split_kernel,
        grid=(groups // step,),
        out_shape=tuple(jax.ShapeDtypeStruct((*x, BLK, HD), BF16) for x in shapes),
        in_specs=[pl.BlockSpec((BLK, step * HPG * HD), lambda j: (0, j))] * 4,
        out_specs=(one, one, two, four),
        compiler_params=pltpu.CompilerParams(vmem_limit_bytes=VMEM_LIMIT),
        cost_estimate=pl.CostEstimate(flops=0, bytes_accessed=16 * key_in.size, transcendentals=0),
        name="split_heads",
    )(key_in, value_in, query_in, out_grad)
    flat = 4 * groups
    return ka.reshape(flat, BLK, HD), va.reshape(flat, BLK, HD), qda.reshape(flat, 2, BLK, HD), b


def join_kernel(dqa_ref, dkva_ref, b_ref, *outs):
    for t, ref in enumerate(outs):
        for j in range(b_ref.shape[0]):
            for m in range(HPG):
                if m == 4:
                    value = b_ref[j, t]
                else:
                    value = dqa_ref[m, j] if t == 0 else dkva_ref[m, j, t - 1]
                ref[:, (j * HPG + m) * HD : (j * HPG + m + 1) * HD] = value


def join_heads(dqa, dkva, back_b):
    groups, step = back_b.shape[0], 2
    out = jax.ShapeDtypeStruct((BLK, groups * HPG * HD), BF16)
    return pl.pallas_call(
        join_kernel,
        grid=(groups // step,),
        out_shape=(out,) * 3,
        in_specs=[
            pl.BlockSpec((4, step, BLK, HD), lambda j: (0, j, 0, 0)),
            pl.BlockSpec((4, step, 2, BLK, HD), lambda j: (0, j, 0, 0, 0)),
            pl.BlockSpec((step, 3, BLK, HD), lambda j: (j, 0, 0, 0)),
        ],
        out_specs=(pl.BlockSpec((BLK, step * HPG * HD), lambda j: (0, j)),) * 3,
        compiler_params=pltpu.CompilerParams(vmem_limit_bytes=VMEM_LIMIT),
        cost_estimate=pl.CostEstimate(
            flops=0, bytes_accessed=groups * HPG * 3 * BLK * HD * 4, transcendentals=0
        ),
        name="join_heads",
    )(dqa.reshape(4, groups, BLK, HD), dkva.reshape(4, groups, 2, BLK, HD), back_b)


def total_kernel(dq_ref, own_ref, *refs):
    terms, out_ref = refs[:-1], refs[-1]
    out_ref[:, 0] = dq_ref[...]
    total = own_ref[...].astype(F32)
    for term in terms:
        total += term[...].astype(F32)
    out_ref[:, 1:] = total.astype(BF16)


def total_grads(dq, own, terms):
    blocks, step = dq.shape[0], 4
    kv_spec = pl.BlockSpec((step, 2, BLK, HD), lambda i: (i, 0, 0, 0))
    return pl.pallas_call(
        total_kernel,
        grid=(blocks // step,),
        out_shape=jax.ShapeDtypeStruct((blocks, 3, BLK, HD), BF16),
        in_specs=[pl.BlockSpec((step, BLK, HD), lambda i: (i, 0, 0))] + [kv_spec] * (1 + len(terms)),
        out_specs=pl.BlockSpec((step, 3, BLK, HD), lambda i: (i, 0, 0, 0)),
        cost_estimate=pl.CostEstimate(
            flops=0, bytes_accessed=(6 + 2 * len(terms)) * dq.size * 2, transcendentals=0
        ),
        name="total_grads",
    )(dq, own, *terms)


def both_halves_kernel(x_ref, own0, own1, right0, right1, left0, left1, out_ref):
    x = x_ref[0]
    for s, own in enumerate((own0, own1)):
        right = jnp.where(x == x_ref[1], (right1, right0)[s][...], (right0, right1)[s][...])
        left = jnp.where(x == 0, (left1, left0)[s][...], (left0, left1)[s][...])
        total = own[...].astype(F32) + right.astype(F32) + left.astype(F32)
        out_ref[s] = total.astype(BF16)


def both_halves(x, last, own, from_right, from_left):
    blocks, step = own[0].shape[0], 4
    spec = pl.BlockSpec((step, 2, BLK, HD), lambda i: (i, 0, 0, 0))
    out = pl.pallas_call(
        both_halves_kernel,
        grid=(blocks // step,),
        out_shape=jax.ShapeDtypeStruct((2, blocks, 2, BLK, HD), BF16),
        in_specs=[pl.BlockSpec(memory_space=pltpu.SMEM)] + [spec] * 6,
        out_specs=pl.BlockSpec((2, step, 2, BLK, HD), lambda i: (0, i, 0, 0, 0)),
        cost_estimate=pl.CostEstimate(flops=0, bytes_accessed=16 * own[0].size, transcendentals=0),
        name="both_halves",
    )(jnp.stack([x, jnp.int32(last)]), *own, *from_right, *from_left)
    return out.reshape(2 * blocks, 2, BLK, HD)


WIDE = ("half", "core", "group")
PAIR = ("core", "group")
CHIPS = ("half", "x")


def shift(value, axes, steps):
    count = lax.axis_size(axes)
    return lax.ppermute(value, axes, [(s, (s + steps) % count) for s in range(count)])


def add(a, b):
    return (a.astype(F32) + b.astype(F32)).astype(BF16)


def exchange(x, axes):
    return lax.all_to_all(x, axes, 0, 0, tiled=True)


def after(x, *done):
    return lax.optimization_barrier((x, *done))[0]


def swap(value):
    return lax.ppermute(value, "core", [(0, 1), (1, 0)])


def shards(query_in, key_in, value_in, out_grad, key_blocks, block_count):
    half, x, core = (lax.axis_index(name) for name in ("half", "x", "core"))
    last, size = lax.axis_size("x") - 1, 2 * BPD
    packed = jnp.concatenate([key_blocks, block_count[:, :, None]], axis=2)
    gathered = lax.all_gather(packed, ("half", "core"))
    list_b = gathered[2 * half + core, 4]
    lists = lax.dynamic_index_in_dim(gathered, 2 * half + core, 1, False)
    ka, va, qda, b = split_heads(key_in, value_in, query_in, out_grad)

    def plain(lists, chip):
        lists = lists.reshape(-1, MAXK + 1)
        first_block = (chip - 1) * 2 * BPD
        return (lists[:, :MAXK] - first_block).reshape(-1), lists[:, MAXK]

    own_b = exchange(after(b, gathered), "group")
    pairs_b = own_b[:, :2]
    mine = (shift(pairs_b, CHIPS, 1), pairs_b, shift(pairs_b, CHIPS, -1))
    theirs = tuple(swap(pairs) for pairs in mine)

    keys = exchange(after(ka, own_b), WIDE)
    key_near = [shift(keys, "x", 1), shift(keys, "x", -1)]
    values = exchange(after(va, keys, *mine), WIDE)
    value_near = [shift(values, "x", 1), shift(values, "x", -1)]

    def run(i, other):
        def fetch(ref, place):
            at = i * size + (BPD - place[1] if other else place[1])
            return [(ref.at[:, t], t, pl.multiple_of(at, 8)) for t in range(2)]

        return fetch

    ids, counts = plain(list_b, half * (last + 1) + x)
    place = jnp.stack([jnp.int32(0), core * BPD])
    fetches = [run(i, other) for other in range(2) for i in range(3)]
    dq_b, (left_b, mine_b, right_b, give_b) = attention(
        ids, counts, place, mine + theirs, fetches, after(own_b, values, *key_near), BPD, size
    )
    give_b = after(give_b, *value_near)
    got_b = [swap(give_b[i]) for i in range(3)]
    out_b = lax.optimization_barrier((add(left_b, got_b[0]), add(right_b, got_b[2])))
    terms_b = [got_b[1], shift(out_b[0], CHIPS, -1), shift(out_b[1], CHIPS, 1)]

    queries = exchange(after(qda, values), WIDE)

    def third(t, i):
        return lambda ref, place: [(ref.at[pl.ds(pl.multiple_of(place[1 + i], 8), size)], t, i * size)]

    fetches = [third(t, i) for t in range(2) for i in range(3)]
    sources = (key_near[0], keys, key_near[1], value_near[0], values, value_near[1])
    done, back_b = [], ()
    for s in range(2):
        ids, counts = plain(lists[2 * s : 2 * s + 2], s * (last + 1) + x)
        left = jnp.where(x == 0, 1 - s, s) * size
        right = jnp.where(x == last, 1 - s, s) * size
        place = after(jnp.stack([jnp.int32(s * size), left, jnp.int32(s * size), right]), *back_b)
        dq, grads = attention(ids, counts, place, sources, fetches, queries, size, size)
        done.append((dq, grads, shift(grads[0], "x", -1), shift(grads[2], "x", 1)))
        if s == 0:
            total_b = total_grads(after(dq_b, dq), mine_b, terms_b)
            back_b = (total_b,)
    back_b = exchange(total_b, "group")
    dqa = exchange(after(jnp.concatenate([d[0] for d in done]), *done[0][2:], back_b), WIDE)
    dkva = both_halves(x, last, [d[1][1] for d in done], [d[2] for d in done], [d[3] for d in done])
    dkva = exchange(after(dkva, dqa), WIDE)
    return tuple(join_heads(dqa, dkva, back_b))


def solution(mesh):
    chips = mesh.shape["frame"] // 4
    mesh = Mesh(mesh.devices.reshape(2, chips, 2, -1), ("half", "x", "core", "group"))
    runs = ("half", "x", "core")
    tokens = P((*runs, "group"), None)
    return jax.shard_map(
        shards,
        mesh=mesh,
        in_specs=(tokens,) * 4 + (P("group", runs, None), P("group", runs)),
        out_specs=(tokens,) * 3,
        check_vma=False,
    )
```

```python
import functools

import jax
import jax.numpy as jnp
from jax import lax
from jax.experimental import pallas as pl
from jax.experimental.pallas import tpu as pltpu
from jax.sharding import Mesh
from jax.sharding import PartitionSpec as P

HD = 128
BLK = 128
BAND = 2
BPD = 8
MAXK = 12
HPG = 5
WAYS = 2
BUCKETS = (4, 6, 8, 10, 12)
STEP = 2
ATTENTION_COST = 10
VMEM_LIMIT = 56 * 2**20
NEG = -1e30
LOG2E = 1.4426950408889634
SCALE = HD**-0.5
F32 = jnp.float32
BF16 = jnp.bfloat16
NT = (((1,), (1,)), ((), ()))
NN = (((1,), (0,)), ((), ()))
TN = (((0,), (0,)), ((), ()))


def dot(a, b, dims):
    return lax.dot_general(a, b, dims, preferred_element_type=F32)


def fold(x):
    return x.reshape(-1, 8, HD)


def query_blocks(n_keys, blocks, ids_ref, counts, qd, kv, acc, dq, kv_cat, sd_scr, x_cat):
    ways = range(len(blocks))
    index = [[ids_ref[b * MAXK + s] for s in range(n_keys)] for b in blocks]
    rows = [pl.ds(s * BLK, BLK) for s in range(n_keys)]
    for i in ways:
        for s in range(n_keys):
            kv_cat[i, rows[s], :] = kv[index[i][s]]
    w_t = [qd[b] for b in blocks]
    for s in range(0, n_keys, STEP):
        part = pl.ds(s * BLK, min(STEP, n_keys - s) * BLK)
        for i in ways:
            sd_scr[i, part, :] = dot(kv_cat[i, part, :], w_t[i], NT)
    top = []
    for i in ways:
        m8 = jnp.full((8, HD), NEG, F32)
        for s in range(n_keys):
            st = sd_scr[i, rows[s], :HD]
            if s > 0:
                st = jnp.where(s < counts[i], st, NEG)
                sd_scr[i, rows[s], :HD] = st
            m8 = jnp.maximum(m8, jnp.max(fold(st), axis=0))
        top.append(jnp.max(m8, axis=0, keepdims=True) * (SCALE * LOG2E))
    inv, rd = [], []
    for i in ways:
        l8 = jnp.zeros((8, HD), F32)
        r8 = jnp.zeros((8, HD), F32)
        for s in range(n_keys):
            p = jnp.exp2(sd_scr[i, rows[s], :HD] * (SCALE * LOG2E) - top[i])
            sd_scr[i, rows[s], :HD] = p
            l8 += jnp.sum(fold(p), axis=0)
            r8 += jnp.sum(fold(p * sd_scr[i, rows[s], HD:]), axis=0)
        inv.append(1.0 / jnp.sum(l8, axis=0, keepdims=True))
        rd.append(jnp.sum(r8, axis=0, keepdims=True) * inv[i])
    for i in ways:
        for s in range(n_keys):
            p = sd_scr[i, rows[s], :HD] * inv[i]
            x_cat[i, rows[s], :HD] = (p * (sd_scr[i, rows[s], HD:] - rd[i])).astype(BF16)
            x_cat[i, rows[s], HD:] = p.astype(BF16)
        for s in range(0, n_keys, STEP):
            n = min(STEP, n_keys - s)
            terms = dot(x_cat[i, pl.ds(s * BLK, n * BLK), :], qd[blocks[i]], NN)
            for j in range(n):
                acc[index[i][s + j]] += terms[j * BLK : (j + 1) * BLK]
        every = pl.ds(0, n_keys * BLK)
        dq[blocks[i]] = (dot(x_cat[i, every, :HD], kv_cat[i, every, :HD], TN) * SCALE).astype(BF16)


def attention_kernel(size, n_query, fetches, ids_ref, cnt_ref, place_ref, *refs):
    sources, refs = refs[: len(fetches)], refs[len(fetches) :]
    shared = n_query < size
    qd_in, dq_out, targets = refs[0], refs[1], refs[2:5]
    if shared:
        give_out, refs = refs[5:8], refs[3:]
    kv, qd, acc, stage, dq, kv_cat, sd_scr, x_cat, order, in_sem, out_sem = refs[5:]
    copies = []
    for source, fetch in zip(sources, fetches):
        for src, t, row in fetch(source, place_ref):
            dst = kv.at[pl.ds(row, src.shape[0]), :, pl.ds(t * HD, HD)]
            copies.append(pltpu.make_async_copy(src, dst, in_sem.at[len(copies)]))
    q_rows = pl.ds(pl.multiple_of(place_ref[0], 8), n_query)
    for t in range(2):
        src = qd_in.at[q_rows, qd_in.shape[1] - 2 + t]
        dst = qd.at[:, pl.ds(t * HD, HD), pl.ds(t * HD, HD)]
        copies.append(pltpu.make_async_copy(src, dst, in_sem.at[len(copies)]))
    for copy in copies:
        copy.start()
    acc[...] = jnp.zeros_like(acc)
    for t in range(2):
        qd[:, t * HD : (t + 1) * HD, (1 - t) * HD : (2 - t) * HD] = jnp.zeros((n_query, HD, HD), BF16)
    def rank(k, at):
        def place(b, at):
            hit = cnt_ref[b] == MAXK - k

            @pl.when(hit)
            def _():
                order[at] = b

            return at + hit.astype(jnp.int32)

        return lax.fori_loop(0, n_query, place, at)

    lax.fori_loop(0, MAXK, rank, 0)
    for copy in copies:
        copy.wait()

    def some(k, carry):
        blocks = [order[k * WAYS + i] for i in range(WAYS)]
        counts = [cnt_ref[b] for b in blocks]
        for least, upto in zip((0, *BUCKETS), BUCKETS):

            @pl.when((counts[0] > least) & (counts[0] <= upto))
            def _():
                query_blocks(upto, blocks, ids_ref, counts, qd, kv, acc, dq, kv_cat, sd_scr, x_cat)

        return carry

    lax.fori_loop(0, n_query // WAYS, some, 0)
    puts = [pltpu.make_async_copy(dq, dq_out, out_sem.at[3])]
    puts[0].start()
    for i, target in enumerate(targets):

        def convert(j, carry):
            stage[j, 0] = (acc[j, :, :HD] * SCALE).astype(BF16)
            stage[j, 1] = acc[j, :, HD:].astype(BF16)
            return carry

        lax.fori_loop(i * size, (i + 1) * size, convert, 0)
        rows = pl.ds(i * size, size)
        if shared:
            keep = pl.multiple_of(i * size + place_ref[1], 8)
            give = pl.multiple_of(i * size + n_query - place_ref[1], 8)
            rows = pl.ds(keep, n_query)
            puts.append(
                pltpu.make_async_copy(stage.at[pl.ds(give, n_query)], give_out[i], out_sem.at[4 + i])
            )
            puts[-1].start()
        puts.append(pltpu.make_async_copy(stage.at[rows], target, out_sem.at[i]))
        puts[-1].start()
    for copy in puts:
        copy.wait()


def attention(ids, counts, place, sources, fetches, qd, n_query, size):
    window = 3 * size
    shared = n_query < size
    kept = jax.ShapeDtypeStruct((n_query, 2, BLK, HD), BF16)
    given = [kept] * 3 if shared else []
    smem = pl.BlockSpec(memory_space=pltpu.SMEM)
    hbm = pl.BlockSpec(memory_space=pl.ANY)
    pairs = n_query * 8
    out = pl.pallas_call(
        functools.partial(attention_kernel, size, n_query, fetches),
        out_shape=[jax.ShapeDtypeStruct((n_query, BLK, HD), BF16)] + [kept] * 3 + given,
        in_specs=[smem] * 3 + [hbm] * (len(sources) + 1),
        out_specs=[hbm] * (4 + len(given)),
        scratch_shapes=[
            pltpu.VMEM((window, BLK, 2 * HD), BF16),
            pltpu.VMEM((n_query, 2 * HD, 2 * HD), BF16),
            pltpu.VMEM((window, BLK, 2 * HD), F32),
            pltpu.VMEM((window, 2, BLK, HD), BF16),
            pltpu.VMEM((n_query, BLK, HD), BF16),
            pltpu.VMEM((WAYS, MAXK * BLK, 2 * HD), BF16),
            pltpu.VMEM((WAYS, MAXK * BLK, 2 * HD), F32),
            pltpu.VMEM((WAYS, MAXK * BLK, 2 * HD), BF16),
            pltpu.SMEM((n_query,), jnp.int32),
            pltpu.SemaphoreType.DMA((14,)),
            pltpu.SemaphoreType.DMA((7,)),
        ],
        compiler_params=pltpu.CompilerParams(vmem_limit_bytes=VMEM_LIMIT),
        cost_estimate=pl.CostEstimate(
            flops=0 if shared else pairs * ATTENTION_COST * BLK * BLK * HD,
            bytes_accessed=0 if shared else (2 * window + n_query) * 2 * BLK * HD * 2,
            transcendentals=0 if shared else pairs * BLK * BLK,
        ),
        name="attention",
    )(ids, counts, place, *sources, qd)
    return out[0], out[1:]


def split_kernel(k_ref, v_ref, q_ref, g_ref, ka_ref, va_ref, qda_ref):
    for j in range(ka_ref.shape[1]):
        for m in range(4):
            cols = slice((j * HPG + m) * HD, (j * HPG + m + 1) * HD)
            ka_ref[m, j] = k_ref[:, cols]
            va_ref[m, j] = v_ref[:, cols]
            qda_ref[m, j, 0] = q_ref[:, cols]
            qda_ref[m, j, 1] = g_ref[:, cols]


def split_heads(key_in, value_in, query_in, out_grad):
    groups, step = key_in.shape[1] // (HPG * HD), 2
    one = pl.BlockSpec((4, step, BLK, HD), lambda j: (0, j, 0, 0))
    two = pl.BlockSpec((4, step, 2, BLK, HD), lambda j: (0, j, 0, 0, 0))
    shapes = ((4, groups), (4, groups), (4, groups, 2))
    ka, va, qda = pl.pallas_call(
        split_kernel,
        grid=(groups // step,),
        out_shape=tuple(jax.ShapeDtypeStruct((*x, BLK, HD), BF16) for x in shapes),
        in_specs=[pl.BlockSpec((BLK, step * HPG * HD), lambda j: (0, j))] * 4,
        out_specs=(one, one, two),
        compiler_params=pltpu.CompilerParams(vmem_limit_bytes=VMEM_LIMIT),
        cost_estimate=pl.CostEstimate(flops=0, bytes_accessed=16 * key_in.size, transcendentals=0),
        name="split_heads",
    )(key_in, value_in, query_in, out_grad)
    flat = 4 * groups
    return ka.reshape(flat, BLK, HD), va.reshape(flat, BLK, HD), qda.reshape(flat, 2, BLK, HD)


def fifth_kernel(k_ref, v_ref, q_ref, g_ref, out_ref, held, sem_in, sem_out):
    groups = out_ref.shape[0]
    fetches, puts = [], []
    for j in range(groups):
        cols = pl.ds((j * HPG + HPG - 1) * HD, HD)
        for t, ref in enumerate((k_ref, v_ref, q_ref, g_ref)):
            fetches.append(pltpu.make_async_copy(ref.at[:, cols], held.at[j, t], sem_in.at[j, t]))
            fetches[-1].start()
    for j in range(groups):
        for t in range(4):
            fetches[4 * j + t].wait()
        puts.append(pltpu.make_async_copy(held.at[j], out_ref.at[j], sem_out.at[j]))
        puts[-1].start()
    for put in puts:
        put.wait()


def fifth_heads(*arrays):
    groups = arrays[0].shape[1] // (HPG * HD)
    hbm = pl.BlockSpec(memory_space=pl.ANY)
    return pl.pallas_call(
        fifth_kernel,
        out_shape=jax.ShapeDtypeStruct((groups, 4, BLK, HD), BF16),
        in_specs=[hbm] * 4,
        out_specs=hbm,
        scratch_shapes=[
            pltpu.VMEM((groups, 4, BLK, HD), BF16),
            pltpu.SemaphoreType.DMA((groups, 4)),
            pltpu.SemaphoreType.DMA((groups,)),
        ],
        compiler_params=pltpu.CompilerParams(vmem_limit_bytes=VMEM_LIMIT),
        cost_estimate=pl.CostEstimate(
            flops=0, bytes_accessed=groups * 16 * BLK * HD, transcendentals=0
        ),
        name="fifth_heads",
    )(*arrays)


def join_kernel(first, a_ref, b_ref, *outs):
    for t, ref in enumerate(outs):
        for j in range(b_ref.shape[0]):
            for m in range(HPG):
                value = b_ref[j, first + t] if m == 4 else a_ref[m, j, t]
                ref[:, (j * HPG + m) * HD : (j * HPG + m + 1) * HD] = value


def join_heads(back_a, back_b, first):
    groups, step, n = back_b.shape[0], 2, back_a.shape[1]
    out = jax.ShapeDtypeStruct((BLK, groups * HPG * HD), BF16)
    return pl.pallas_call(
        functools.partial(join_kernel, first),
        grid=(groups // step,),
        out_shape=(out,) * n,
        in_specs=[
            pl.BlockSpec((4, step, n, BLK, HD), lambda j: (0, j, 0, 0, 0)),
            pl.BlockSpec((step, 3, BLK, HD), lambda j: (j, 0, 0, 0)),
        ],
        out_specs=(pl.BlockSpec((BLK, step * HPG * HD), lambda j: (0, j)),) * n,
        compiler_params=pltpu.CompilerParams(vmem_limit_bytes=VMEM_LIMIT),
        cost_estimate=pl.CostEstimate(
            flops=0, bytes_accessed=groups * HPG * n * BLK * HD * 4, transcendentals=0
        ),
        name="join_heads",
    )(back_a.reshape(4, groups, n, BLK, HD), back_b)


def total_kernel(dq_ref, own_ref, *refs):
    terms, out_ref = refs[:-1], refs[-1]
    out_ref[:, 0] = dq_ref[...]
    total = own_ref[...].astype(F32)
    for term in terms:
        total += term[...].astype(F32)
    out_ref[:, 1:] = total.astype(BF16)


def total_grads(dq, own, terms):
    blocks, step = dq.shape[0], 4
    kv_spec = pl.BlockSpec((step, 2, BLK, HD), lambda i: (i, 0, 0, 0))
    return pl.pallas_call(
        total_kernel,
        grid=(blocks // step,),
        out_shape=jax.ShapeDtypeStruct((blocks, 3, BLK, HD), BF16),
        in_specs=[pl.BlockSpec((step, BLK, HD), lambda i: (i, 0, 0))] + [kv_spec] * (1 + len(terms)),
        out_specs=pl.BlockSpec((step, 3, BLK, HD), lambda i: (i, 0, 0, 0)),
        cost_estimate=pl.CostEstimate(
            flops=0, bytes_accessed=(6 + 2 * len(terms)) * dq.size * 2, transcendentals=0
        ),
        name="total_grads",
    )(dq, own, *terms)


def both_halves_kernel(x_ref, own0, own1, right0, right1, left0, left1, out_ref):
    x = x_ref[0]
    for s, own in enumerate((own0, own1)):
        right = jnp.where(x == x_ref[1], (right1, right0)[s][...], (right0, right1)[s][...])
        left = jnp.where(x == 0, (left1, left0)[s][...], (left0, left1)[s][...])
        total = own[...].astype(F32) + right.astype(F32) + left.astype(F32)
        out_ref[s] = total.astype(BF16)


def both_halves(x, last, own, from_right, from_left):
    blocks, step = own[0].shape[0], 4
    spec = pl.BlockSpec((step, 2, BLK, HD), lambda i: (i, 0, 0, 0))
    out = pl.pallas_call(
        both_halves_kernel,
        grid=(blocks // step,),
        out_shape=jax.ShapeDtypeStruct((2, blocks, 2, BLK, HD), BF16),
        in_specs=[pl.BlockSpec(memory_space=pltpu.SMEM)] + [spec] * 6,
        out_specs=pl.BlockSpec((2, step, 2, BLK, HD), lambda i: (0, i, 0, 0, 0)),
        cost_estimate=pl.CostEstimate(flops=0, bytes_accessed=16 * own[0].size, transcendentals=0),
        name="both_halves",
    )(jnp.stack([x, jnp.int32(last)]), *own, *from_right, *from_left)
    return out.reshape(2 * blocks, 2, BLK, HD)


WIDE = ("half", "core", "group")
PAIR = ("core", "group")
CHIPS = ("half", "x")


def shift(value, axes, steps):
    count = lax.axis_size(axes)
    ends = range(count) if axes == "x" else range(max(0, -steps), min(count, count - steps))
    return lax.ppermute(value, axes, [(s, (s + steps) % count) for s in ends])


def add(a, b):
    return (a.astype(F32) + b.astype(F32)).astype(BF16)


def exchange(x, axes):
    return lax.all_to_all(x, axes, 0, 0, tiled=True)


def after(x, *done):
    return lax.optimization_barrier((x, *done))[0]


def swap(value):
    return lax.ppermute(value, "core", [(0, 1), (1, 0)])


def shards(query_in, key_in, value_in, out_grad, key_blocks, block_count):
    half, x, core = (lax.axis_index(name) for name in ("half", "x", "core"))
    last, size = lax.axis_size("x") - 1, 2 * BPD
    packed = jnp.concatenate([key_blocks, block_count[:, :, None]], axis=2)
    b = fifth_heads(key_in, value_in, query_in, out_grad)
    gathered = lax.all_gather(after(packed, b), ("half", "core"))
    list_b = gathered[2 * half + core, 4]
    lists = lax.dynamic_index_in_dim(gathered, 2 * half + core, 1, False)
    ka, va, qda = split_heads(*lax.optimization_barrier((key_in, value_in, query_in, out_grad, b))[:4])

    def plain(lists, chip):
        lists = lists.reshape(-1, MAXK + 1)
        first_block = (chip - 1) * 2 * BPD
        return (lists[:, :MAXK] - first_block).reshape(-1), lists[:, MAXK]

    own_b = exchange(b, "group")
    pairs_b = own_b[:, :2]
    mine = (shift(pairs_b, CHIPS, 1), pairs_b, shift(pairs_b, CHIPS, -1))
    theirs = tuple(swap(pairs) for pairs in mine)

    keys = exchange(after(ka, own_b, gathered), WIDE)
    key_near = [shift(keys, "x", 1), shift(keys, "x", -1)]
    values = exchange(after(va, keys, *mine), WIDE)
    value_near = [shift(values, "x", 1), shift(values, "x", -1)]

    def run(i, other):
        def fetch(ref, place):
            at = i * size + (BPD - place[1] if other else place[1])
            return [(ref.at[:, t], t, pl.multiple_of(at, 8)) for t in range(2)]

        return fetch

    ids, counts = plain(list_b, half * (last + 1) + x)
    place = jnp.stack([jnp.int32(0), core * BPD])
    fetches = [run(i, other) for other in range(2) for i in range(3)]
    dq_b, (left_b, mine_b, right_b, *give_b) = attention(
        ids, counts, place, mine + theirs, fetches, after(own_b, values, *key_near), BPD, size
    )
    got_b = [swap(after(give, *value_near)) for give in give_b]
    out_b = lax.optimization_barrier((add(left_b, got_b[0]), add(right_b, got_b[2])))
    terms_b = [got_b[1], shift(out_b[0], CHIPS, -1), shift(out_b[1], CHIPS, 1)]

    queries = exchange(after(qda, values), WIDE)

    def third(t, i):
        return lambda ref, place: [(ref.at[pl.ds(pl.multiple_of(place[1 + i], 8), size)], t, i * size)]

    fetches = [third(t, i) for t in range(2) for i in range(3)]
    sources = (key_near[0], keys, key_near[1], value_near[0], values, value_near[1])
    done, back_b = [], ()
    for s in range(2):
        ids, counts = plain(lists[2 * s : 2 * s + 2], s * (last + 1) + x)
        left = jnp.where(x == 0, 1 - s, s) * size
        right = jnp.where(x == last, 1 - s, s) * size
        place = after(jnp.stack([jnp.int32(s * size), left, jnp.int32(s * size), right]), *back_b)
        dq, grads = attention(ids, counts, place, sources, fetches, queries, size, size)
        done.append((dq, grads, shift(grads[0], "x", -1), shift(grads[2], "x", 1)))
        if s == 0:
            total_b = total_grads(after(dq_b, dq), mine_b, terms_b)
            back_b = (total_b,)
    back_b = exchange(total_b, "group")
    dqa = exchange(after(jnp.concatenate([d[0] for d in done]), *done[0][2:], back_b), WIDE)
    dkva = both_halves(x, last, [d[1][1] for d in done], [d[2] for d in done], [d[3] for d in done])
    dkva = exchange(after(dkva, dqa), WIDE)
    return (*join_heads(dqa[:, None], back_b, 0), *join_heads(dkva, back_b, 1))


def solution(mesh):
    chips = mesh.shape["frame"] // 4
    mesh = Mesh(mesh.devices.reshape(2, chips, 2, -1), ("half", "x", "core", "group"))
    runs = ("half", "x", "core")
    tokens = P((*runs, "group"), None)
    return jax.shard_map(
        shards,
        mesh=mesh,
        in_specs=(tokens,) * 4 + (P("group", runs, None), P("group", runs)),
        out_specs=(tokens,) * 3,
        check_vma=False,
    )
```

```python
import functools

import jax
import jax.numpy as jnp
from jax import lax
from jax.experimental import pallas as pl
from jax.experimental.pallas import tpu as pltpu
from jax.sharding import Mesh
from jax.sharding import PartitionSpec as P

HD = 128
BLK = 128
BAND = 2
BPD = 8
MAXK = 12
HPG = 5
WAYS = 2
BUCKETS = (4, 6, 8, 10, 12)
STEP = 2
ATTENTION_COST = 10
VMEM_LIMIT = 56 * 2**20
NEG = -1e30
LOG2E = 1.4426950408889634
SCALE = HD**-0.5
F32 = jnp.float32
BF16 = jnp.bfloat16
NT = (((1,), (1,)), ((), ()))
NN = (((1,), (0,)), ((), ()))
TN = (((0,), (0,)), ((), ()))


def dot(a, b, dims):
    return lax.dot_general(a, b, dims, preferred_element_type=F32)


def fold(x):
    return x.reshape(-1, 8, HD)


def query_blocks(n_keys, blocks, ids_ref, counts, qd, kv, acc, dq, kv_cat, sd_scr, x_cat):
    ways = range(len(blocks))
    index = [[ids_ref[b * MAXK + s] for s in range(n_keys)] for b in blocks]
    rows = [pl.ds(s * BLK, BLK) for s in range(n_keys)]
    for i in ways:
        for s in range(n_keys):
            kv_cat[i, rows[s], :] = kv[index[i][s]]
    w_t = [qd[b] for b in blocks]
    for s in range(0, n_keys, STEP):
        part = pl.ds(s * BLK, min(STEP, n_keys - s) * BLK)
        for i in ways:
            sd_scr[i, part, :] = dot(kv_cat[i, part, :], w_t[i], NT)
    top = []
    for i in ways:
        m8 = jnp.full((8, HD), NEG, F32)
        for s in range(n_keys):
            st = sd_scr[i, rows[s], :HD]
            if s > 0:
                st = jnp.where(s < counts[i], st, NEG)
                sd_scr[i, rows[s], :HD] = st
            m8 = jnp.maximum(m8, jnp.max(fold(st), axis=0))
        top.append(jnp.max(m8, axis=0, keepdims=True) * (SCALE * LOG2E))
    inv, rd = [], []
    for i in ways:
        l8 = jnp.zeros((8, HD), F32)
        r8 = jnp.zeros((8, HD), F32)
        for s in range(n_keys):
            p = jnp.exp2(sd_scr[i, rows[s], :HD] * (SCALE * LOG2E) - top[i])
            sd_scr[i, rows[s], :HD] = p
            l8 += jnp.sum(fold(p), axis=0)
            r8 += jnp.sum(fold(p * sd_scr[i, rows[s], HD:]), axis=0)
        inv.append(1.0 / jnp.sum(l8, axis=0, keepdims=True))
        rd.append(jnp.sum(r8, axis=0, keepdims=True) * inv[i])
    for i in ways:
        for s in range(n_keys):
            p = sd_scr[i, rows[s], :HD] * inv[i]
            x_cat[i, rows[s], :HD] = (p * (sd_scr[i, rows[s], HD:] - rd[i])).astype(BF16)
            x_cat[i, rows[s], HD:] = p.astype(BF16)
        for s in range(0, n_keys, STEP):
            n = min(STEP, n_keys - s)
            terms = dot(x_cat[i, pl.ds(s * BLK, n * BLK), :], qd[blocks[i]], NN)
            for j in range(n):
                acc[index[i][s + j]] += terms[j * BLK : (j + 1) * BLK]
        every = pl.ds(0, n_keys * BLK)
        dq[blocks[i]] = (dot(x_cat[i, every, :HD], kv_cat[i, every, :HD], TN) * SCALE).astype(BF16)


def attention_kernel(size, n_query, fetches, ids_ref, cnt_ref, place_ref, *refs):
    sources, refs = refs[: len(fetches)], refs[len(fetches) :]
    shared = n_query < size
    qd_in, dq_out, targets = refs[0], refs[1], refs[2:5]
    if shared:
        give_out, refs = refs[5:8], refs[3:]
    kv, qd, acc, stage, dq, kv_cat, sd_scr, x_cat, order, in_sem, out_sem = refs[5:]
    copies = []
    for source, fetch in zip(sources, fetches):
        for src, t, row in fetch(source, place_ref):
            dst = kv.at[pl.ds(row, src.shape[0]), :, pl.ds(t * HD, HD)]
            copies.append(pltpu.make_async_copy(src, dst, in_sem.at[len(copies)]))
    q_rows = pl.ds(pl.multiple_of(place_ref[0], 8), n_query)
    for t in range(2):
        src = qd_in.at[q_rows, qd_in.shape[1] - 2 + t]
        dst = qd.at[:, pl.ds(t * HD, HD), pl.ds(t * HD, HD)]
        copies.append(pltpu.make_async_copy(src, dst, in_sem.at[len(copies)]))
    for copy in copies:
        copy.start()
    acc[...] = jnp.zeros_like(acc)
    for t in range(2):
        qd[:, t * HD : (t + 1) * HD, (1 - t) * HD : (2 - t) * HD] = jnp.zeros((n_query, HD, HD), BF16)
    def rank(k, at):
        def place(b, at):
            hit = cnt_ref[b] == MAXK - k

            @pl.when(hit)
            def _():
                order[at] = b

            return at + hit.astype(jnp.int32)

        return lax.fori_loop(0, n_query, place, at)

    lax.fori_loop(0, MAXK, rank, 0)
    for copy in copies:
        copy.wait()

    def some(k, carry):
        blocks = [order[k * WAYS + i] for i in range(WAYS)]
        counts = [cnt_ref[b] for b in blocks]
        for least, upto in zip((0, *BUCKETS), BUCKETS):

            @pl.when((counts[0] > least) & (counts[0] <= upto))
            def _():
                query_blocks(upto, blocks, ids_ref, counts, qd, kv, acc, dq, kv_cat, sd_scr, x_cat)

        return carry

    lax.fori_loop(0, n_query // WAYS, some, 0)
    puts = [pltpu.make_async_copy(dq, dq_out, out_sem.at[3])]
    puts[0].start()
    for i, target in enumerate(targets):

        def convert(j, carry):
            stage[j, 0] = (acc[j, :, :HD] * SCALE).astype(BF16)
            stage[j, 1] = acc[j, :, HD:].astype(BF16)
            return carry

        lax.fori_loop(i * size, (i + 1) * size, convert, 0)
        rows = pl.ds(i * size, size)
        if shared:
            keep = pl.multiple_of(i * size + place_ref[1], 8)
            give = pl.multiple_of(i * size + n_query - place_ref[1], 8)
            rows = pl.ds(keep, n_query)
            puts.append(
                pltpu.make_async_copy(stage.at[pl.ds(give, n_query)], give_out[i], out_sem.at[4 + i])
            )
            puts[-1].start()
        puts.append(pltpu.make_async_copy(stage.at[rows], target, out_sem.at[i]))
        puts[-1].start()
    for copy in puts:
        copy.wait()


def attention(ids, counts, place, sources, fetches, qd, n_query, size):
    window = 3 * size
    shared = n_query < size
    kept = jax.ShapeDtypeStruct((n_query, 2, BLK, HD), BF16)
    given = [kept] * 3 if shared else []
    smem = pl.BlockSpec(memory_space=pltpu.SMEM)
    hbm = pl.BlockSpec(memory_space=pl.ANY)
    pairs = n_query * 8
    out = pl.pallas_call(
        functools.partial(attention_kernel, size, n_query, fetches),
        out_shape=[jax.ShapeDtypeStruct((n_query, BLK, HD), BF16)] + [kept] * 3 + given,
        in_specs=[smem] * 3 + [hbm] * (len(sources) + 1),
        out_specs=[hbm] * (4 + len(given)),
        scratch_shapes=[
            pltpu.VMEM((window, BLK, 2 * HD), BF16),
            pltpu.VMEM((n_query, 2 * HD, 2 * HD), BF16),
            pltpu.VMEM((window, BLK, 2 * HD), F32),
            pltpu.VMEM((window, 2, BLK, HD), BF16),
            pltpu.VMEM((n_query, BLK, HD), BF16),
            pltpu.VMEM((WAYS, MAXK * BLK, 2 * HD), BF16),
            pltpu.VMEM((WAYS, MAXK * BLK, 2 * HD), F32),
            pltpu.VMEM((WAYS, MAXK * BLK, 2 * HD), BF16),
            pltpu.SMEM((n_query,), jnp.int32),
            pltpu.SemaphoreType.DMA((14,)),
            pltpu.SemaphoreType.DMA((7,)),
        ],
        compiler_params=pltpu.CompilerParams(vmem_limit_bytes=VMEM_LIMIT),
        cost_estimate=pl.CostEstimate(
            flops=0 if shared else pairs * ATTENTION_COST * BLK * BLK * HD,
            bytes_accessed=0 if shared else (2 * window + n_query) * 2 * BLK * HD * 2,
            transcendentals=0 if shared else pairs * BLK * BLK,
        ),
        name="attention",
    )(ids, counts, place, *sources, qd)
    return out[0], out[1:]


def split_kernel(k_ref, v_ref, q_ref, g_ref, ka_ref, va_ref, qda_ref):
    for j in range(ka_ref.shape[1]):
        for m in range(4):
            cols = slice((j * HPG + m) * HD, (j * HPG + m + 1) * HD)
            ka_ref[m, j] = k_ref[:, cols]
            va_ref[m, j] = v_ref[:, cols]
            qda_ref[m, j, 0] = q_ref[:, cols]
            qda_ref[m, j, 1] = g_ref[:, cols]


def split_heads(key_in, value_in, query_in, out_grad):
    groups, step = key_in.shape[1] // (HPG * HD), 2
    one = pl.BlockSpec((4, step, BLK, HD), lambda j: (0, j, 0, 0))
    two = pl.BlockSpec((4, step, 2, BLK, HD), lambda j: (0, j, 0, 0, 0))
    shapes = ((4, groups), (4, groups), (4, groups, 2))
    ka, va, qda = pl.pallas_call(
        split_kernel,
        grid=(groups // step,),
        out_shape=tuple(jax.ShapeDtypeStruct((*x, BLK, HD), BF16) for x in shapes),
        in_specs=[pl.BlockSpec((BLK, step * HPG * HD), lambda j: (0, j))] * 4,
        out_specs=(one, one, two),
        compiler_params=pltpu.CompilerParams(vmem_limit_bytes=VMEM_LIMIT),
        cost_estimate=pl.CostEstimate(flops=0, bytes_accessed=16 * key_in.size, transcendentals=0),
        name="split_heads",
    )(key_in, value_in, query_in, out_grad)
    flat = 4 * groups
    return ka.reshape(flat, BLK, HD), va.reshape(flat, BLK, HD), qda.reshape(flat, 2, BLK, HD)


def fifth_kernel(k_ref, v_ref, q_ref, g_ref, out_ref, held, sem_in, sem_out):
    groups = out_ref.shape[0]
    fetches, puts = [], []
    for j in range(groups):
        cols = pl.ds((j * HPG + HPG - 1) * HD, HD)
        for t, ref in enumerate((k_ref, v_ref, q_ref, g_ref)):
            fetches.append(pltpu.make_async_copy(ref.at[:, cols], held.at[j, t], sem_in.at[j, t]))
            fetches[-1].start()
    for j in range(groups):
        for t in range(4):
            fetches[4 * j + t].wait()
        puts.append(pltpu.make_async_copy(held.at[j], out_ref.at[j], sem_out.at[j]))
        puts[-1].start()
    for put in puts:
        put.wait()


def fifth_heads(*arrays):
    groups = arrays[0].shape[1] // (HPG * HD)
    hbm = pl.BlockSpec(memory_space=pl.ANY)
    return pl.pallas_call(
        fifth_kernel,
        out_shape=jax.ShapeDtypeStruct((groups, 4, BLK, HD), BF16),
        in_specs=[hbm] * 4,
        out_specs=hbm,
        scratch_shapes=[
            pltpu.VMEM((groups, 4, BLK, HD), BF16),
            pltpu.SemaphoreType.DMA((groups, 4)),
            pltpu.SemaphoreType.DMA((groups,)),
        ],
        compiler_params=pltpu.CompilerParams(vmem_limit_bytes=VMEM_LIMIT),
        cost_estimate=pl.CostEstimate(
            flops=0, bytes_accessed=groups * 16 * BLK * HD, transcendentals=0
        ),
        name="fifth_heads",
    )(*arrays)


def join_kernel(first, a_ref, b_ref, *outs):
    for t, ref in enumerate(outs):
        for j in range(b_ref.shape[0]):
            for m in range(HPG):
                value = b_ref[j, first + t] if m == 4 else a_ref[m, j, t]
                ref[:, (j * HPG + m) * HD : (j * HPG + m + 1) * HD] = value


def join_heads(back_a, back_b, first):
    groups, step, n = back_b.shape[0], 2, back_a.shape[1]
    out = jax.ShapeDtypeStruct((BLK, groups * HPG * HD), BF16)
    return pl.pallas_call(
        functools.partial(join_kernel, first),
        grid=(groups // step,),
        out_shape=(out,) * n,
        in_specs=[
            pl.BlockSpec((4, step, n, BLK, HD), lambda j: (0, j, 0, 0, 0)),
            pl.BlockSpec((step, 3, BLK, HD), lambda j: (j, 0, 0, 0)),
        ],
        out_specs=(pl.BlockSpec((BLK, step * HPG * HD), lambda j: (0, j)),) * n,
        compiler_params=pltpu.CompilerParams(vmem_limit_bytes=VMEM_LIMIT),
        cost_estimate=pl.CostEstimate(
            flops=0, bytes_accessed=groups * HPG * n * BLK * HD * 4, transcendentals=0
        ),
        name="join_heads",
    )(back_a.reshape(4, groups, n, BLK, HD), back_b)


def total_kernel(dq_ref, own_ref, *refs):
    terms, out_ref = refs[:-1], refs[-1]
    out_ref[:, 0] = dq_ref[...]
    total = own_ref[...].astype(F32)
    for term in terms:
        total += term[...].astype(F32)
    out_ref[:, 1:] = total.astype(BF16)


def total_grads(dq, own, terms):
    blocks, step = dq.shape[0], 4
    kv_spec = pl.BlockSpec((step, 2, BLK, HD), lambda i: (i, 0, 0, 0))
    return pl.pallas_call(
        total_kernel,
        grid=(blocks // step,),
        out_shape=jax.ShapeDtypeStruct((blocks, 3, BLK, HD), BF16),
        in_specs=[pl.BlockSpec((step, BLK, HD), lambda i: (i, 0, 0))] + [kv_spec] * (1 + len(terms)),
        out_specs=pl.BlockSpec((step, 3, BLK, HD), lambda i: (i, 0, 0, 0)),
        cost_estimate=pl.CostEstimate(
            flops=0, bytes_accessed=(6 + 2 * len(terms)) * dq.size * 2, transcendentals=0
        ),
        name="total_grads",
    )(dq, own, *terms)


def both_halves_kernel(x_ref, own0, own1, right0, right1, left0, left1, out_ref):
    x = x_ref[0]
    for s, own in enumerate((own0, own1)):
        right = jnp.where(x == x_ref[1], (right1, right0)[s][...], (right0, right1)[s][...])
        left = jnp.where(x == 0, (left1, left0)[s][...], (left0, left1)[s][...])
        total = own[...].astype(F32) + right.astype(F32) + left.astype(F32)
        out_ref[s] = total.astype(BF16)


def both_halves(x, last, own, from_right, from_left):
    blocks, step = own[0].shape[0], 4
    spec = pl.BlockSpec((step, 2, BLK, HD), lambda i: (i, 0, 0, 0))
    out = pl.pallas_call(
        both_halves_kernel,
        grid=(blocks // step,),
        out_shape=jax.ShapeDtypeStruct((2, blocks, 2, BLK, HD), BF16),
        in_specs=[pl.BlockSpec(memory_space=pltpu.SMEM)] + [spec] * 6,
        out_specs=pl.BlockSpec((2, step, 2, BLK, HD), lambda i: (0, i, 0, 0, 0)),
        cost_estimate=pl.CostEstimate(flops=0, bytes_accessed=16 * own[0].size, transcendentals=0),
        name="both_halves",
    )(jnp.stack([x, jnp.int32(last)]), *own, *from_right, *from_left)
    return out.reshape(2 * blocks, 2, BLK, HD)


WIDE = ("half", "core", "group")
PAIR = ("core", "group")
CHIPS = ("half", "x")


def shift(value, axes, steps):
    count = lax.axis_size(axes)
    return lax.ppermute(value, axes, [(s, (s + steps) % count) for s in range(count)])


def add(a, b):
    return (a.astype(F32) + b.astype(F32)).astype(BF16)


def exchange(x, axes):
    return lax.all_to_all(x, axes, 0, 0, tiled=True)


def after(x, *done):
    return lax.optimization_barrier((x, *done))[0]


def swap(value):
    return lax.ppermute(value, "core", [(0, 1), (1, 0)])


def shards(query_in, key_in, value_in, out_grad, key_blocks, block_count):
    half, x, core = (lax.axis_index(name) for name in ("half", "x", "core"))
    last, size = lax.axis_size("x") - 1, 2 * BPD
    packed = jnp.concatenate([key_blocks, block_count[:, :, None]], axis=2)
    b = fifth_heads(key_in, value_in, query_in, out_grad)
    gathered = lax.all_gather(after(packed, b), ("half", "core"))
    list_b = gathered[2 * half + core, 4]
    lists = lax.dynamic_index_in_dim(gathered, 2 * half + core, 1, False)
    ka, va, qda = split_heads(*lax.optimization_barrier((key_in, value_in, query_in, out_grad, b))[:4])

    def plain(lists, chip):
        lists = lists.reshape(-1, MAXK + 1)
        first_block = (chip - 1) * 2 * BPD
        return (lists[:, :MAXK] - first_block).reshape(-1), lists[:, MAXK]

    own_b = exchange(b, "group")
    pairs_b = own_b[:, :2]
    mine = (shift(pairs_b, CHIPS, 1), pairs_b, shift(pairs_b, CHIPS, -1))

    keys = exchange(after(ka, own_b, gathered), WIDE)
    key_near = [shift(keys, "x", 1), shift(keys, "x", -1)]
    values = first_values = exchange(after(va, keys, *mine), WIDE)
    values = after(values, *key_near)
    value_near = [shift(values, "x", 1), shift(values, "x", -1)]
    theirs = tuple(swap(after(pairs, values, *key_near)) for pairs in mine)

    def run(i, other):
        def fetch(ref, place):
            at = i * size + (BPD - place[1] if other else place[1])
            return [(ref.at[:, t], t, pl.multiple_of(at, 8)) for t in range(2)]

        return fetch

    ids, counts = plain(list_b, half * (last + 1) + x)
    place = jnp.stack([jnp.int32(0), core * BPD])
    fetches = [run(i, other) for other in range(2) for i in range(3)]
    dq_b, (left_b, mine_b, right_b, *give_b) = attention(
        ids, counts, place, mine + theirs, fetches, after(own_b, values, *key_near), BPD, size
    )
    got_b = [swap(after(give, *value_near)) for give in give_b]

    queries = exchange(after(qda, first_values), WIDE)

    def third(t, i):
        return lambda ref, place: [(ref.at[pl.ds(pl.multiple_of(place[1 + i], 8), size)], t, i * size)]

    fetches = [third(t, i) for t in range(2) for i in range(3)]
    sources = (key_near[0], keys, key_near[1], value_near[0], values, value_near[1])
    done = []
    for s in range(2):
        ids, counts = plain(lists[2 * s : 2 * s + 2], s * (last + 1) + x)
        left = jnp.where(x == 0, 1 - s, s) * size
        right = jnp.where(x == last, 1 - s, s) * size
        place = jnp.stack([jnp.int32(s * size), left, jnp.int32(s * size), right])
        place = after(place, *[d[0] for d in done])
        dq, grads = attention(ids, counts, place, sources, fetches, queries, size, size)
        done.append((dq, grads, shift(grads[0], "x", -1), shift(grads[2], "x", 1)))
        if s == 0:
            left_b, right_b = add(after(left_b, dq), got_b[0]), add(after(right_b, dq), got_b[2])
            terms_b = [got_b[1], shift(left_b, CHIPS, -1), shift(right_b, CHIPS, 1)]
    total_b = total_grads(after(dq_b, done[1][0]), mine_b, terms_b)
    back_b = exchange(total_b, "group")
    dqa = exchange(after(jnp.concatenate([d[0] for d in done]), *done[0][2:], back_b), WIDE)
    dkva = both_halves(x, last, [d[1][1] for d in done], [d[2] for d in done], [d[3] for d in done])
    dkva = exchange(after(dkva, dqa), WIDE)
    return (*join_heads(dqa[:, None], back_b, 0), *join_heads(dkva, back_b, 1))


def solution(mesh):
    chips = mesh.shape["frame"] // 4
    mesh = Mesh(mesh.devices.reshape(2, chips, 2, -1), ("half", "x", "core", "group"))
    runs = ("half", "x", "core")
    tokens = P((*runs, "group"), None)
    return jax.shard_map(
        shards,
        mesh=mesh,
        in_specs=(tokens,) * 4 + (P("group", runs, None), P("group", runs)),
        out_specs=(tokens,) * 3,
        check_vma=False,
    )
```

```python
import functools

import jax
import jax.numpy as jnp
from jax import lax
from jax.experimental import pallas as pl
from jax.experimental.pallas import tpu as pltpu
from jax.sharding import Mesh
from jax.sharding import PartitionSpec as P

HD = 128
BLK = 128
BAND = 2
BPD = 8
MAXK = 12
HPG = 5
WAYS = 2
PLACES = 7
BUCKETS = (4, 6, 8, 10, 12)
STEP = 2
ATTENTION_COST = 10
VMEM_LIMIT = 56 * 2**20
NEG = -1e30
LOG2E = 1.4426950408889634
SCALE = HD**-0.5
F32 = jnp.float32
BF16 = jnp.bfloat16
NT = (((1,), (1,)), ((), ()))
NN = (((1,), (0,)), ((), ()))
TN = (((0,), (0,)), ((), ()))


def dot(a, b, dims):
    return lax.dot_general(a, b, dims, preferred_element_type=F32)


def fold(x):
    return x.reshape(-1, 8, HD)


def query_blocks(n_keys, blocks, ids, counts, qd, kv, acc, dq, kv_cat, sd_scr, x_cat):
    ways = range(len(blocks))
    index = [[ids(b, s) for s in range(n_keys)] for b in blocks]
    rows = [pl.ds(s * BLK, BLK) for s in range(n_keys)]
    for i in ways:
        for s in range(n_keys):
            kv_cat[i, rows[s], :] = kv[index[i][s]]
    w_t = [qd[b] for b in blocks]
    for s in range(0, n_keys, STEP):
        part = pl.ds(s * BLK, min(STEP, n_keys - s) * BLK)
        for i in ways:
            sd_scr[i, part, :] = dot(kv_cat[i, part, :], w_t[i], NT)
    hidden = [[jnp.where(s < counts[i], 0.0, NEG) for s in range(n_keys)] for i in ways]
    top = []
    for i in ways:
        m8 = jnp.full((8, HD), NEG, F32)
        for s in range(n_keys):
            m8 = jnp.maximum(m8, jnp.max(fold(sd_scr[i, rows[s], :HD]), axis=0) + hidden[i][s])
        top.append(jnp.max(m8, axis=0, keepdims=True) * (SCALE * LOG2E))
    inv, rd = [], []
    for i in ways:
        l8 = jnp.zeros((8, HD), F32)
        r8 = jnp.zeros((8, HD), F32)
        for s in range(n_keys):
            p = jnp.exp2(sd_scr[i, rows[s], :HD] * (SCALE * LOG2E) - (top[i] - hidden[i][s]))
            sd_scr[i, rows[s], :HD] = p
            l8 += jnp.sum(fold(p), axis=0)
            r8 += jnp.sum(fold(p * sd_scr[i, rows[s], HD:]), axis=0)
        inv.append(1.0 / jnp.sum(l8, axis=0, keepdims=True))
        rd.append(jnp.sum(r8, axis=0, keepdims=True) * inv[i])
    for i in ways:
        for s in range(n_keys):
            p = sd_scr[i, rows[s], :HD] * inv[i]
            x_cat[i, rows[s], :HD] = (p * (sd_scr[i, rows[s], HD:] - rd[i])).astype(BF16)
            x_cat[i, rows[s], HD:] = p.astype(BF16)
        for s in range(0, n_keys, STEP):
            n = min(STEP, n_keys - s)
            terms = dot(x_cat[i, pl.ds(s * BLK, n * BLK), :], qd[blocks[i]], NN)
            for j in range(n):
                acc[index[i][s + j]] += terms[j * BLK : (j + 1) * BLK]
        every = pl.ds(0, n_keys * BLK)
        dq[blocks[i]] = (dot(x_cat[i, every, :HD], kv_cat[i, every, :HD], TN) * SCALE).astype(BF16)


def attention_kernel(part, size, n_query, fetches, lists_ref, places_ref, *refs):
    place = [places_ref[part * PLACES + i] for i in range(PLACES)]
    sources, refs = refs[: len(fetches)], refs[len(fetches) :]
    shared = n_query < size
    qd_in, dq_out, targets = refs[0], refs[1], refs[2:5]
    if shared:
        give_out, refs = refs[5:8], refs[3:]
    kv, qd, acc, stage, dq, kv_cat, sd_scr, x_cat, order, counted, in_sem, out_sem = refs[5:]
    copies = []
    for source, fetch in zip(sources, fetches):
        for src, t, row in fetch(source, place):
            dst = kv.at[pl.ds(row, src.shape[0]), :, pl.ds(t * HD, HD)]
            copies.append(pltpu.make_async_copy(src, dst, in_sem.at[len(copies)]))
    q_rows = pl.ds(pl.multiple_of(place[0], 8), n_query)
    for t in range(2):
        src = qd_in.at[q_rows, qd_in.shape[1] - 2 + t]
        dst = qd.at[:, pl.ds(t * HD, HD), pl.ds(t * HD, HD)]
        copies.append(pltpu.make_async_copy(src, dst, in_sem.at[len(copies)]))
    for copy in copies:
        copy.start()
    acc[...] = jnp.zeros_like(acc)
    for t in range(2):
        qd[:, t * HD : (t + 1) * HD, (1 - t) * HD : (2 - t) * HD] = jnp.zeros((n_query, HD, HD), BF16)
    def entry(b, s):
        run = lax.shift_right_logical(b, 3)
        return lists_ref[place[4] + run * place[6] + (b - run * BPD) * (MAXK + 1) + s]

    def ids(b, s):
        return entry(b, s) - place[5]

    def note(b, carry):
        counted[b] = entry(b, MAXK)
        return carry

    lax.fori_loop(0, n_query, note, 0)

    def rank(k, at):
        def put(b, at):
            hit = counted[b] == MAXK - k

            @pl.when(hit)
            def _():
                order[at] = b

            return at + hit.astype(jnp.int32)

        return lax.fori_loop(0, n_query, put, at)

    lax.fori_loop(0, MAXK, rank, 0)
    for copy in copies:
        copy.wait()

    def some(k, carry):
        blocks = [order[k * WAYS + i] for i in range(WAYS)]
        counts = [counted[b] for b in blocks]
        for least, upto in zip((0, *BUCKETS), BUCKETS):

            @pl.when((counts[0] > least) & (counts[0] <= upto))
            def _():
                query_blocks(upto, blocks, ids, counts, qd, kv, acc, dq, kv_cat, sd_scr, x_cat)

        return carry

    lax.fori_loop(0, n_query // WAYS, some, 0)
    puts = [pltpu.make_async_copy(dq, dq_out, out_sem.at[3])]
    puts[0].start()
    for i, target in enumerate(targets):

        def convert(j, carry):
            stage[j, 0] = (acc[j, :, :HD] * SCALE).astype(BF16)
            stage[j, 1] = acc[j, :, HD:].astype(BF16)
            return carry

        lax.fori_loop(i * size, (i + 1) * size, convert, 0)
        rows = pl.ds(i * size, size)
        if shared:
            keep = pl.multiple_of(i * size + place[1], 8)
            give = pl.multiple_of(i * size + n_query - place[1], 8)
            rows = pl.ds(keep, n_query)
            puts.append(
                pltpu.make_async_copy(stage.at[pl.ds(give, n_query)], give_out[i], out_sem.at[4 + i])
            )
            puts[-1].start()
        puts.append(pltpu.make_async_copy(stage.at[rows], target, out_sem.at[i]))
        puts[-1].start()
    for copy in puts:
        copy.wait()


def attention(part, lists, places, sources, fetches, qd, n_query, size):
    window = 3 * size
    shared = n_query < size
    kept = jax.ShapeDtypeStruct((n_query, 2, BLK, HD), BF16)
    given = [kept] * 3 if shared else []
    smem = pl.BlockSpec(memory_space=pltpu.SMEM)
    hbm = pl.BlockSpec(memory_space=pl.ANY)
    pairs = n_query * 8
    out = pl.pallas_call(
        functools.partial(attention_kernel, part, size, n_query, fetches),
        out_shape=[jax.ShapeDtypeStruct((n_query, BLK, HD), BF16)] + [kept] * 3 + given,
        in_specs=[smem] * 2 + [hbm] * (len(sources) + 1),
        out_specs=[hbm] * (4 + len(given)),
        scratch_shapes=[
            pltpu.VMEM((window, BLK, 2 * HD), BF16),
            pltpu.VMEM((n_query, 2 * HD, 2 * HD), BF16),
            pltpu.VMEM((window, BLK, 2 * HD), F32),
            pltpu.VMEM((window, 2, BLK, HD), BF16),
            pltpu.VMEM((n_query, BLK, HD), BF16),
            pltpu.VMEM((WAYS, MAXK * BLK, 2 * HD), BF16),
            pltpu.VMEM((WAYS, MAXK * BLK, 2 * HD), F32),
            pltpu.VMEM((WAYS, MAXK * BLK, 2 * HD), BF16),
            pltpu.SMEM((n_query,), jnp.int32),
            pltpu.SMEM((n_query,), jnp.int32),
            pltpu.SemaphoreType.DMA((14,)),
            pltpu.SemaphoreType.DMA((7,)),
        ],
        compiler_params=pltpu.CompilerParams(vmem_limit_bytes=VMEM_LIMIT),
        cost_estimate=pl.CostEstimate(
            flops=0 if shared else pairs * ATTENTION_COST * BLK * BLK * HD,
            bytes_accessed=0 if shared else (2 * window + n_query) * 2 * BLK * HD * 2,
            transcendentals=0 if shared else pairs * BLK * BLK,
        ),
        name="attention",
    )(lists, places, *sources, qd)
    return out[0], out[1:]


def split_kernel(k_ref, v_ref, q_ref, g_ref, ka_ref, va_ref, qda_ref):
    for j in range(ka_ref.shape[1]):
        for m in range(4):
            cols = slice((j * HPG + m) * HD, (j * HPG + m + 1) * HD)
            ka_ref[m, j] = k_ref[:, cols]
            va_ref[m, j] = v_ref[:, cols]
            qda_ref[m, j, 0] = q_ref[:, cols]
            qda_ref[m, j, 1] = g_ref[:, cols]


def split_heads(key_in, value_in, query_in, out_grad):
    groups, step = key_in.shape[1] // (HPG * HD), 2
    one = pl.BlockSpec((4, step, BLK, HD), lambda j: (0, j, 0, 0))
    two = pl.BlockSpec((4, step, 2, BLK, HD), lambda j: (0, j, 0, 0, 0))
    shapes = ((4, groups), (4, groups), (4, groups, 2))
    ka, va, qda = pl.pallas_call(
        split_kernel,
        grid=(groups // step,),
        out_shape=tuple(jax.ShapeDtypeStruct((*x, BLK, HD), BF16) for x in shapes),
        in_specs=[pl.BlockSpec((BLK, step * HPG * HD), lambda j: (0, j))] * 4,
        out_specs=(one, one, two),
        compiler_params=pltpu.CompilerParams(vmem_limit_bytes=VMEM_LIMIT),
        cost_estimate=pl.CostEstimate(flops=0, bytes_accessed=16 * key_in.size, transcendentals=0),
        name="split_heads",
    )(key_in, value_in, query_in, out_grad)
    flat = 4 * groups
    return ka.reshape(flat, BLK, HD), va.reshape(flat, BLK, HD), qda.reshape(flat, 2, BLK, HD)


def fifth_kernel(k_ref, v_ref, q_ref, g_ref, out_ref, held, sem_in, sem_out):
    groups = out_ref.shape[0]
    fetches, puts = [], []
    for j in range(groups):
        cols = pl.ds((j * HPG + HPG - 1) * HD, HD)
        for t, ref in enumerate((k_ref, v_ref, q_ref, g_ref)):
            fetches.append(pltpu.make_async_copy(ref.at[:, cols], held.at[j, t], sem_in.at[j, t]))
            fetches[-1].start()
    for j in range(groups):
        for t in range(4):
            fetches[4 * j + t].wait()
        puts.append(pltpu.make_async_copy(held.at[j], out_ref.at[j], sem_out.at[j]))
        puts[-1].start()
    for put in puts:
        put.wait()


def fifth_heads(*arrays):
    groups = arrays[0].shape[1] // (HPG * HD)
    hbm = pl.BlockSpec(memory_space=pl.ANY)
    return pl.pallas_call(
        fifth_kernel,
        out_shape=jax.ShapeDtypeStruct((groups, 4, BLK, HD), BF16),
        in_specs=[hbm] * 4,
        out_specs=hbm,
        scratch_shapes=[
            pltpu.VMEM((groups, 4, BLK, HD), BF16),
            pltpu.SemaphoreType.DMA((groups, 4)),
            pltpu.SemaphoreType.DMA((groups,)),
        ],
        compiler_params=pltpu.CompilerParams(vmem_limit_bytes=VMEM_LIMIT),
        cost_estimate=pl.CostEstimate(
            flops=0, bytes_accessed=groups * 16 * BLK * HD, transcendentals=0
        ),
        name="fifth_heads",
    )(*arrays)


def join_kernel(first, a_ref, b_ref, *outs):
    for t, ref in enumerate(outs):
        for j in range(b_ref.shape[0]):
            for m in range(HPG):
                value = b_ref[j, first + t] if m == 4 else a_ref[m, j, t]
                ref[:, (j * HPG + m) * HD : (j * HPG + m + 1) * HD] = value


def join_heads(back_a, back_b, first):
    groups, step, n = back_b.shape[0], 2, back_a.shape[1]
    out = jax.ShapeDtypeStruct((BLK, groups * HPG * HD), BF16)
    return pl.pallas_call(
        functools.partial(join_kernel, first),
        grid=(groups // step,),
        out_shape=(out,) * n,
        in_specs=[
            pl.BlockSpec((4, step, n, BLK, HD), lambda j: (0, j, 0, 0, 0)),
            pl.BlockSpec((step, 3, BLK, HD), lambda j: (j, 0, 0, 0)),
        ],
        out_specs=(pl.BlockSpec((BLK, step * HPG * HD), lambda j: (0, j)),) * n,
        compiler_params=pltpu.CompilerParams(vmem_limit_bytes=VMEM_LIMIT),
        cost_estimate=pl.CostEstimate(
            flops=0, bytes_accessed=groups * HPG * n * BLK * HD * 4, transcendentals=0
        ),
        name="join_heads",
    )(back_a.reshape(4, groups, n, BLK, HD), back_b)


def total_kernel(dq_ref, own_ref, *refs):
    terms, out_ref = refs[:-1], refs[-1]
    out_ref[:, 0] = dq_ref[...]
    total = own_ref[...].astype(F32)
    for term in terms:
        total += term[...].astype(F32)
    out_ref[:, 1:] = total.astype(BF16)


def total_grads(dq, own, terms):
    blocks, step = dq.shape[0], 4
    kv_spec = pl.BlockSpec((step, 2, BLK, HD), lambda i: (i, 0, 0, 0))
    return pl.pallas_call(
        total_kernel,
        grid=(blocks // step,),
        out_shape=jax.ShapeDtypeStruct((blocks, 3, BLK, HD), BF16),
        in_specs=[pl.BlockSpec((step, BLK, HD), lambda i: (i, 0, 0))] + [kv_spec] * (1 + len(terms)),
        out_specs=pl.BlockSpec((step, 3, BLK, HD), lambda i: (i, 0, 0, 0)),
        cost_estimate=pl.CostEstimate(
            flops=0, bytes_accessed=(6 + 2 * len(terms)) * dq.size * 2, transcendentals=0
        ),
        name="total_grads",
    )(dq, own, *terms)


def both_halves_kernel(x_ref, own0, own1, right0, right1, left0, left1, out_ref):
    x = x_ref[0]
    for s, own in enumerate((own0, own1)):
        right = jnp.where(x == x_ref[1], (right1, right0)[s][...], (right0, right1)[s][...])
        left = jnp.where(x == 0, (left1, left0)[s][...], (left0, left1)[s][...])
        total = own[...].astype(F32) + right.astype(F32) + left.astype(F32)
        out_ref[s] = total.astype(BF16)


def both_halves(x, last, own, from_right, from_left):
    blocks, step = own[0].shape[0], 4
    spec = pl.BlockSpec((step, 2, BLK, HD), lambda i: (i, 0, 0, 0))
    out = pl.pallas_call(
        both_halves_kernel,
        grid=(blocks // step,),
        out_shape=jax.ShapeDtypeStruct((2, blocks, 2, BLK, HD), BF16),
        in_specs=[pl.BlockSpec(memory_space=pltpu.SMEM)] + [spec] * 6,
        out_specs=pl.BlockSpec((2, step, 2, BLK, HD), lambda i: (0, i, 0, 0, 0)),
        cost_estimate=pl.CostEstimate(flops=0, bytes_accessed=16 * own[0].size, transcendentals=0),
        name="both_halves",
    )(jnp.stack([x, jnp.int32(last)]), *own, *from_right, *from_left)
    return out.reshape(2 * blocks, 2, BLK, HD)


WIDE = ("half", "core", "group")
PAIR = ("core", "group")
CHIPS = ("half", "x")


def shift(value, axes, steps):
    count = lax.axis_size(axes)
    return lax.ppermute(value, axes, [(s, (s + steps) % count) for s in range(count)])


def add(a, b):
    return (a.astype(F32) + b.astype(F32)).astype(BF16)


def exchange(x, axes):
    return lax.all_to_all(x, axes, 0, 0, tiled=True)


def after(x, *done):
    return lax.optimization_barrier((x, *done))[0]


def swap(value):
    return lax.ppermute(value, "core", [(0, 1), (1, 0)])


def shards(query_in, key_in, value_in, out_grad, key_blocks, block_count):
    half, x, core = (lax.axis_index(name) for name in ("half", "x", "core"))
    last, size = lax.axis_size("x") - 1, 2 * BPD
    packed = jnp.concatenate([key_blocks, block_count[:, :, None]], axis=2)
    b = fifth_heads(key_in, value_in, query_in, out_grad)
    gathered = lax.all_gather(after(packed, b), ("half", "core"))
    runs_first = [(h * (last + 1) + x - 1) * size for h in (0, 1, half)]
    heads = BPD * (MAXK + 1)
    places = []
    for s in range(2):
        left, right = jnp.where(x == 0, 1 - s, s) * size, jnp.where(x == last, 1 - s, s) * size
        begin = (2 * s * HPG + 2 * half + core) * heads
        places += [s * size, left, s * size, right, begin, runs_first[s], HPG * heads]
    places += [0, core * BPD, 0, 0, ((2 * half + core) * HPG + HPG - 1) * heads, runs_first[2], 0]
    places = jnp.stack([jnp.asarray(p, jnp.int32) for p in places])
    lists, places = lax.optimization_barrier((gathered.reshape(-1), places))
    ka, va, qda = split_heads(*lax.optimization_barrier((key_in, value_in, query_in, out_grad, b))[:4])

    own_b = exchange(b, "group")
    pairs_b = own_b[:, :2]
    mine = (shift(pairs_b, CHIPS, 1), pairs_b, shift(pairs_b, CHIPS, -1))

    keys = exchange(after(ka, own_b, lists, places), WIDE)
    key_near = [shift(keys, "x", 1), shift(keys, "x", -1)]
    values = first_values = exchange(after(va, keys, *mine), WIDE)
    values = after(values, *key_near)
    value_near = [shift(values, "x", 1), shift(values, "x", -1)]
    theirs = tuple(swap(after(pairs, values, *key_near)) for pairs in mine)

    def run(i, other):
        def fetch(ref, place):
            at = i * size + (BPD - place[1] if other else place[1])
            return [(ref.at[:, t], t, pl.multiple_of(at, 8)) for t in range(2)]

        return fetch

    fetches = [run(i, other) for other in range(2) for i in range(3)]
    dq_b, (left_b, mine_b, right_b, *give_b) = attention(
        2, lists, places, mine + theirs, fetches, after(own_b, values, *key_near), BPD, size
    )
    got_b = [swap(after(give, *value_near)) for give in give_b]

    queries = exchange(after(qda, first_values), WIDE)

    def third(t, i):
        return lambda ref, place: [(ref.at[pl.ds(pl.multiple_of(place[1 + i], 8), size)], t, i * size)]

    fetches = [third(t, i) for t in range(2) for i in range(3)]
    sources = (key_near[0], keys, key_near[1], value_near[0], values, value_near[1])
    done = []
    for s in range(2):
        part_places = after(places, *[d[0] for d in done])
        dq, grads = attention(s, lists, part_places, sources, fetches, queries, size, size)
        done.append((dq, grads, shift(grads[0], "x", -1), shift(grads[2], "x", 1)))
        if s == 0:
            left_b, right_b = add(after(left_b, dq), got_b[0]), add(after(right_b, dq), got_b[2])
            terms_b = [got_b[1], shift(left_b, CHIPS, -1), shift(right_b, CHIPS, 1)]
    total_b = total_grads(after(dq_b, done[1][0]), mine_b, terms_b)
    back_b = exchange(total_b, "group")
    dqa = exchange(after(jnp.concatenate([d[0] for d in done]), *done[0][2:], back_b), WIDE)
    dkva = both_halves(x, last, [d[1][1] for d in done], [d[2] for d in done], [d[3] for d in done])
    dkva = exchange(after(dkva, dqa), WIDE)
    return (*join_heads(dqa[:, None], back_b, 0), *join_heads(dkva, back_b, 1))


def solution(mesh):
    chips = mesh.shape["frame"] // 4
    mesh = Mesh(mesh.devices.reshape(2, chips, 2, -1), ("half", "x", "core", "group"))
    runs = ("half", "x", "core")
    tokens = P((*runs, "group"), None)
    return jax.shard_map(
        shards,
        mesh=mesh,
        in_specs=(tokens,) * 4 + (P("group", runs, None), P("group", runs)),
        out_specs=(tokens,) * 3,
        check_vma=False,
    )
```

```python
import functools

import jax
import jax.numpy as jnp
from jax import lax
from jax.experimental import pallas as pl
from jax.experimental.pallas import tpu as pltpu
from jax.sharding import Mesh
from jax.sharding import PartitionSpec as P

HD = 128
BLK = 128
BAND = 2
BPD = 8
MAXK = 12
HPG = 5
WAYS = 2
PLACES = 7
BUCKETS = (4, 6, 8, 10, 12)
STEP = 2
ATTENTION_COST = 10
VMEM_LIMIT = 56 * 2**20
NEG = -1e30
LOG2E = 1.4426950408889634
SCALE = HD**-0.5
F32 = jnp.float32
BF16 = jnp.bfloat16
NT = (((1,), (1,)), ((), ()))
NN = (((1,), (0,)), ((), ()))
TN = (((0,), (0,)), ((), ()))


def dot(a, b, dims):
    return lax.dot_general(a, b, dims, preferred_element_type=F32)


def fold(x):
    return x.reshape(-1, 8, HD)


def query_blocks(n_keys, blocks, ids, counts, qd, kv, acc, dq, kv_cat, sd_scr, x_cat):
    ways = range(len(blocks))
    index = [[ids(b, s) for s in range(n_keys)] for b in blocks]
    rows = [pl.ds(s * BLK, BLK) for s in range(n_keys)]
    for i in ways:
        for s in range(n_keys):
            kv_cat[i, rows[s], :] = kv[index[i][s]]
    w_t = [qd[b] for b in blocks]
    for s in range(0, n_keys, STEP):
        part = pl.ds(s * BLK, min(STEP, n_keys - s) * BLK)
        for i in ways:
            sd_scr[i, part, :] = dot(kv_cat[i, part, :], w_t[i], NT)
    hidden = [[jnp.where(s < counts[i], 0.0, NEG) for s in range(n_keys)] for i in ways]
    top = []
    for i in ways:
        m8 = jnp.full((8, HD), NEG, F32)
        for s in range(n_keys):
            m8 = jnp.maximum(m8, jnp.max(fold(sd_scr[i, rows[s], :HD]), axis=0) + hidden[i][s])
        top.append(jnp.max(m8, axis=0, keepdims=True) * (SCALE * LOG2E))
    inv, rd = [], []
    for i in ways:
        l8 = jnp.zeros((8, HD), F32)
        r8 = jnp.zeros((8, HD), F32)
        for s in range(n_keys):
            p = jnp.exp2(sd_scr[i, rows[s], :HD] * (SCALE * LOG2E) - (top[i] - hidden[i][s]))
            sd_scr[i, rows[s], :HD] = p
            l8 += jnp.sum(fold(p), axis=0)
            r8 += jnp.sum(fold(p * sd_scr[i, rows[s], HD:]), axis=0)
        inv.append(1.0 / jnp.sum(l8, axis=0, keepdims=True))
        rd.append(jnp.sum(r8, axis=0, keepdims=True) * inv[i])
    for i in ways:
        for s in range(n_keys):
            p = sd_scr[i, rows[s], :HD] * inv[i]
            x_cat[i, rows[s], :HD] = (p * (sd_scr[i, rows[s], HD:] - rd[i])).astype(BF16)
            x_cat[i, rows[s], HD:] = p.astype(BF16)
        for s in range(0, n_keys, STEP):
            n = min(STEP, n_keys - s)
            terms = dot(x_cat[i, pl.ds(s * BLK, n * BLK), :], qd[blocks[i]], NN)
            for j in range(n):
                acc[index[i][s + j]] += terms[j * BLK : (j + 1) * BLK]
        every = pl.ds(0, n_keys * BLK)
        dq[blocks[i]] = (dot(x_cat[i, every, :HD], kv_cat[i, every, :HD], TN) * SCALE).astype(BF16)


def attention_kernel(part, size, n_query, fetches, lists_ref, places_ref, *refs):
    place = [places_ref[part * PLACES + i] for i in range(PLACES)]
    sources, refs = refs[: len(fetches)], refs[len(fetches) :]
    shared = n_query < size
    qd_in, dq_out, targets = refs[0], refs[1], refs[2:5]
    if shared:
        give_out, refs = refs[5:8], refs[3:]
    kv, qd, acc, stage, dq, kv_cat, sd_scr, x_cat, order, counted, in_sem, out_sem = refs[5:]
    copies = []
    for source, fetch in zip(sources, fetches):
        for src, t, row in fetch(source, place):
            dst = kv.at[pl.ds(row, src.shape[0]), :, pl.ds(t * HD, HD)]
            copies.append(pltpu.make_async_copy(src, dst, in_sem.at[len(copies)]))
    q_rows = pl.ds(pl.multiple_of(place[0], 8), n_query)
    for t in range(2):
        src = qd_in.at[q_rows, qd_in.shape[1] - 2 + t]
        dst = qd.at[:, pl.ds(t * HD, HD), pl.ds(t * HD, HD)]
        copies.append(pltpu.make_async_copy(src, dst, in_sem.at[len(copies)]))
    for copy in copies:
        copy.start()
    acc[...] = jnp.zeros_like(acc)
    for t in range(2):
        qd[:, t * HD : (t + 1) * HD, (1 - t) * HD : (2 - t) * HD] = jnp.zeros((n_query, HD, HD), BF16)
    def entry(b, s):
        run = lax.shift_right_logical(b, 3)
        return lists_ref[place[4] + run * place[6] + (b - run * BPD) * (MAXK + 1) + s]

    def ids(b, s):
        return entry(b, s) - place[5]

    def note(b, carry):
        counted[b] = entry(b, MAXK)
        return carry

    lax.fori_loop(0, n_query, note, 0)

    def rank(k, at):
        def put(b, at):
            hit = counted[b] == MAXK - k

            @pl.when(hit)
            def _():
                order[at] = b

            return at + hit.astype(jnp.int32)

        return lax.fori_loop(0, n_query, put, at)

    lax.fori_loop(0, MAXK, rank, 0)
    for copy in copies:
        copy.wait()

    def some(k, carry):
        blocks = [order[k * WAYS + i] for i in range(WAYS)]
        counts = [counted[b] for b in blocks]
        for least, upto in zip((0, *BUCKETS), BUCKETS):

            @pl.when((counts[0] > least) & (counts[0] <= upto))
            def _():
                query_blocks(upto, blocks, ids, counts, qd, kv, acc, dq, kv_cat, sd_scr, x_cat)

        return carry

    lax.fori_loop(0, n_query // WAYS, some, 0)
    puts = [pltpu.make_async_copy(dq, dq_out, out_sem.at[3])]
    puts[0].start()
    for i, target in enumerate(targets):

        def convert(j, carry):
            stage[j, 0] = (acc[j, :, :HD] * SCALE).astype(BF16)
            stage[j, 1] = acc[j, :, HD:].astype(BF16)
            return carry

        lax.fori_loop(i * size, (i + 1) * size, convert, 0)
        rows = pl.ds(i * size, size)
        if shared:
            keep = pl.multiple_of(i * size + place[1], 8)
            give = pl.multiple_of(i * size + n_query - place[1], 8)
            rows = pl.ds(keep, n_query)
            puts.append(
                pltpu.make_async_copy(stage.at[pl.ds(give, n_query)], give_out[i], out_sem.at[4 + i])
            )
            puts[-1].start()
        puts.append(pltpu.make_async_copy(stage.at[rows], target, out_sem.at[i]))
        puts[-1].start()
    for copy in puts:
        copy.wait()


def attention(part, lists, places, sources, fetches, qd, n_query, size):
    window = 3 * size
    shared = n_query < size
    kept = jax.ShapeDtypeStruct((n_query, 2, BLK, HD), BF16)
    given = [kept] * 3 if shared else []
    smem = pl.BlockSpec(memory_space=pltpu.SMEM)
    hbm = pl.BlockSpec(memory_space=pl.ANY)
    pairs = n_query * 8
    out = pl.pallas_call(
        functools.partial(attention_kernel, part, size, n_query, fetches),
        out_shape=[jax.ShapeDtypeStruct((n_query, BLK, HD), BF16)] + [kept] * 3 + given,
        in_specs=[smem] * 2 + [hbm] * (len(sources) + 1),
        out_specs=[hbm] * (4 + len(given)),
        scratch_shapes=[
            pltpu.VMEM((window, BLK, 2 * HD), BF16),
            pltpu.VMEM((n_query, 2 * HD, 2 * HD), BF16),
            pltpu.VMEM((window, BLK, 2 * HD), F32),
            pltpu.VMEM((window, 2, BLK, HD), BF16),
            pltpu.VMEM((n_query, BLK, HD), BF16),
            pltpu.VMEM((WAYS, MAXK * BLK, 2 * HD), BF16),
            pltpu.VMEM((WAYS, MAXK * BLK, 2 * HD), F32),
            pltpu.VMEM((WAYS, MAXK * BLK, 2 * HD), BF16),
            pltpu.SMEM((n_query,), jnp.int32),
            pltpu.SMEM((n_query,), jnp.int32),
            pltpu.SemaphoreType.DMA((14,)),
            pltpu.SemaphoreType.DMA((7,)),
        ],
        compiler_params=pltpu.CompilerParams(vmem_limit_bytes=VMEM_LIMIT),
        cost_estimate=pl.CostEstimate(
            flops=0 if shared else pairs * ATTENTION_COST * BLK * BLK * HD,
            bytes_accessed=0 if shared else (2 * window + n_query) * 2 * BLK * HD * 2,
            transcendentals=0 if shared else pairs * BLK * BLK,
        ),
        name="attention",
    )(lists, places, *sources, qd)
    return out[0], out[1:]


def split_kernel(k_ref, v_ref, q_ref, g_ref, ka_ref, va_ref, qda_ref):
    for j in range(ka_ref.shape[1]):
        for m in range(4):
            cols = slice((j * HPG + m) * HD, (j * HPG + m + 1) * HD)
            ka_ref[m, j] = k_ref[:, cols]
            va_ref[m, j] = v_ref[:, cols]
            qda_ref[m, j, 0] = q_ref[:, cols]
            qda_ref[m, j, 1] = g_ref[:, cols]


def split_heads(key_in, value_in, query_in, out_grad):
    groups, step = key_in.shape[1] // (HPG * HD), 2
    one = pl.BlockSpec((4, step, BLK, HD), lambda j: (0, j, 0, 0))
    two = pl.BlockSpec((4, step, 2, BLK, HD), lambda j: (0, j, 0, 0, 0))
    shapes = ((4, groups), (4, groups), (4, groups, 2))
    ka, va, qda = pl.pallas_call(
        split_kernel,
        grid=(groups // step,),
        out_shape=tuple(jax.ShapeDtypeStruct((*x, BLK, HD), BF16) for x in shapes),
        in_specs=[pl.BlockSpec((BLK, step * HPG * HD), lambda j: (0, j))] * 4,
        out_specs=(one, one, two),
        compiler_params=pltpu.CompilerParams(vmem_limit_bytes=VMEM_LIMIT),
        cost_estimate=pl.CostEstimate(flops=0, bytes_accessed=16 * key_in.size, transcendentals=0),
        name="split_heads",
    )(key_in, value_in, query_in, out_grad)
    flat = 4 * groups
    return ka.reshape(flat, BLK, HD), va.reshape(flat, BLK, HD), qda.reshape(flat, 2, BLK, HD)


def fifth_kernel(k_ref, v_ref, q_ref, g_ref, out_ref, held, sem_in, sem_out):
    groups = out_ref.shape[0]
    fetches, puts = [], []
    for j in range(groups):
        cols = pl.ds((j * HPG + HPG - 1) * HD, HD)
        for t, ref in enumerate((k_ref, v_ref, q_ref, g_ref)):
            fetches.append(pltpu.make_async_copy(ref.at[:, cols], held.at[j, t], sem_in.at[j, t]))
            fetches[-1].start()
    for j in range(groups):
        for t in range(4):
            fetches[4 * j + t].wait()
        puts.append(pltpu.make_async_copy(held.at[j], out_ref.at[j], sem_out.at[j]))
        puts[-1].start()
    for put in puts:
        put.wait()


def fifth_heads(*arrays):
    groups = arrays[0].shape[1] // (HPG * HD)
    hbm = pl.BlockSpec(memory_space=pl.ANY)
    return pl.pallas_call(
        fifth_kernel,
        out_shape=jax.ShapeDtypeStruct((groups, 4, BLK, HD), BF16),
        in_specs=[hbm] * 4,
        out_specs=hbm,
        scratch_shapes=[
            pltpu.VMEM((groups, 4, BLK, HD), BF16),
            pltpu.SemaphoreType.DMA((groups, 4)),
            pltpu.SemaphoreType.DMA((groups,)),
        ],
        compiler_params=pltpu.CompilerParams(vmem_limit_bytes=VMEM_LIMIT),
        cost_estimate=pl.CostEstimate(
            flops=0, bytes_accessed=groups * 16 * BLK * HD, transcendentals=0
        ),
        name="fifth_heads",
    )(*arrays)


def join_kernel(first, a_ref, b_ref, *outs):
    for t, ref in enumerate(outs):
        for j in range(b_ref.shape[0]):
            for m in range(HPG):
                value = b_ref[j, first + t] if m == 4 else a_ref[m, j, t]
                ref[:, (j * HPG + m) * HD : (j * HPG + m + 1) * HD] = value


def join_heads(back_a, back_b, first):
    groups, step, n = back_b.shape[0], 2, back_a.shape[1]
    out = jax.ShapeDtypeStruct((BLK, groups * HPG * HD), BF16)
    return pl.pallas_call(
        functools.partial(join_kernel, first),
        grid=(groups // step,),
        out_shape=(out,) * n,
        in_specs=[
            pl.BlockSpec((4, step, n, BLK, HD), lambda j: (0, j, 0, 0, 0)),
            pl.BlockSpec((step, 3, BLK, HD), lambda j: (j, 0, 0, 0)),
        ],
        out_specs=(pl.BlockSpec((BLK, step * HPG * HD), lambda j: (0, j)),) * n,
        compiler_params=pltpu.CompilerParams(vmem_limit_bytes=VMEM_LIMIT),
        cost_estimate=pl.CostEstimate(
            flops=0, bytes_accessed=groups * HPG * n * BLK * HD * 4, transcendentals=0
        ),
        name="join_heads",
    )(back_a.reshape(4, groups, n, BLK, HD), back_b)


def total_kernel(dq_ref, own_ref, *refs):
    terms, out_ref = refs[:-1], refs[-1]
    out_ref[:, 0] = dq_ref[...]
    total = own_ref[...].astype(F32)
    for term in terms:
        total += term[...].astype(F32)
    out_ref[:, 1:] = total.astype(BF16)


def total_grads(dq, own, terms):
    blocks, step = dq.shape[0], 4
    kv_spec = pl.BlockSpec((step, 2, BLK, HD), lambda i: (i, 0, 0, 0))
    return pl.pallas_call(
        total_kernel,
        grid=(blocks // step,),
        out_shape=jax.ShapeDtypeStruct((blocks, 3, BLK, HD), BF16),
        in_specs=[pl.BlockSpec((step, BLK, HD), lambda i: (i, 0, 0))] + [kv_spec] * (1 + len(terms)),
        out_specs=pl.BlockSpec((step, 3, BLK, HD), lambda i: (i, 0, 0, 0)),
        cost_estimate=pl.CostEstimate(
            flops=0, bytes_accessed=(6 + 2 * len(terms)) * dq.size * 2, transcendentals=0
        ),
        name="total_grads",
    )(dq, own, *terms)


def both_halves_kernel(x_ref, own0, own1, right0, right1, left0, left1, out_ref):
    x = x_ref[0]
    for s, own in enumerate((own0, own1)):
        right = jnp.where(x == x_ref[1], (right1, right0)[s][...], (right0, right1)[s][...])
        left = jnp.where(x == 0, (left1, left0)[s][...], (left0, left1)[s][...])
        total = own[...].astype(F32) + right.astype(F32) + left.astype(F32)
        out_ref[s] = total.astype(BF16)


def both_halves(x, last, own, from_right, from_left):
    blocks, step = own[0].shape[0], 4
    spec = pl.BlockSpec((step, 2, BLK, HD), lambda i: (i, 0, 0, 0))
    out = pl.pallas_call(
        both_halves_kernel,
        grid=(blocks // step,),
        out_shape=jax.ShapeDtypeStruct((2, blocks, 2, BLK, HD), BF16),
        in_specs=[pl.BlockSpec(memory_space=pltpu.SMEM)] + [spec] * 6,
        out_specs=pl.BlockSpec((2, step, 2, BLK, HD), lambda i: (0, i, 0, 0, 0)),
        cost_estimate=pl.CostEstimate(flops=0, bytes_accessed=16 * own[0].size, transcendentals=0),
        name="both_halves",
    )(jnp.stack([x, jnp.int32(last)]), *own, *from_right, *from_left)
    return out.reshape(2 * blocks, 2, BLK, HD)


WIDE = ("half", "core", "group")
PAIR = ("core", "group")
CHIPS = ("half", "x")


def shift(value, axes, steps):
    count = lax.axis_size(axes)
    return lax.ppermute(value, axes, [(s, (s + steps) % count) for s in range(count)])


def add(a, b):
    return (a.astype(F32) + b.astype(F32)).astype(BF16)


def exchange(x, axes):
    return lax.all_to_all(x, axes, 0, 0, tiled=True)


def after(x, *done):
    return lax.optimization_barrier((x, *done))[0]


def swap(value):
    return lax.ppermute(value, "core", [(0, 1), (1, 0)])


def shards(query_in, key_in, value_in, out_grad, key_blocks, block_count):
    half, x, core = (lax.axis_index(name) for name in ("half", "x", "core"))
    last, size = lax.axis_size("x") - 1, 2 * BPD
    packed = jnp.concatenate([key_blocks, block_count[:, :, None]], axis=2)
    b = fifth_heads(key_in, value_in, query_in, out_grad)
    ka, va, qda = split_heads(*lax.optimization_barrier((key_in, value_in, query_in, out_grad, b))[:4])
    gathered = lax.all_gather(after(packed, ka), ("half", "core"))
    runs_first = [(h * (last + 1) + x - 1) * size for h in (0, 1, half)]
    heads = BPD * (MAXK + 1)
    places = []
    for s in range(2):
        left, right = jnp.where(x == 0, 1 - s, s) * size, jnp.where(x == last, 1 - s, s) * size
        begin = (2 * s * HPG + 2 * half + core) * heads
        places += [s * size, left, s * size, right, begin, runs_first[s], HPG * heads]
    places += [0, core * BPD, 0, 0, ((2 * half + core) * HPG + HPG - 1) * heads, runs_first[2], 0]
    places = jnp.stack([jnp.asarray(p, jnp.int32) for p in places])
    lists, places = lax.optimization_barrier((gathered.reshape(-1), places))

    own_b = exchange(b, "group")
    pairs_b = own_b[:, :2]
    mine = (shift(pairs_b, CHIPS, 1), pairs_b, shift(pairs_b, CHIPS, -1))

    keys = exchange(after(ka, own_b, lists, places), WIDE)
    key_near = [shift(keys, "x", 1), shift(keys, "x", -1)]
    values = first_values = exchange(after(va, keys, *mine), WIDE)
    values = after(values, *key_near)
    value_near = [shift(values, "x", 1), shift(values, "x", -1)]
    theirs = tuple(swap(after(pairs, values, *key_near)) for pairs in mine)

    def run(i, other):
        def fetch(ref, place):
            at = i * size + (BPD - place[1] if other else place[1])
            return [(ref.at[:, t], t, pl.multiple_of(at, 8)) for t in range(2)]

        return fetch

    fetches = [run(i, other) for other in range(2) for i in range(3)]
    dq_b, (left_b, mine_b, right_b, *give_b) = attention(
        2, lists, places, mine + theirs, fetches, after(own_b, values, *key_near), BPD, size
    )
    got_b = [swap(after(give, *value_near)) for give in give_b]

    queries = exchange(after(qda, first_values), WIDE)

    def third(t, i):
        return lambda ref, place: [(ref.at[pl.ds(pl.multiple_of(place[1 + i], 8), size)], t, i * size)]

    fetches = [third(t, i) for t in range(2) for i in range(3)]
    sources = (key_near[0], keys, key_near[1], value_near[0], values, value_near[1])
    done = []
    for s in range(2):
        part_places = after(places, *[d[0] for d in done])
        dq, grads = attention(s, lists, part_places, sources, fetches, queries, size, size)
        done.append((dq, grads, shift(grads[0], "x", -1), shift(grads[2], "x", 1)))
        if s == 0:
            left_b, right_b = add(after(left_b, dq), got_b[0]), add(after(right_b, dq), got_b[2])
            terms_b = [got_b[1], shift(left_b, CHIPS, -1), shift(right_b, CHIPS, 1)]
    total_b = total_grads(after(dq_b, done[1][0]), mine_b, terms_b)
    back_b = exchange(total_b, "group")
    dqa = exchange(after(jnp.concatenate([d[0] for d in done]), *done[0][2:], back_b), WIDE)
    dkva = both_halves(x, last, [d[1][1] for d in done], [d[2] for d in done], [d[3] for d in done])
    dkva = exchange(after(dkva, dqa), WIDE)
    return (*join_heads(dqa[:, None], back_b, 0), *join_heads(dkva, back_b, 1))


def solution(mesh):
    chips = mesh.shape["frame"] // 4
    mesh = Mesh(mesh.devices.reshape(2, chips, 2, -1), ("half", "x", "core", "group"))
    runs = ("half", "x", "core")
    tokens = P((*runs, "group"), None)
    return jax.shard_map(
        shards,
        mesh=mesh,
        in_specs=(tokens,) * 4 + (P("group", runs, None), P("group", runs)),
        out_specs=(tokens,) * 3,
        check_vma=False,
    )
```
